32 devices in a mesh: dp: 8 (over y, x, core), mp: 4 (over z).
Axes of the slice: x: 2, y: 2, z: 4, core: 2. Of those that a mesh axis runs over, the one named last changes fastest.
Arguments:
- inputs: bfloat16 [16384, 2048], P('dp', 'mp'), may hold values from -8 to 8, as said below
- cotangent: bfloat16 [16384, 2048], P('dp', 'mp'), may hold values from -6 to 6
- reset_mask: int32 [16384], P('dp'), may hold values 0 or 1
- norm1_gain: bfloat16 [2048], P(('mp', 'dp')), may hold values from 0.25 to 1.75
- w_input: bfloat16 [2048, 2560], P('dp', 'mp'), may hold values from -0.125 to 0.125
- w_branch: bfloat16 [2048, 2560], P('dp', 'mp'), may hold values from -0.125 to 0.125
- w_output: bfloat16 [2560, 2048], P('mp', 'dp'), may hold values from -0.3125 to 0.3125
- conv_weight: bfloat16 [4, 2560], P(None, ('mp', 'dp')), may hold values from -3 to 3
- conv_bias: bfloat16 [2560], P(('mp', 'dp')), may hold values from -3 to 3
- gate_a_weight: bfloat16 [16, 160, 160], P('mp', 'dp'), may hold values from -0.5 to 0.5
- gate_a_bias: bfloat16 [2560], P(('mp', 'dp')), may hold values from -3 to 3
- gate_x_weight: bfloat16 [16, 160, 160], P('mp', 'dp'), may hold values from -0.5 to 0.5
- gate_x_bias: bfloat16 [2560], P(('mp', 'dp')), may hold values from -3 to 3
- decay_param: bfloat16 [2560], P(('mp', 'dp')), may hold values from -8 to -2
- norm2_gain: bfloat16 [2048], P(('mp', 'dp')), may hold values from 0.25 to 1.75
- w_gate: bfloat16 [2048, 6144], P('dp', 'mp'), may hold values from -0.125 to 0.125
- w_up: bfloat16 [2048, 6144], P('dp', 'mp'), may hold values from -0.125 to 0.125
- w_down: bfloat16 [6144, 2048], P('mp', 'dp'), may hold values from -0.125 to 0.125
Outputs:
- output: bfloat16 [16384, 2048], P('dp', 'mp')
- input_grad: float32 [16384, 2048], P('dp', 'mp')
- norm1_gain_grad: float32 [2048], P(('mp', 'dp'))
- w_input_grad: float32 [2048, 2560], P('dp', 'mp')
- w_branch_grad: float32 [2048, 2560], P('dp', 'mp')
- w_output_grad: float32 [2560, 2048], P('mp', 'dp')
- conv_weight_grad: float32 [4, 2560], P(None, ('mp', 'dp'))
- conv_bias_grad: float32 [2560], P(('mp', 'dp'))
- gate_a_weight_grad: float32 [16, 160, 160], P('mp', 'dp')
- gate_a_bias_grad: float32 [2560], P(('mp', 'dp'))
- gate_x_weight_grad: float32 [16, 160, 160], P('mp', 'dp')
- gate_x_bias_grad: float32 [2560], P(('mp', 'dp'))
- decay_param_grad: float32 [2560], P(('mp', 'dp'))
- norm2_gain_grad: float32 [2048], P(('mp', 'dp'))
- w_gate_grad: float32 [2048, 6144], P('dp', 'mp')
- w_up_grad: float32 [2048, 6144], P('dp', 'mp')
- w_down_grad: float32 [6144, 2048], P('mp', 'dp')
The draws below stay inside these ranges and needn't reach their ends.
Inputs may be any that keep to these rules, and one draw needn't show every extreme that they name: `inputs`: activations of order one. `reset_mask`: 1 marks a token where a new document begins; a token whose index is a multiple of 2048 begins a sequence whatever it holds.
All inputs are finite; a program needn't handle non-finite values. No bound on the sum of `reset_mask` on one device may be relied on, other than what follows from the above.
Results may differ from the reference program's by a relative error of at most 0.0089.
Values may be sent and summed in bfloat16 or wider, within the bound.
A program may use at most 448 MiB of HBM per device.

```python
import jax
import jax.numpy as jnp
from jax import lax

D = 2048
HEADS = 16
BW = 160
FF = 6144
CONV = 4
SEQ = 2048
RW = 2560
TOKENS = 16384


def draw_inputs(key, part):
    key = jax.random.fold_in(key, 7)
    key_base, key_cols = jax.random.split(key, 2)
    column_pos = jnp.arange(D, dtype=jnp.float32) / D
    column = (0.5 + 1.1 * column_pos) * jax.random.uniform(key_cols, (D,), jnp.float32, 0.8, 1.25)
    base = jnp.clip(jax.random.normal(key_base, (TOKENS, D), jnp.float32), -4.0, 4.0)
    return (base * column).astype(jnp.bfloat16)


def plant(array, own_key, smallest, top_value):
    place = [jax.random.randint(jax.random.fold_in(own_key, axis), (), 0, length) for axis, length in enumerate(array.shape)]
    main_axis = array.shape.index(max(array.shape))
    neighbour = place[:main_axis] + [(place[main_axis] + 1) % array.shape[main_axis]] + place[main_axis + 1:]
    return array.at[tuple(place)].set(smallest).at[tuple(neighbour)].set(top_value)


def level_of(stream_key, extent, cuts, smallest, largest):
    factor_of = 1.0
    for dim, shards_of in cuts:
        draws = jax.random.uniform(jax.random.fold_in(jax.random.fold_in(stream_key, 6), dim), (shards_of,), jnp.float32, smallest / len(cuts), largest / len(cuts))
        factor_of = factor_of * jnp.repeat(jnp.exp(draws), extent[dim] // shards_of).reshape((-1,) + (1,) * (len(extent) - 1 - dim))
    return factor_of


def gaussian(stream_key, dims, deviation, reach, shards=(), held_as=jnp.bfloat16):
    values = deviation * jax.random.normal(stream_key, dims, jnp.float32)
    if shards:
        values = values * level_of(stream_key, dims, shards, -0.22, 0.18)
    return jnp.clip(values, -reach, reach).astype(held_as)


def setup_inputs(seed: int = 0) -> dict:
    seeds = jax.random.split(jax.random.key(seed), 19)
    return {
        "inputs": draw_inputs(jax.random.fold_in(seeds[18], 71), 0),
        "cotangent": gaussian(seeds[1], (TOKENS, D), 1.0, 6.0, ((0, 8), (1, 4))),
        "reset_mask": plant((jax.random.randint(seeds[2], (TOKENS,), 0, 256) < 1).astype(jnp.int32), jax.random.fold_in(seeds[2], 1), 0, 1),
        "norm1_gain": jnp.clip(1.0 + 0.15 * jax.random.normal(seeds[3], (D,), jnp.float32), 0.25, 1.75).astype(jnp.bfloat16),
        "w_input": gaussian(seeds[4], (D, RW), D ** -0.5, 0.125, ((0, 8), (1, 4))),
        "w_branch": gaussian(seeds[5], (D, RW), D ** -0.5, 0.125, ((0, 8), (1, 4))),
        "w_output": gaussian(seeds[6], (RW, D), (RW // 8) ** -0.5, 0.3125, ((0, 4), (1, 8))),
        "conv_weight": gaussian(seeds[7], (CONV, RW), 0.5, 3.0, ((1, 32),)),
        "conv_bias": gaussian(seeds[8], (RW,), 0.5, 3.0, ((0, 32),)),
        "gate_a_weight": gaussian(seeds[9], (HEADS, BW, BW), BW ** -0.5, 0.5, ((0, 4), (1, 8))),
        "gate_a_bias": gaussian(seeds[10], (RW,), 0.5, 3.0, ((0, 32),)),
        "gate_x_weight": gaussian(seeds[11], (HEADS, BW, BW), BW ** -0.5, 0.5, ((0, 4), (1, 8))),
        "gate_x_bias": gaussian(seeds[12], (RW,), 0.5, 3.0, ((0, 32),)),
        "decay_param": jnp.clip(-8.0 + 6.0 * jax.random.uniform(seeds[13], (RW,), jnp.float32) ** level_of(seeds[13], (RW,), ((0, 32),), -0.2, 0.2), -8.0, -2.0).astype(jnp.bfloat16),
        "norm2_gain": jnp.clip(1.0 + 0.15 * jax.random.normal(seeds[14], (D,), jnp.float32), 0.25, 1.75).astype(jnp.bfloat16),
        "w_gate": gaussian(seeds[15], (D, FF), D ** -0.5, 0.125, ((0, 8), (1, 4))),
        "w_up": gaussian(seeds[16], (D, FF), D ** -0.5, 0.125, ((0, 8), (1, 4))),
        "w_down": gaussian(seeds[17], (FF, D), (FF // 3) ** -0.5, 0.125, ((0, 4), (1, 8))),
    }


@jax.custom_vjp
def low(v):
    return lax.optimization_barrier(v.astype(jnp.bfloat16)).astype(jnp.float32)

@jax.custom_vjp
def low_back(v):
    return v

def low_keep(v):
    return (low(v), None)

def low_pass(kept, grad):
    return (grad,)

def back_keep(v):
    return (v, None)

def back_low(kept, grad):
    return (low(grad),)
low.defvjp(low_keep, low_pass)
low_back.defvjp(back_keep, back_low)
epsilon = 1e-06

def product(left, right):
    return jnp.dot(left, right, precision=lax.Precision.HIGHEST)

def rms_scale(values, gain):
    return values * lax.rsqrt(lax.optimization_barrier(jnp.mean(values * values, axis=-1, keepdims=True)) + epsilon) * gain

def block_gate(mixed, weight, bias):
    length = mixed.shape[0]
    blocks = mixed.reshape(length, weight.shape[0], weight.shape[2])
    inner = jnp.einsum('thi,hij->thj', blocks, weight, precision=lax.Precision.HIGHEST)
    return jax.nn.sigmoid(inner.reshape(length, -1) + bias)

def linear_scan(carried, driven):

    def combine(earlier, later):
        return (earlier[0] * later[0], later[0] * earlier[1] + later[1])
    return lax.associative_scan(combine, (carried, driven), axis=0)[1]

def recurrence(rnn_in, gate_in, conv_weight, conv_bias, gate_a_weight, gate_a_bias, gate_x_weight, gate_x_bias, decay_param, starts):
    length = rnn_in.shape[0]
    segment = jnp.cumsum(starts)
    mixed = conv_bias + conv_weight[0] * rnn_in
    for offset in range(1, conv_weight.shape[0]):
        moved = jnp.pad(rnn_in, ((offset, 0), (0, 0)))[:length]
        earlier_seg = jnp.pad(segment, (offset, 0), constant_values=-1)[:length]
        same_doc = (earlier_seg == segment).astype(jnp.float32)[:, None]
        mixed = mixed + conv_weight[offset] * moved * same_doc
    gate_a = block_gate(mixed, gate_a_weight, gate_a_bias)
    gate_x = block_gate(mixed, gate_x_weight, gate_x_bias)
    log_decay = -8.0 * gate_a * jax.nn.softplus(decay_param)
    begins = starts.astype(jnp.float32)[:, None]
    carried = jnp.exp(log_decay) * (1.0 - begins)
    input_scale = jnp.sqrt(-jnp.expm1(2.0 * log_decay)) * (1.0 - begins) + begins
    state = linear_scan(carried, mixed * gate_x * input_scale)
    return jax.nn.gelu(gate_in) * state

def layer(sequence, starts, params):
    norm1_gain, w_input, w_branch, w_output, conv_weight, conv_bias, gate_a_weight, gate_a_bias, gate_x_weight, gate_x_bias, decay_param, norm2_gain, w_gate, w_up, w_down = params
    normed_one = low(rms_scale(sequence, norm1_gain))
    rnn_in = low_back(product(normed_one, w_input))
    gate_in = low_back(product(normed_one, w_branch))
    mixer_out = low(recurrence(rnn_in, gate_in, conv_weight, conv_bias, gate_a_weight, gate_a_bias, gate_x_weight, gate_x_bias, decay_param, starts))
    rec_branch = low_back(product(mixer_out, w_output))
    resid_mid = sequence + rec_branch
    normed_two = low(rms_scale(resid_mid, norm2_gain))
    gate_val = low_back(product(normed_two, w_gate))
    up_val = low_back(product(normed_two, w_up))
    hidden = low(jax.nn.gelu(gate_val) * up_val)
    return resid_mid + product(hidden, w_down)

def reference(inputs, cotangent, reset_mask, norm1_gain, w_input, w_branch, w_output, conv_weight, conv_bias, gate_a_weight, gate_a_bias, gate_x_weight, gate_x_bias, decay_param, norm2_gain, w_gate, w_up, w_down):
    params = tuple((weight.astype(jnp.float32) for weight in (norm1_gain, w_input, w_branch, w_output, conv_weight, conv_bias, gate_a_weight, gate_a_bias, gate_x_weight, gate_x_bias, decay_param, norm2_gain, w_gate, w_up, w_down)))
    count = inputs.shape[0] // SEQ
    first_pos = (jnp.arange(inputs.shape[0]) % SEQ == 0).astype(jnp.int32)
    starts = jnp.maximum(reset_mask, first_pos).reshape(count, SEQ)
    stacked = inputs.astype(jnp.float32).reshape(count, SEQ, -1)

    def whole(stacked_in, weights):

        def seq_layer(paired):
            return layer(paired[0], paired[1], weights)
        return lax.map(jax.checkpoint(seq_layer), (stacked_in, starts))
    result, pull = jax.vjp(whole, stacked, params)
    grad_in, grads = pull(cotangent.astype(jnp.float32).reshape(count, SEQ, -1))
    return (result.reshape(inputs.shape).astype(jnp.bfloat16), grad_in.reshape(inputs.shape), grads[0], grads[1], grads[2], grads[3], grads[4], grads[5], grads[6], grads[7], grads[8], grads[9], grads[10], grads[11], grads[12], grads[13], grads[14])
```

```python
import functools

import jax
import jax.numpy as jnp
from jax import lax
from jax.experimental import pallas as pl
from jax.experimental.pallas import tpu as pltpu
from jax.sharding import PartitionSpec as P

SEQ = 2048
epsilon = 1e-06
BF = jnp.bfloat16
F32 = jnp.float32
ROWS = 64
HALO = 8


def dot_nt(left, right):
    return lax.dot_general(
        left, right, (((1,), (1,)), ((), ())), preferred_element_type=F32
    )


def dot_nn(left, right):
    return jnp.dot(left, right, preferred_element_type=F32)


def dot_tn(left, right):
    return lax.dot_general(
        left, right, (((0,), (0,)), ((), ())), preferred_element_type=F32
    )


def gelu_parts(value):
    inner = 0.7978845608028654 * (value + 0.044715 * value * value * value)
    tanh = jnp.tanh(inner)
    slope = 0.7978845608028654 * (1.0 + 3.0 * 0.044715 * value * value)
    gelu = 0.5 * value * (1.0 + tanh)
    grad = 0.5 * (1.0 + tanh) + 0.5 * value * (1.0 - tanh * tanh) * slope
    return gelu, grad


def sigmoid(value):
    return 1.0 / (1.0 + jnp.exp(-value))


def one_minus_exp(log_value):
    y = -2.0 * log_value
    series = y * (
        1.0
        - y
        * (1 / 2)
        * (
            1.0
            - y
            * (1 / 3)
            * (1.0 - y * (1 / 4) * (1.0 - y * (1 / 5) * (1.0 - y * (1 / 6))))
        )
    )
    return jnp.where(y < 0.25, series, 1.0 - jnp.exp(-y))


def conv_terms(ext, masks, rows):
    terms = [ext[HALO : HALO + rows]]
    for k in range(1, 4):
        moved = pltpu.roll(ext, k, axis=0)[HALO : HALO + rows]
        terms.append(moved * masks[:, k - 1 : k])
    return terms


def forward_kernel(
    rnn_ref,
    halo_ref,
    mask_ref,
    conv_ref,
    vec_ref,
    wa_ref,
    wx_ref,
    mixed_ref,
    ga_ref,
    gx_ref,
    h_ref,
    p_ref,
    end_ref,
    ext_ref,
):
    length, width = rnn_ref.shape[1:]
    ext_ref[0:HALO, :] = halo_ref[0]
    ext_ref[HALO:, :] = rnn_ref[0]
    row8 = lax.broadcasted_iota(jnp.int32, (ROWS, 1), 0) % 8

    def block(i, carry):
        h_in, p_in = carry
        r0 = pl.multiple_of(i * ROWS, ROWS)
        masks = mask_ref[0, pl.ds(r0, ROWS), :]
        terms = conv_terms(ext_ref[pl.ds(r0, ROWS + HALO), :], masks, ROWS)
        mixed = vec_ref[0:1, :] + conv_ref[0:1, :] * terms[0]
        for k in range(1, 4):
            mixed = mixed + conv_ref[k : k + 1, :] * terms[k]
        high = mixed.astype(BF)
        low = (mixed - high.astype(F32)).astype(BF)
        gate_a = sigmoid(
            dot_nn(high, wa_ref[...]) + dot_nn(low, wa_ref[...]) + vec_ref[1:2, :]
        )
        gate_x = sigmoid(
            dot_nn(high, wx_ref[...]) + dot_nn(low, wx_ref[...]) + vec_ref[2:3, :]
        )
        begins = masks[:, 3:4]
        log_a = gate_a * vec_ref[3:4, :]
        a = jnp.exp(log_a) * (1.0 - begins)
        scale = jnp.sqrt(one_minus_exp(log_a)) * (1.0 - begins) + begins
        b = mixed * gate_x * scale
        mixed_ref[0, pl.ds(r0, ROWS), :] = mixed
        ga_ref[0, pl.ds(r0, ROWS), :] = gate_a
        gx_ref[0, pl.ds(r0, ROWS), :] = gate_x
        for d in (1, 2, 4):
            valid = row8 >= d
            b = jnp.where(valid, a * pltpu.roll(b, d, axis=0) + b, b)
            a = jnp.where(valid, a * pltpu.roll(a, d, axis=0), a)
        for g in range(ROWS // 8):
            rows = slice(8 * g, 8 * g + 8)
            h = b[rows] + a[rows] * h_in
            p = a[rows] * p_in
            h_ref[0, pl.ds(r0 + 8 * g, 8), :] = h
            p_ref[0, pl.ds(r0 + 8 * g, 8), :] = p
            h_in = h[7:8]
            p_in = p[7:8]
        return h_in, p_in

    h_end, p_end = lax.fori_loop(
        0,
        length // ROWS,
        block,
        (jnp.zeros((1, width), F32), jnp.ones((1, width), F32)),
    )
    end_ref[0, 0:4, :] = jnp.broadcast_to(p_end, (4, width))
    end_ref[0, 4:8, :] = jnp.broadcast_to(h_end, (4, width))


def adjoint_kernel(
    dmix_ref,
    gate_ref,
    state_ref,
    ga_ref,
    mask_ref,
    vec_ref,
    lam_ref,
    q_ref,
    dgi_ref,
    end_ref,
):
    length, width = dmix_ref.shape[1:]
    row = lax.broadcasted_iota(jnp.int32, (ROWS, 1), 0)
    row8 = row % 8
    blocks = length // ROWS

    def block(i, carry):
        lam_in, q_in, a_next = carry
        r0 = pl.multiple_of((blocks - 1 - i) * ROWS, ROWS)
        here = pl.ds(r0, ROWS)
        begins = mask_ref[0, here, :][:, 3:4]
        d_mixer = dmix_ref[0, here, :]
        gelu, slope = gelu_parts(gate_ref[0, here, :])
        dgi_ref[0, here, :] = (d_mixer * state_ref[0, here, :] * slope).astype(BF)
        b = d_mixer * gelu
        a = jnp.exp(ga_ref[0, here, :] * vec_ref[3:4, :]) * (1.0 - begins)
        c = jnp.where(row == ROWS - 1, a_next, pltpu.roll(a, ROWS - 1, axis=0))
        for d in (1, 2, 4):
            valid = row8 < 8 - d
            b = jnp.where(valid, c * pltpu.roll(b, ROWS - d, axis=0) + b, b)
            c = jnp.where(valid, c * pltpu.roll(c, ROWS - d, axis=0), c)
        for g in reversed(range(ROWS // 8)):
            rows = slice(8 * g, 8 * g + 8)
            lam = b[rows] + c[rows] * lam_in
            q = c[rows] * q_in
            lam_ref[0, pl.ds(r0 + 8 * g, 8), :] = lam
            q_ref[0, pl.ds(r0 + 8 * g, 8), :] = q
            lam_in = lam[0:1]
            q_in = q[0:1]
        return lam_in, q_in, a[0:1]

    one = jnp.ones((1, width), F32)
    lam0, q0, a0 = lax.fori_loop(
        0, blocks, block, (jnp.zeros((1, width), F32), one, one)
    )
    end_ref[0, 0:4, :] = jnp.broadcast_to(a0 * q0, (4, width))
    end_ref[0, 4:8, :] = jnp.broadcast_to(a0 * lam0, (4, width))


def fold8(value):
    total = value[0:8]
    for g in range(1, value.shape[0] // 8):
        total = total + value[8 * g : 8 * g + 8]
    return total


def backward_kernel(
    lam_ref,
    q_ref,
    state_ref,
    ga_ref,
    gx_ref,
    mixed_ref,
    rnn_ref,
    halo_ref,
    mask_ref,
    edge_ref,
    conv_ref,
    vec_ref,
    wa_ref,
    wx_ref,
    drnn_ref,
    head_ref,
    tail_ref,
    wag_ref,
    wxg_ref,
    vg_ref,
    ext_ref,
    prev_ref,
    dm_ref,
):
    length, width = lam_ref.shape[1:]
    first = pl.program_id(0) == 0

    @pl.when(first)
    def _():
        wag_ref[...] = jnp.zeros_like(wag_ref)
        wxg_ref[...] = jnp.zeros_like(wxg_ref)
        vg_ref[...] = jnp.zeros_like(vg_ref)

    ext_ref[0:HALO, :] = halo_ref[0]
    ext_ref[HALO:, :] = rnn_ref[0]
    prev_ref[0:HALO, :] = jnp.broadcast_to(edge_ref[0, 0:1, :], (HALO, width))
    prev_ref[HALO:, :] = state_ref[0]
    dm_ref[length:, :] = jnp.zeros((HALO, width), F32)

    def block(i, carry):
        r0 = pl.multiple_of(i * ROWS, ROWS)
        here = pl.ds(r0, ROWS)
        masks = mask_ref[0, here, :]
        begins = masks[:, 3:4]
        lam = lam_ref[0, here, :] + q_ref[0, here, :] * edge_ref[0, 4:5, :]
        before = pltpu.roll(prev_ref[pl.ds(r0, ROWS + HALO), :], 1, axis=0)[
            HALO : HALO + ROWS
        ]
        gate_a = ga_ref[0, here, :]
        gate_x = gx_ref[0, here, :]
        mixed = mixed_ref[0, here, :]
        log_a = gate_a * vec_ref[3:4, :]
        decay = jnp.exp(log_a)
        inv_scale = lax.rsqrt(one_minus_exp(log_a))
        scale_raw = jnp.sqrt(one_minus_exp(log_a))
        keep = 1.0 - begins
        scale = scale_raw * keep + begins
        through = lam * mixed
        d_log = lam * before * decay * keep + jnp.where(
            begins > 0.5, 0.0, through * gate_x * (-(decay * decay) * inv_scale)
        )
        log_gate = d_log * gate_a
        d_pre_a = log_gate * (1.0 - gate_a) * vec_ref[3:4, :]
        d_pre_x = through * scale * gate_x * (1.0 - gate_x)
        pa = d_pre_a.astype(BF)
        px = d_pre_x.astype(BF)
        mb = mixed.astype(BF)
        d_mixed = (
            lam * gate_x * scale + dot_nt(pa, wa_ref[...]) + dot_nt(px, wx_ref[...])
        )
        dm_ref[here, :] = d_mixed
        wag_ref[...] += dot_tn(mb, pa)
        wxg_ref[...] += dot_tn(mb, px)
        terms = conv_terms(ext_ref[pl.ds(r0, ROWS + HALO), :], masks, ROWS)
        sums = [d_mixed * term for term in terms]
        sums += [d_mixed, d_pre_a, d_pre_x, log_gate]
        for n, value in enumerate(sums):
            vg_ref[n] += fold8(value)
        return carry

    lax.fori_loop(0, length // ROWS, block, 0)

    def shift(i, carry):
        r0 = pl.multiple_of(i * ROWS, ROWS)
        ext = dm_ref[pl.ds(r0, ROWS + HALO), :]
        masks = mask_ref[0, pl.ds(r0, ROWS + HALO), :]
        total = conv_ref[0:1, :] * ext[0:ROWS]
        for k in range(1, 4):
            moved = pltpu.roll(ext * masks[:, k - 1 : k], ROWS + HALO - k, axis=0)
            total = total + conv_ref[k : k + 1, :] * moved[0:ROWS]
        drnn_ref[0, pl.ds(r0, ROWS), :] = total.astype(BF)

        @pl.when(i == length // ROWS - 1)
        def _():
            tail_ref[0] = total[ROWS - HALO :]

        return carry

    lax.fori_loop(0, length // ROWS, shift, 0)
    head_ref[0] = dm_ref[0:HALO, :]


def block_specs(shapes):
    specs = []
    for shape, moving in shapes:
        if moving:
            specs.append(
                pl.BlockSpec((1,) + shape[1:], lambda i, n=len(shape): (i,) + (0,) * (n - 1))
            )
        else:
            specs.append(pl.BlockSpec(shape, lambda i, n=len(shape): (0,) * n))
    return specs


def seq_call(kernel, moving, fixed, outs, scratch, name, flops=0, trans=0):
    count = moving[0].shape[0]
    out_shape = [jax.ShapeDtypeStruct(shape, dtype) for shape, dtype, _ in outs]
    bytes_accessed = sum(a.size * a.dtype.itemsize for a in moving + fixed) + sum(
        o.size * o.dtype.itemsize for o in out_shape
    )
    return pl.pallas_call(
        kernel,
        grid=(count,),
        in_specs=block_specs(
            [(a.shape, True) for a in moving] + [(a.shape, False) for a in fixed]
        ),
        out_specs=block_specs([(shape, move) for shape, _, move in outs]),
        out_shape=out_shape,
        scratch_shapes=scratch,
        compiler_params=pltpu.CompilerParams(
            dimension_semantics=("arbitrary",), vmem_limit_bytes=60 * 1024 * 1024
        ),
        cost_estimate=pl.CostEstimate(
            flops=flops, bytes_accessed=bytes_accessed, transcendentals=trans
        ),
        name=name,
    )(*moving, *fixed)


def body(
    DP,
    M,
    inputs,
    cotangent,
    reset_mask,
    norm1_gain,
    w_input,
    w_branch,
    w_output,
    conv_weight,
    conv_bias,
    gate_a_weight,
    gate_a_bias,
    gate_x_weight,
    gate_x_bias,
    decay_param,
    norm2_gain,
    w_gate,
    w_up,
    w_down,
):
    heads_here, bw_here, bw = gate_a_weight.shape
    t = 4 if heads_here % 4 == 0 and DP % 4 == 0 else 2
    O = DP // t
    hpg = heads_here // t
    nh = M * hpg
    L, FH = inputs.shape
    D = FH * M
    Dl = w_input.shape[0]
    Lc = L // M
    half_cols = t * Dl
    cz = w_input.shape[1] // t
    fz = w_gate.shape[1] // t
    C = M * cz
    FC = M * fz
    conv = conv_weight.shape[0]
    parts = t // 2

    i_dp = lax.axis_index("dp")
    z = lax.axis_index("mp")
    q = i_dp % t
    o = i_dp // t

    def tp(value, j):
        return lax.ppermute(value, "dp", [(i, i ^ j) for i in range(DP)])

    def oshift(value, r):
        return lax.ppermute(
            value, "dp", [(i, ((i // t + r) % O) * t + i % t) for i in range(DP)]
        )

    def zshift(value, k):
        return lax.ppermute(value, "mp", [(i, (i + k) % M) for i in range(M)])

    def zline(value, k):
        got = lax.ppermute(
            value, "mp", [(i, i + k) for i in range(M) if 0 <= i + k < M]
        )
        return jnp.roll(got, k * cz, axis=-1)

    def after(value, *deps):
        return lax.optimization_barrier((value,) + deps)[0]

    def pick(array, index, axis=0):
        return lax.dynamic_index_in_dim(array, index, axis, keepdims=False)

    def to_chunk(value):
        rows = value.reshape(M, Lc, FH)
        own = jnp.zeros((Lc, D), value.dtype)
        far = jnp.zeros((Lc, D), value.dtype)
        for k in range(M):
            piece = pick(rows, (z + k) % M)
            if k:
                piece = zshift(piece, k)
            column = ((z - k) % M) * FH
            own = lax.dynamic_update_slice(own, piece, (0, column))
            if parts > 1:
                far = lax.dynamic_update_slice(far, tp(piece, 2), (0, column))
        groups = [jnp.concatenate([own, tp(own, 1)])]
        if parts > 1:
            groups.append(jnp.concatenate([far, tp(far, 1)]))
        return own, groups

    def from_chunk(value):
        cols = value.reshape(Lc, M, FH)
        out = jnp.zeros((M, Lc, FH), value.dtype)
        for k in range(M):
            piece = pick(cols, (z + k) % M, 1)
            if k:
                piece = zshift(piece, k)
            out = lax.dynamic_update_slice(out, piece[None], ((z - k) % M, 0, 0))
        return out.reshape(L, FH)

    def spread(own):
        groups = [jnp.concatenate([own, tp(own, 1)])]
        if parts > 1:
            far = tp(own, 2)
            groups.append(jnp.concatenate([far, tp(far, 1)]))
        return groups

    def gather_sum(partials):
        total = None
        for p in reversed(range(parts)):
            part = partials[p]
            mine = part[:Lc].astype(F32) + tp(part[Lc:], 1).astype(F32)
            if p:
                mine = tp(mine.astype(BF), 2).astype(F32)
            total = mine if total is None else total + mine
        return total

    def gather_weight(mine, dep=None):
        rows = mine.shape[1]
        block = jnp.zeros((rows, half_cols), BF)
        for j in range(t):
            piece = pick(mine, q ^ j)
            if j:
                if dep is not None:
                    piece = after(piece, dep)
                piece = tp(piece, j)
            block = lax.dynamic_update_slice(block, piece, (0, (q ^ j) * Dl))
        full = jnp.zeros((M, rows, D), BF)
        for s in range(M):
            if s:
                block = zshift(block, 1)
            for r in range(O):
                piece = oshift(block, r) if r else block
                full = lax.dynamic_update_slice(
                    full, piece[None], (s, 0, ((o - r) % O) * half_cols)
                )
        return full, block

    def scatter_grad(grad):
        rows = grad.shape[1]
        total = None
        for r in range(O):
            piece = lax.dynamic_slice(
                grad, (0, 0, ((o + r) % O) * half_cols), (M, rows, half_cols)
            )
            piece = (oshift(piece, r) if r else piece).astype(F32)
            total = piece if total is None else total + piece
        if M > 1:
            moving = total[1].astype(BF)
            for s in range(1, M):
                moving = zshift(moving, 1)
                moving = moving.astype(F32) + total[(s + 1) % M]
                if s < M - 1:
                    moving = moving.astype(BF)
        else:
            moving = total[0]
        slots = []
        send = moving.astype(BF).reshape(rows, t, Dl)
        for j in range(t):
            piece = pick(send, q ^ j, 1)
            slots.append(tp(piece, j) if j else piece)
        slots = jnp.stack(slots)
        return jnp.stack([pick(slots, q ^ k) for k in range(t)]).astype(F32)

    def rel(array, axis):
        return jnp.stack([pick(array, (z - s) % M, axis) for s in range(M)], axis)

    gate_size = 2 * hpg * bw_here * bw
    gate_rows = -(-gate_size // (16 * Dl)) * 16
    gates_flat = jnp.stack([gate_a_weight, gate_x_weight]).reshape(
        2, t, hpg, bw_here, bw
    )
    gates_flat = gates_flat.transpose(1, 0, 2, 3, 4).reshape(t, gate_size)
    gates_flat = jnp.pad(gates_flat, ((0, 0), (0, gate_rows * Dl - gate_size)))
    mixer_mine = jnp.concatenate(
        [
            w_input.T.reshape(t, cz, Dl),
            w_branch.T.reshape(t, cz, Dl),
            gates_flat.reshape(t, gate_rows, Dl),
        ],
        axis=1,
    )

    own_in, groups_in = to_chunk(inputs)
    full_a, dep_a = gather_weight(mixer_mine)
    full_b, dep_b = gather_weight(w_output.reshape(t, cz, Dl), dep_a)
    full_g, dep_g = gather_weight(w_gate.T.reshape(t, fz, Dl), dep_b)
    full_u, dep_u = gather_weight(w_up.T.reshape(t, fz, Dl), dep_g)
    full_d, _ = gather_weight(w_down.reshape(t, fz, Dl), dep_u)
    _, groups_cot = to_chunk(after(cotangent, dep_a))

    w_in_t = full_a[:, :cz].reshape(C, D)
    w_br_t = full_a[:, cz : 2 * cz].reshape(C, D)
    gates = full_a[:, 2 * cz :].reshape(M, gate_rows, DP, Dl).transpose(0, 2, 1, 3)
    gates = gates.reshape(M, DP, gate_rows * Dl)[:, :, :gate_size]
    gates = gates.reshape(M, DP, 2, hpg, bw_here, bw).transpose(2, 0, 3, 1, 4, 5)
    gates = gates.reshape(2, nh, bw, bw)
    eye = jnp.eye(nh, dtype=BF)
    dense = (gates[:, :, :, None, :] * eye[None, :, None, :, None]).reshape(2, C, C)
    wa, wx = dense[0], dense[1]
    w_out = full_b.reshape(C, D)
    w_gate_t = full_g.reshape(FC, D)
    w_up_t = full_u.reshape(FC, D)
    w_dn = full_d.reshape(FC, D)

    ng, nc = norm1_gain.shape[0], conv_bias.shape[0]
    packed = jnp.concatenate(
        [
            norm1_gain,
            norm2_gain,
            conv_weight.reshape(-1),
            conv_bias,
            gate_a_bias,
            gate_x_bias,
            decay_param,
        ]
    )
    every = lax.all_gather(packed, ("mp", "dp"), axis=0, tiled=False).astype(F32)
    gain_one = every[:, :ng].reshape(1, D)
    gain_two = every[:, ng : 2 * ng].reshape(1, D)
    vectors = every[:, 2 * ng :].reshape(M, DP, conv + 4, nc).transpose(2, 0, 1, 3)
    vectors = pick(vectors.reshape(conv + 4, M, t, cz), q, 2)
    vectors = rel(vectors, 1).reshape(conv + 4, C)
    conv_w = vectors[:conv]
    decay = vectors[conv + 3]
    log_slope = -8.0 * jax.nn.softplus(decay)
    vec = jnp.stack(
        [vectors[conv], vectors[conv + 1], vectors[conv + 2], log_slope]
        + [jnp.zeros_like(decay)] * 4
    )

    starts = jnp.maximum(
        reset_mask, (jnp.arange(L) % SEQ == 0).astype(jnp.int32)
    )
    starts = jnp.stack([starts] + [tp(starts, j) for j in range(1, t)])
    open_ = 1.0 - starts.astype(F32)
    back1 = jnp.pad(open_, ((0, 0), (1, 0)))[:, :L]
    back2 = jnp.pad(open_, ((0, 0), (2, 0)))[:, :L]
    masks = jnp.stack(
        [open_, open_ * back1, open_ * back1 * back2, 1.0 - open_], axis=-1
    )
    masks = jnp.pad(masks, ((0, 0), (0, HALO), (0, 0)))
    masks = lax.dynamic_slice(masks, (0, z * Lc, 0), (t, Lc + HALO, 4))

    def normed(value, gain):
        wide = value.astype(F32)
        scale = lax.rsqrt(jnp.mean(wide * wide, axis=1, keepdims=True) + epsilon)
        return wide * scale, scale

    n1, rnn, gin, fwd, halos = [], [], [], [], []
    for p in range(parts):
        unit, _ = normed(groups_in[p], gain_one)
        n1.append((unit * gain_one).astype(BF))
        rnn.append(dot_nt(n1[p], w_in_t).reshape(2, Lc, C))
        gin.append(dot_nt(n1[p], w_br_t).reshape(2, Lc, C))
        halos.append(zline(rnn[p][:, Lc - HALO :], 1))
        shape = (2, Lc, C)
        fwd.append(
            seq_call(
                forward_kernel,
                [rnn[p], halos[p], masks[2 * p : 2 * p + 2]],
                [conv_w, vec, wa, wx],
                [(shape, F32, True)] * 5 + [((2, 8, C), F32, True)],
                [pltpu.VMEM((Lc + HALO, C), F32)],
                "recurrence",
                flops=2 * Lc * 2 * C * C * 4,
                trans=6 * 2 * Lc * C,
            )
        )

    def chain(ends, sign):
        total = jnp.zeros_like(ends[:, 4:5])
        for k in reversed(range(1, M)):
            got = zline(ends, sign * k)
            total = got[:, 4:5] + got[:, 0:1] * total
        return total

    state, mixer, cin = [], [], []
    rec_partial = []
    for p in range(parts):
        _, _, _, h, prod, ends = fwd[p]
        cin.append(chain(ends, 1))
        state.append(h + prod * cin[p])
        gelu, _ = gelu_parts(gin[p])
        mixer.append((gelu * state[p]).astype(BF).reshape(2 * Lc, C))
        rec_partial.append(dot_nn(mixer[p], w_out).astype(BF))
    resid_mid = own_in.astype(F32) + gather_sum(rec_partial)

    unit_two, scale_two = normed(resid_mid, gain_two)
    n2 = spread((unit_two * gain_two).astype(BF))
    gate_val = [dot_nt(v, w_gate_t) for v in n2]
    up_val = [dot_nt(v, w_up_t) for v in n2]
    hidden = [(gelu_parts(g)[0] * u).astype(BF) for g, u in zip(gate_val, up_val)]
    out_sum = gather_sum([dot_nn(h, w_dn).astype(BF) for h in hidden])
    output = from_chunk((resid_mid + out_sum).astype(BF))

    def summed(lefts, rights):
        total = None
        for left, right in zip(lefts, rights):
            term = dot_tn(left, right)
            total = term if total is None else total + term
        return total.astype(BF).reshape(M, -1, D)

    grad_down = scatter_grad(summed(hidden, groups_cot))
    d_gate, d_up, dn2_partial = [], [], []
    for p in range(parts):
        d_hidden = dot_nt(groups_cot[p], w_dn)
        gelu, slope = gelu_parts(gate_val[p])
        d_gate.append((d_hidden * up_val[p] * slope).astype(BF))
        d_up.append((d_hidden * gelu).astype(BF))
        dn2_partial.append(
            (dot_nn(d_gate[p], w_gate_t) + dot_nn(d_up[p], w_up_t)).astype(BF)
        )
    d_n2 = gather_sum(dn2_partial)
    grad_gate = scatter_grad(summed(d_gate, n2))
    grad_up = scatter_grad(summed(d_up, n2))

    def norm_back(grad, unit, scale, gain):
        weighted = grad * gain
        dots = jnp.mean(weighted * unit, axis=1, keepdims=True)
        return scale * (weighted - unit * dots), jnp.sum(grad * unit, axis=0)

    back_two, gain_two_grad = norm_back(d_n2, unit_two, scale_two, gain_two)
    d_mid = groups_cot[0][:Lc].astype(F32) + back_two
    d_branch = spread(d_mid.astype(BF))

    adj, grad_vec, grad_wa, grad_wx = [], 0.0, 0.0, 0.0
    d_rnn, d_gin, dn1_partial = [], [], []
    grad_output = scatter_grad(summed(mixer, d_branch))
    for p in range(parts):
        d_mixer = dot_nt(d_branch[p], w_out).reshape(2, Lc, C)
        mixed, gate_a, gate_x = fwd[p][:3]
        here = masks[2 * p : 2 * p + 2]
        shape = (2, Lc, C)
        lam, prod, dgi, ends = seq_call(
            adjoint_kernel,
            [d_mixer, gin[p], state[p], gate_a, here],
            [vec],
            [(shape, F32, True)] * 2
            + [(shape, BF, True), ((2, 8, C), F32, True)],
            [],
            "adjoint",
            trans=2 * 2 * Lc * C,
        )
        mu = chain(ends, -1)
        edge = jnp.concatenate(
            [jnp.broadcast_to(cin[p], (2, 4, C)), jnp.broadcast_to(mu, (2, 4, C))], 1
        )
        drnn, head, tail, wag, wxg, vg = seq_call(
            backward_kernel,
            [
                lam,
                prod,
                state[p],
                gate_a,
                gate_x,
                mixed,
                rnn[p],
                halos[p],
                here,
                edge,
            ],
            [conv_w, vec, wa, wx],
            [
                (shape, BF, True),
                ((2, HALO, C), F32, True),
                ((2, HALO, C), F32, True),
                ((C, C), F32, False),
                ((C, C), F32, False),
                ((8, 8, C), F32, False),
            ],
            [pltpu.VMEM((Lc + HALO, C), F32)] * 3,
            "recurrence_back",
            flops=2 * Lc * 2 * C * C * 4,
            trans=4 * 2 * Lc * C,
        )
        following = zline(head, -1)
        fix = [jnp.zeros((2, 1, C), F32)] * HALO
        for k in range(1, 4):
            for n in range(k):
                row = HALO - k + n
                fix[row] = fix[row] + conv_w[k] * (
                    here[:, Lc + n : Lc + n + 1, k - 1 : k] * following[:, n : n + 1]
                )
        tail = (tail + jnp.concatenate(fix, axis=1)).astype(BF)
        drnn = lax.dynamic_update_slice(drnn, tail, (0, Lc - HALO, 0))
        grad_vec = grad_vec + vg
        grad_wa = grad_wa + wag
        grad_wx = grad_wx + wxg
        d_rnn.append(drnn.reshape(2 * Lc, C))
        d_gin.append(dgi.reshape(2 * Lc, C))
        dn1_partial.append(
            (dot_nn(d_rnn[p], w_in_t) + dot_nn(d_gin[p], w_br_t)).astype(BF)
        )
    d_n1 = gather_sum(dn1_partial)
    unit_one, scale_one = normed(own_in, gain_one)
    back_one, gain_one_grad = norm_back(d_n1, unit_one, scale_one, gain_one)
    input_grad = from_chunk((d_mid + back_one).astype(BF)).astype(F32)

    blocks = [
        jnp.stack([g[n * bw : (n + 1) * bw, n * bw : (n + 1) * bw] for n in range(nh)])
        for g in (grad_wa, grad_wx)
    ]
    gates_grad = jnp.stack(blocks).reshape(2, M, hpg, DP, bw_here, bw)
    gates_grad = gates_grad.transpose(1, 3, 0, 2, 4, 5).reshape(M, DP, gate_size)
    gates_grad = jnp.pad(
        gates_grad, ((0, 0), (0, 0), (0, gate_rows * Dl - gate_size))
    )
    gates_grad = gates_grad.reshape(M, DP, gate_rows, Dl).transpose(0, 2, 1, 3)
    gates_grad = gates_grad.reshape(M, gate_rows, D).astype(BF)
    grad_a = scatter_grad(
        jnp.concatenate([summed(d_rnn, n1), summed(d_gin, n1), gates_grad], axis=1)
    )

    small = jnp.sum(grad_vec, axis=1).reshape(2 * conv, M, cz)
    small = jnp.stack(
        [pick(small, (z - b) % M, 1) for b in range(M)], axis=1
    )
    slots = jnp.zeros((2 * conv, M, t, cz), F32)
    slots = lax.dynamic_update_slice(slots, small[:, :, None], (0, 0, q, 0))
    flat = jnp.concatenate([slots.reshape(-1), gain_one_grad, gain_two_grad])
    flat = lax.psum(flat, ("dp", "mp"))
    count = 2 * conv * M * t * cz
    vectors = flat[:count].reshape(2 * conv, M, DP, nc)
    mine = pick(pick(vectors, z, 1), i_dp, 1)
    place = z * DP + i_dp
    gain_one_grad = pick(flat[count : count + D].reshape(-1, ng), place)
    gain_two_grad = pick(flat[count + D :].reshape(-1, ng), place)
    decay_grad = mine[conv + 3] * (-8.0 * jax.nn.sigmoid(decay_param.astype(F32)))

    gates_back = grad_a[:, 2 * cz :].reshape(t, gate_rows * Dl)[:, :gate_size]
    gates_back = gates_back.reshape(t, 2, hpg, bw_here, bw).transpose(1, 0, 2, 3, 4)
    gates_back = gates_back.reshape(2, heads_here, bw_here, bw)

    return (
        output,
        input_grad,
        gain_one_grad,
        grad_a[:, :cz].reshape(t * cz, Dl).T,
        grad_a[:, cz : 2 * cz].reshape(t * cz, Dl).T,
        grad_output.reshape(t * cz, Dl),
        mine[:conv],
        mine[conv],
        gates_back[0],
        mine[conv + 1],
        gates_back[1],
        mine[conv + 2],
        decay_grad,
        gain_two_grad,
        grad_gate.reshape(t * fz, Dl).T,
        grad_up.reshape(t * fz, Dl).T,
        grad_down.reshape(t * fz, Dl),
    )


def solution(mesh):
    both = P(("mp", "dp"))
    wide = P("dp", "mp")
    tall = P("mp", "dp")
    taps = P(None, ("mp", "dp"))
    gate = P("mp", "dp", None)
    params = (both, wide, wide, tall, taps, both, gate, both, gate, both, both, both, wide, wide, tall)
    return jax.shard_map(
        functools.partial(body, mesh.shape["dp"], mesh.shape["mp"]),
        mesh=mesh,
        in_specs=(wide, wide, P("dp")) + params,
        out_specs=(wide, wide) + params,
        check_vma=False,
    )
```

```python
import functools

import jax
import jax.numpy as jnp
from jax import lax
from jax.experimental import pallas as pl
from jax.experimental.pallas import tpu as pltpu
from jax.sharding import PartitionSpec as P

SEQ = 2048
epsilon = 1e-06
BF = jnp.bfloat16
F32 = jnp.float32
ROWS = 64
HALO = 8


def dot_nt(left, right):
    return lax.dot_general(
        left, right, (((1,), (1,)), ((), ())), preferred_element_type=F32
    )


def dot_nn(left, right):
    return jnp.dot(left, right, preferred_element_type=F32)


def dot_tn(left, right):
    return lax.dot_general(
        left, right, (((0,), (0,)), ((), ())), preferred_element_type=F32
    )


def gelu_parts(value):
    inner = 0.7978845608028654 * (value + 0.044715 * value * value * value)
    tanh = jnp.tanh(inner)
    slope = 0.7978845608028654 * (1.0 + 3.0 * 0.044715 * value * value)
    gelu = 0.5 * value * (1.0 + tanh)
    grad = 0.5 * (1.0 + tanh) + 0.5 * value * (1.0 - tanh * tanh) * slope
    return gelu, grad


def sigmoid(value):
    return 1.0 / (1.0 + jnp.exp(-value))


def one_minus_exp(log_value):
    y = -2.0 * log_value
    series = y * (
        1.0
        - y
        * (1 / 2)
        * (
            1.0
            - y
            * (1 / 3)
            * (1.0 - y * (1 / 4) * (1.0 - y * (1 / 5) * (1.0 - y * (1 / 6))))
        )
    )
    return jnp.where(y < 0.25, series, 1.0 - jnp.exp(-y))


def conv_terms(ext, masks, rows):
    terms = [ext[HALO : HALO + rows]]
    for k in range(1, 4):
        moved = pltpu.roll(ext, k, axis=0)[HALO : HALO + rows]
        terms.append(moved * masks[:, k - 1 : k])
    return terms


def forward_kernel(
    rnn_ref,
    halo_ref,
    mask_ref,
    conv_ref,
    vec_ref,
    wa_ref,
    wx_ref,
    mixed_ref,
    ga_ref,
    gx_ref,
    h_ref,
    p_ref,
    end_ref,
    ext_ref,
):
    length, width = rnn_ref.shape[1:]
    ext_ref[0:HALO, :] = halo_ref[0]
    ext_ref[HALO:, :] = rnn_ref[0]
    row8 = lax.broadcasted_iota(jnp.int32, (ROWS, 1), 0) % 8

    def block(i, carry):
        h_in, p_in = carry
        r0 = pl.multiple_of(i * ROWS, ROWS)
        masks = mask_ref[0, pl.ds(r0, ROWS), :]
        terms = conv_terms(ext_ref[pl.ds(r0, ROWS + HALO), :], masks, ROWS)
        mixed = vec_ref[0:1, :] + conv_ref[0:1, :] * terms[0]
        for k in range(1, 4):
            mixed = mixed + conv_ref[k : k + 1, :] * terms[k]
        high = mixed.astype(BF)
        low = (mixed - high.astype(F32)).astype(BF)
        gate_a = sigmoid(
            dot_nn(high, wa_ref[...]) + dot_nn(low, wa_ref[...]) + vec_ref[1:2, :]
        )
        gate_x = sigmoid(
            dot_nn(high, wx_ref[...]) + dot_nn(low, wx_ref[...]) + vec_ref[2:3, :]
        )
        begins = masks[:, 3:4]
        log_a = gate_a * vec_ref[3:4, :]
        a = jnp.exp(log_a) * (1.0 - begins)
        scale = jnp.sqrt(one_minus_exp(log_a)) * (1.0 - begins) + begins
        b = mixed * gate_x * scale
        mixed_ref[0, pl.ds(r0, ROWS), :] = mixed
        ga_ref[0, pl.ds(r0, ROWS), :] = gate_a
        gx_ref[0, pl.ds(r0, ROWS), :] = gate_x
        for d in (1, 2, 4):
            valid = row8 >= d
            b = jnp.where(valid, a * pltpu.roll(b, d, axis=0) + b, b)
            a = jnp.where(valid, a * pltpu.roll(a, d, axis=0), a)
        for g in range(ROWS // 8):
            rows = slice(8 * g, 8 * g + 8)
            h = b[rows] + a[rows] * h_in
            p = a[rows] * p_in
            h_ref[0, pl.ds(r0 + 8 * g, 8), :] = h
            p_ref[0, pl.ds(r0 + 8 * g, 8), :] = p
            h_in = h[7:8]
            p_in = p[7:8]
        return h_in, p_in

    h_end, p_end = lax.fori_loop(
        0,
        length // ROWS,
        block,
        (jnp.zeros((1, width), F32), jnp.ones((1, width), F32)),
    )
    end_ref[0, 0:4, :] = jnp.broadcast_to(p_end, (4, width))
    end_ref[0, 4:8, :] = jnp.broadcast_to(h_end, (4, width))


def adjoint_kernel(
    dmix_ref,
    gate_ref,
    state_ref,
    ga_ref,
    mask_ref,
    vec_ref,
    lam_ref,
    q_ref,
    dgi_ref,
    end_ref,
):
    length, width = dmix_ref.shape[1:]
    row = lax.broadcasted_iota(jnp.int32, (ROWS, 1), 0)
    row8 = row % 8
    blocks = length // ROWS

    def block(i, carry):
        lam_in, q_in, a_next = carry
        r0 = pl.multiple_of((blocks - 1 - i) * ROWS, ROWS)
        here = pl.ds(r0, ROWS)
        begins = mask_ref[0, here, :][:, 3:4]
        d_mixer = dmix_ref[0, here, :]
        gelu, slope = gelu_parts(gate_ref[0, here, :])
        dgi_ref[0, here, :] = (d_mixer * state_ref[0, here, :] * slope).astype(BF)
        b = d_mixer * gelu
        a = jnp.exp(ga_ref[0, here, :] * vec_ref[3:4, :]) * (1.0 - begins)
        c = jnp.where(row == ROWS - 1, a_next, pltpu.roll(a, ROWS - 1, axis=0))
        for d in (1, 2, 4):
            valid = row8 < 8 - d
            b = jnp.where(valid, c * pltpu.roll(b, ROWS - d, axis=0) + b, b)
            c = jnp.where(valid, c * pltpu.roll(c, ROWS - d, axis=0), c)
        for g in reversed(range(ROWS // 8)):
            rows = slice(8 * g, 8 * g + 8)
            lam = b[rows] + c[rows] * lam_in
            q = c[rows] * q_in
            lam_ref[0, pl.ds(r0 + 8 * g, 8), :] = lam
            q_ref[0, pl.ds(r0 + 8 * g, 8), :] = q
            lam_in = lam[0:1]
            q_in = q[0:1]
        return lam_in, q_in, a[0:1]

    one = jnp.ones((1, width), F32)
    lam0, q0, a0 = lax.fori_loop(
        0, blocks, block, (jnp.zeros((1, width), F32), one, one)
    )
    end_ref[0, 0:4, :] = jnp.broadcast_to(a0 * q0, (4, width))
    end_ref[0, 4:8, :] = jnp.broadcast_to(a0 * lam0, (4, width))


def fold8(value):
    total = value[0:8]
    for g in range(1, value.shape[0] // 8):
        total = total + value[8 * g : 8 * g + 8]
    return total


def backward_kernel(
    lam_ref,
    q_ref,
    state_ref,
    ga_ref,
    gx_ref,
    mixed_ref,
    rnn_ref,
    halo_ref,
    mask_ref,
    edge_ref,
    conv_ref,
    vec_ref,
    wa_ref,
    wx_ref,
    drnn_ref,
    head_ref,
    tail_ref,
    wag_ref,
    wxg_ref,
    vg_ref,
    ext_ref,
    prev_ref,
    dm_ref,
):
    length, width = lam_ref.shape[1:]
    first = pl.program_id(0) == 0

    @pl.when(first)
    def _():
        wag_ref[...] = jnp.zeros_like(wag_ref)
        wxg_ref[...] = jnp.zeros_like(wxg_ref)
        vg_ref[...] = jnp.zeros_like(vg_ref)

    ext_ref[0:HALO, :] = halo_ref[0]
    ext_ref[HALO:, :] = rnn_ref[0]
    prev_ref[0:HALO, :] = jnp.broadcast_to(edge_ref[0, 0:1, :], (HALO, width))
    prev_ref[HALO:, :] = state_ref[0]
    dm_ref[length:, :] = jnp.zeros((HALO, width), F32)

    def block(i, carry):
        r0 = pl.multiple_of(i * ROWS, ROWS)
        here = pl.ds(r0, ROWS)
        masks = mask_ref[0, here, :]
        begins = masks[:, 3:4]
        lam = lam_ref[0, here, :] + q_ref[0, here, :] * edge_ref[0, 4:5, :]
        before = pltpu.roll(prev_ref[pl.ds(r0, ROWS + HALO), :], 1, axis=0)[
            HALO : HALO + ROWS
        ]
        gate_a = ga_ref[0, here, :]
        gate_x = gx_ref[0, here, :]
        mixed = mixed_ref[0, here, :]
        log_a = gate_a * vec_ref[3:4, :]
        decay = jnp.exp(log_a)
        inv_scale = lax.rsqrt(one_minus_exp(log_a))
        scale_raw = jnp.sqrt(one_minus_exp(log_a))
        keep = 1.0 - begins
        scale = scale_raw * keep + begins
        through = lam * mixed
        d_log = lam * before * decay * keep + jnp.where(
            begins > 0.5, 0.0, through * gate_x * (-(decay * decay) * inv_scale)
        )
        log_gate = d_log * gate_a
        d_pre_a = log_gate * (1.0 - gate_a) * vec_ref[3:4, :]
        d_pre_x = through * scale * gate_x * (1.0 - gate_x)
        pa = d_pre_a.astype(BF)
        px = d_pre_x.astype(BF)
        mb = mixed.astype(BF)
        d_mixed = (
            lam * gate_x * scale + dot_nt(pa, wa_ref[...]) + dot_nt(px, wx_ref[...])
        )
        dm_ref[here, :] = d_mixed
        wag_ref[...] += dot_tn(mb, pa)
        wxg_ref[...] += dot_tn(mb, px)
        terms = conv_terms(ext_ref[pl.ds(r0, ROWS + HALO), :], masks, ROWS)
        sums = [d_mixed * term for term in terms]
        sums += [d_mixed, d_pre_a, d_pre_x, log_gate]
        for n, value in enumerate(sums):
            vg_ref[n] += fold8(value)
        return carry

    lax.fori_loop(0, length // ROWS, block, 0)

    def shift(i, carry):
        r0 = pl.multiple_of(i * ROWS, ROWS)
        ext = dm_ref[pl.ds(r0, ROWS + HALO), :]
        masks = mask_ref[0, pl.ds(r0, ROWS + HALO), :]
        total = conv_ref[0:1, :] * ext[0:ROWS]
        for k in range(1, 4):
            moved = pltpu.roll(ext * masks[:, k - 1 : k], ROWS + HALO - k, axis=0)
            total = total + conv_ref[k : k + 1, :] * moved[0:ROWS]
        drnn_ref[0, pl.ds(r0, ROWS), :] = total.astype(BF)

        @pl.when(i == length // ROWS - 1)
        def _():
            tail_ref[0] = total[ROWS - HALO :]

        return carry

    lax.fori_loop(0, length // ROWS, shift, 0)
    head_ref[0] = dm_ref[0:HALO, :]


def block_specs(shapes):
    specs = []
    for shape, moving in shapes:
        if moving:
            specs.append(
                pl.BlockSpec((1,) + shape[1:], lambda i, n=len(shape): (i,) + (0,) * (n - 1))
            )
        else:
            specs.append(pl.BlockSpec(shape, lambda i, n=len(shape): (0,) * n))
    return specs


def seq_call(kernel, moving, fixed, outs, scratch, name, flops=0, trans=0):
    count = moving[0].shape[0]
    out_shape = [jax.ShapeDtypeStruct(shape, dtype) for shape, dtype, _ in outs]
    bytes_accessed = sum(a.size * a.dtype.itemsize for a in moving + fixed) + sum(
        o.size * o.dtype.itemsize for o in out_shape
    )
    return pl.pallas_call(
        kernel,
        grid=(count,),
        in_specs=block_specs(
            [(a.shape, True) for a in moving] + [(a.shape, False) for a in fixed]
        ),
        out_specs=block_specs([(shape, move) for shape, _, move in outs]),
        out_shape=out_shape,
        scratch_shapes=scratch,
        compiler_params=pltpu.CompilerParams(
            dimension_semantics=("arbitrary",), vmem_limit_bytes=60 * 1024 * 1024
        ),
        cost_estimate=pl.CostEstimate(
            flops=flops, bytes_accessed=bytes_accessed, transcendentals=trans
        ),
        name=name,
    )(*moving, *fixed)


def body(
    DP,
    M,
    inputs,
    cotangent,
    reset_mask,
    norm1_gain,
    w_input,
    w_branch,
    w_output,
    conv_weight,
    conv_bias,
    gate_a_weight,
    gate_a_bias,
    gate_x_weight,
    gate_x_bias,
    decay_param,
    norm2_gain,
    w_gate,
    w_up,
    w_down,
):
    heads_here, bw_here, bw = gate_a_weight.shape
    t = 4 if heads_here % 4 == 0 and DP % 4 == 0 else 2
    O = DP // t
    hpg = heads_here // t
    nh = M * hpg
    L, FH = inputs.shape
    D = FH * M
    Dl = w_input.shape[0]
    Lc = L // M
    half = t * Dl
    cz = w_input.shape[1] // t
    fz = w_gate.shape[1] // t
    C = M * cz
    FC = M * fz
    conv = conv_weight.shape[0]
    parts = t // 2
    last = parts - 1

    i_dp = lax.axis_index("dp")
    z = lax.axis_index("mp")
    q = i_dp % t
    o = i_dp // t

    def tp(value, j):
        return lax.ppermute(value, "dp", [(i, i ^ j) for i in range(DP)])

    def oshift(value, r):
        return lax.ppermute(
            value, "dp", [(i, ((i // t + r) % O) * t + i % t) for i in range(DP)]
        )

    def zshift(value, k):
        return lax.ppermute(value, "mp", [(i, (i + k) % M) for i in range(M)])

    def zline(value, k):
        got = lax.ppermute(
            value, "mp", [(i, i + k) for i in range(M) if 0 <= i + k < M]
        )
        return jnp.roll(got, k * cz, axis=-1)

    class Live(dict):
        __getattr__ = dict.__getitem__
        __setattr__ = dict.__setitem__

        def barrier(self):
            held = lax.optimization_barrier(dict(self))
            self.clear()
            self.update(held)

        def take(self, name):
            return self.pop(name)

    v = Live()

    def cut(array, index, size, axis):
        return lax.dynamic_slice_in_dim(array, index * size, size, axis)

    def put(array, piece, *starts):
        return lax.dynamic_update_slice(array, piece, starts)

    def pick(array, index, axis=0):
        return lax.dynamic_index_in_dim(array, index, axis, keepdims=False)

    def chunk_pieces(value):
        pieces = [cut(value, (z + k) % M, Lc, 0) for k in range(M)]
        return [zshift(piece, k) if k else piece for k, piece in enumerate(pieces)]

    def joined(pieces):
        own = jnp.zeros((Lc, D), pieces[0].dtype)
        for k, piece in enumerate(pieces):
            own = put(own, piece, 0, ((z - k) % M) * FH)
        return own

    def far(value):
        return tp(value, 2) if parts > 1 else None

    def back_pieces(value):
        return [cut(value, (z + k) % M, FH, 1) for k in range(M)]

    def back_joined(pieces):
        out = jnp.zeros((L, FH), pieces[0].dtype)
        for k, piece in enumerate(pieces):
            out = put(out, piece, ((z - k) % M) * Lc, 0)
        return out

    def send_sum(part, p):
        mine = part[:Lc].astype(F32) + tp(part[Lc:], 1).astype(F32)
        if p:
            mine = tp(mine.astype(BF), 2).astype(F32)
        return mine

    def stacked(blocks):
        return jnp.concatenate(blocks) if len(blocks) > 1 else blocks[0]

    def parted(joint, blocks):
        at, out = 0, []
        for block in blocks:
            out.append(joint[at : at + block.shape[0]])
            at += block.shape[0]
        return out

    def exchange(mine):
        if parts == 1:
            return [mine(q), tp(mine(q ^ 1), 1)]
        got = tp(jnp.stack([mine(q ^ 1), mine(q ^ 3)]), 1)
        after = tp(jnp.stack([mine(q ^ 2), got[1]]), 2)
        return [mine(q), got[0], after[0], after[1]]

    def from_group(pieces):
        block = jnp.zeros((pieces[0].shape[0], half), BF)
        for j, piece in enumerate(pieces):
            block = put(block, piece, 0, (q ^ j) * Dl)
        return block

    def to_groups(*blocks):
        joint = stacked(blocks)
        got = [parted(oshift(joint, r), blocks) for r in range(1, O)]
        return [[g[n] for g in got] for n in range(len(blocks))]

    def ring_next(*blocks):
        return parted(zshift(stacked(blocks), 1), blocks)

    def fill(full, block, others, s):
        rows = block.shape[0]
        for r, piece in enumerate([block] + others):
            full = put(full, piece, s * rows, ((o - r) % O) * half)
        return full

    def grad_y(*grads):
        own = [cut(g, o, half, 1) for g in grads]
        got = [
            parted(oshift(stacked([cut(g, (o + r) % O, half, 1) for g in grads]), r), own)
            for r in range(1, O)
        ]
        return [[own[n]] + [g[n] for g in got] for n in range(len(grads))]

    def slot(pieces, k):
        size = pieces[0].shape[0] // M
        return sum(piece[k * size : (k + 1) * size].astype(F32) for piece in pieces)

    def ring_step(*rings):
        sends = []
        for pieces, k, moving in rings:
            total = slot(pieces, k)
            if moving is not None:
                total = total + moving.astype(F32)
            sends.append(total.astype(BF))
        return ring_next(*sends)

    def ring_end(pieces, moving):
        for k in range(4, M):
            (moving,) = ring_step((pieces, k, moving))
        return (moving.astype(F32) + slot(pieces, 0)).astype(BF)

    def direct_sends(*grads):
        return [[slot(pieces, k).astype(BF) for pieces in grads] for k in range(M)]

    def grad_end(pieces):
        size = pieces[0].shape[0]
        out = jnp.zeros((t * size, Dl), BF)
        for j, piece in enumerate(pieces):
            out = put(out, piece, (q ^ j) * size, 0)
        return out

    def exchange_grads(*totals):
        joint = stacked(totals)
        got = [
            parted(piece, totals) for piece in exchange(lambda k: cut(joint, k, Dl, 1))
        ]
        return [[g[n] for g in got] for n in range(len(totals))]

    ng, nc = norm1_gain.shape[0], conv_bias.shape[0]
    packed = jnp.concatenate(
        [
            norm1_gain,
            norm2_gain,
            conv_weight.reshape(-1),
            conv_bias,
            gate_a_bias,
            gate_x_bias,
            decay_param,
        ]
    )
    every = put(jnp.zeros((DP, packed.shape[0]), BF), packed[None], i_dp, 0)
    step = 1
    while step < DP:
        every = every + tp(every, step)
        step *= 2
    gate_size = 2 * hpg * bw_here * bw
    gate_rows = -(-(gate_size + 2 * conv * nc + ng) // (16 * Dl)) * 16
    gates_flat = jnp.stack([gate_a_weight, gate_x_weight]).reshape(
        2, t, hpg, bw_here, bw
    )
    gates_flat = gates_flat.transpose(1, 0, 2, 3, 4).reshape(t, gate_size)
    gates_flat = jnp.pad(gates_flat, ((0, 0), (0, gate_rows * Dl - gate_size)))
    mine_all = jnp.concatenate(
        [
            w_input.T.reshape(t, cz, Dl),
            w_branch.T.reshape(t, cz, Dl),
            gates_flat.reshape(t, gate_rows, Dl),
            w_output.reshape(t, cz, Dl),
            w_gate.T.reshape(t, fz, Dl),
            w_up.T.reshape(t, fz, Dl),
            w_down.reshape(t, fz, Dl),
        ],
        axis=1,
    )
    starts = jnp.maximum(reset_mask, (jnp.arange(L) % SEQ == 0).astype(jnp.int32))
    starts = jnp.stack([starts] + [tp(starts, j) for j in range(1, t)])
    open_ = 1.0 - starts.astype(F32)
    back1 = jnp.pad(open_, ((0, 0), (1, 0)))[:, :L]
    back2 = jnp.pad(open_, ((0, 0), (2, 0)))[:, :L]
    masks = jnp.stack([open_, open_ * back1, open_ * back1 * back2, 1.0 - open_], axis=1)
    masks = jnp.pad(masks, ((0, 0), (0, 0), (0, HALO)))
    masks = lax.dynamic_slice(masks, (0, 0, z * Lc), (t, 4, Lc + HALO))
    masks = masks.transpose(0, 2, 1)

    def normed(value, gain):
        wide = value.astype(F32)
        scale = lax.rsqrt(jnp.mean(wide * wide, axis=1, keepdims=True) + epsilon)
        return wide * scale, scale

    rows_a = 2 * cz + gate_rows
    v.z_in = chunk_pieces(inputs)
    v.blocks = exchange(lambda k: pick(mine_all, k))
    v.every, v.masks, v.cotangent = every, masks, cotangent
    v.barrier()

    block = from_group(v.take("blocks"))
    block_a = block[:rows_a]
    block_b = block[rows_a : rows_a + cz]
    block_g = block[rows_a + cz : rows_a + cz + 2 * fz]
    v.d = [block[rows_a + cz + 2 * fz :]]
    v.ring_a = [block_a] + [zshift(block_a, k) for k in range(1, M)]
    v.b, v.g = [block_b], [block_g]
    v.y_a, v.y_b, v.y_g = [[y] for y in to_groups(block_a, block_b, block_g)]
    v.every = [v.every] + [zshift(v.every, k) for k in range(1, M)]
    v.own_in = joined(v.take("z_in"))
    v.far_in = far(v.own_in)
    v.near_in = tp(v.own_in, 1)
    v.barrier()

    v.y_a = v.y_a + to_groups(*v.ring_a[1:])
    v.b = v.b + [zshift(v.b[0], k) for k in range(1, M)]
    v.g = v.g + ring_next(v.g[0])
    every = jnp.stack(v.take("every")).astype(F32)
    gains = jnp.stack([pick(every[:, :, : 2 * ng], (z - b) % M) for b in range(M)])
    gain_one = gains[:, :, :ng].reshape(1, D)
    gain_two = gains[:, :, ng:].reshape(1, D)
    vectors = every[:, :, 2 * ng :].reshape(M, DP, conv + 4, nc).transpose(2, 0, 1, 3)
    vectors = pick(vectors.reshape(conv + 4, M, t, cz), q, 2).reshape(conv + 4, C)
    conv_w = vectors[:conv]
    decay = vectors[conv + 3]
    log_slope = -8.0 * jax.nn.softplus(decay)
    vec = jnp.stack(
        [vectors[conv], vectors[conv + 1], vectors[conv + 2], log_slope]
        + [jnp.zeros_like(decay)] * 4
    )

    v.vec, v.conv_w, v.gain_one, v.gain_two = vec, conv_w, gain_one, gain_two
    groups_in = [jnp.concatenate([v.own_in, v.take("near_in")])]
    if parts > 1:
        groups_in.append(jnp.concatenate([v.far_in, tp(v.far_in, 1)]))
    v.take("far_in")
    v.n1 = [(normed(g, v.gain_one)[0] * v.gain_one).astype(BF) for g in groups_in]
    v.barrier()

    got = to_groups(*(v.b[1:] + v.g[1:]))
    v.y_b = v.y_b + got[: M - 1]
    v.y_g = v.y_g + got[M - 1 :]
    g_next, d_next = ring_next(v.g[-1], v.d[-1])
    v.g, v.d = v.g + [g_next], v.d + [d_next]
    w_in_t, w_br_t = jnp.zeros((C, D), BF), jnp.zeros((C, D), BF)
    rest = jnp.zeros((M * gate_rows, D), BF)
    for k, (mine, others) in enumerate(zip(v.take("ring_a"), v.take("y_a"))):
        w_in_t = fill(w_in_t, mine[:cz], [y[:cz] for y in others], k)
        w_br_t = fill(w_br_t, mine[cz : 2 * cz], [y[cz : 2 * cz] for y in others], k)
        rest = fill(rest, mine[2 * cz :], [y[2 * cz :] for y in others], k)
    rest = rest.reshape(M, gate_rows, DP, Dl).transpose(0, 2, 1, 3)
    rest = rest.reshape(M, DP, gate_rows * Dl)
    gates = rest[:, :, :gate_size].reshape(M, DP, 2, hpg, bw_here, bw)
    gates = gates.transpose(2, 0, 3, 1, 4, 5).reshape(2, nh, bw, bw)
    dense = []
    for kind in range(2):
        rows = [
            jnp.pad(gates[kind, n], ((0, 0), (n * bw, (nh - 1 - n) * bw)))
            for n in range(nh)
        ]
        dense.append(jnp.concatenate(rows))
    wa, wx = dense
    v.w_in_t, v.w_br_t, v.wa, v.wx = w_in_t, w_br_t, wa, wx

    def chain(ends, sign):
        total = jnp.zeros_like(ends[..., 4:5, :])
        for k in reversed(range(1, M)):
            got = zline(ends, sign * k)
            total = got[..., 4:5, :] + got[..., 0:1, :] * total
        return total

    shape = (2, Lc, C)

    def run_forward(p):
        return seq_call(
            forward_kernel,
            [v.rnn[p], v.halos[p], v.masks[2 * p : 2 * p + 2]],
            [v.conv_w, v.vec, v.wa, v.wx],
            [(shape, F32, True)] * 5 + [((2, 8, C), F32, True)],
            [pltpu.VMEM((Lc + HALO, C), F32)],
            "recurrence",
            flops=2 * Lc * 2 * C * C * 4,
            trans=6 * 2 * Lc * C,
        )

    v.rnn = [dot_nt(n, v.w_in_t).reshape(shape) for n in v.n1]
    v.gin = [dot_nt(n, v.w_br_t).reshape(shape) for n in v.n1]
    tails = jnp.stack([r[:, Lc - HALO :] for r in v.rnn])
    v.halos = list(zline(tails, 1))
    v.fwd = [None] * parts
    v.fwd[last] = run_forward(last)
    v.barrier()

    got = to_groups(v.g[2], v.d[0])
    v.y_g, v.y_d = v.y_g + [got[0]], [got[1]]
    g_next, d_next = ring_next(v.g[-1], v.d[-1])
    v.g, v.d = v.g + [g_next], v.d + [d_next]
    while len(v.g) < M:
        v.g = v.g + ring_next(v.g[-1])
    w_out = jnp.zeros((C, D), BF)
    for k, (mine, others) in enumerate(zip(v.take("b"), v.take("y_b"))):
        w_out = fill(w_out, mine, others, k)
    v.w_out = w_out
    for p in range(last):
        v.fwd[p] = run_forward(p)
    enters = chain(jnp.stack([f[5] for f in v.fwd]), 1)
    v.cin, v.state, v.mixer = [], [], []
    for p in range(parts):
        _, _, _, h, prod, _ = v.fwd[p]
        v.cin.append(enters[p])
        v.state.append(h + prod * v.cin[p])
        v.mixer.append((gelu_parts(v.gin[p])[0] * v.state[p]).astype(BF).reshape(2 * Lc, C))
    v.fwd = [f[:3] for f in v.fwd]
    v.barrier()

    got = to_groups(*(v.g[3:] + v.d[1:2]))
    v.y_g, v.y_d = v.y_g + got[:-1], v.y_d + got[-1:]
    while len(v.d) < M:
        v.d = v.d + ring_next(v.d[-1])
    rec_sum = None
    for p in reversed(range(parts)):
        part = send_sum(dot_nn(v.mixer[p], v.w_out).astype(BF), p)
        rec_sum = part if rec_sum is None else rec_sum + part
    v.resid_mid = v.own_in.astype(F32) + rec_sum
    v.unit_two, v.scale_two = normed(v.resid_mid, v.gain_two)
    v.n2_own = (v.unit_two * v.gain_two).astype(BF)
    v.barrier()

    v.y_d = v.y_d + to_groups(*v.d[2:])
    w_gate_t, w_up_t = jnp.zeros((FC, D), BF), jnp.zeros((FC, D), BF)
    for k, (mine, others) in enumerate(zip(v.take("g"), v.take("y_g"))):
        w_gate_t = fill(w_gate_t, mine[:fz], [y[:fz] for y in others], k)
        w_up_t = fill(w_up_t, mine[fz:], [y[fz:] for y in others], k)
    v.w_gate_t, v.w_up_t = w_gate_t, w_up_t
    v.z_cot = chunk_pieces(v.take("cotangent"))
    v.n2_far = far(v.n2_own)
    v.n2 = [jnp.concatenate([v.n2_own, tp(v.n2_own, 1)])]
    v.take("n2_own")

    def mlp_forward(p):
        gate, up = dot_nt(v.n2[p], v.w_gate_t), dot_nt(v.n2[p], v.w_up_t)
        return gate, up, (gelu_parts(gate)[0] * up).astype(BF)

    v.mlp = [mlp_forward(0)]
    v.barrier()

    w_dn = jnp.zeros((FC, D), BF)
    for k, (mine, others) in enumerate(zip(v.take("d"), v.take("y_d"))):
        w_dn = fill(w_dn, mine, others, k)
    v.w_dn = w_dn
    cot_own = joined(v.take("z_cot"))
    v.cot = [jnp.concatenate([cot_own, tp(cot_own, 1)])]
    v.far_cot = far(cot_own)
    if parts > 1:
        v.n2.append(jnp.concatenate([v.n2_far, tp(v.n2_far, 1)]))
        v.mlp.append(mlp_forward(1))
    v.take("n2_far")
    v.barrier()

    def summed(lefts, rights):
        total = None
        for left, right in zip(lefts, rights):
            term = dot_tn(left, right)
            total = term if total is None else total + term
        return total.astype(BF)

    if parts > 1:
        v.cot.append(jnp.concatenate([v.far_cot, tp(v.far_cot, 1)]))
    v.take("far_cot")

    def mlp_back(p):
        d_hidden = dot_nt(v.cot[p], v.w_dn)
        gate, up, _ = v.mlp[p]
        gelu, slope = gelu_parts(gate)
        return (d_hidden * up * slope).astype(BF), (d_hidden * gelu).astype(BF)

    def mlp_back_in(p):
        gate, up = v.d_mlp[p]
        return (dot_nn(gate, v.w_gate_t) + dot_nn(up, v.w_up_t)).astype(BF)

    v.grad_down = summed([m[2] for m in v.mlp], v.cot)
    v.d_mlp = [None] * parts
    v.d_mlp[last] = mlp_back(last)
    v.barrier()

    (v.y_down,) = grad_y(v.take("grad_down"))
    v.dn2 = [None] * parts
    v.dn2[last] = mlp_back_in(last)
    v.dn2_sum = send_sum(v.dn2[last], last) if last else None
    for p in range(last):
        v.d_mlp[p] = mlp_back(p)
        v.dn2[p] = mlp_back_in(p)
    v.grad_gate = summed([d[0] for d in v.d_mlp], v.n2)
    v.hidden = [m[2] for m in v.take("mlp")]
    v.cot_own = v.take("cot")[0][:Lc]
    v.barrier()

    (v.r_down,) = ring_step((v.y_down, 1, None))
    (v.y_gate,) = grad_y(v.take("grad_gate"))
    dn2_sum = v.take("dn2_sum")
    for p in reversed(range(last if last else 1)):
        part = send_sum(v.dn2[p], p)
        dn2_sum = part if dn2_sum is None else dn2_sum + part
    v.take("dn2")

    def norm_back(grad, unit, scale, gain):
        weighted = grad * gain
        dots = jnp.mean(weighted * unit, axis=1, keepdims=True)
        return scale * (weighted - unit * dots), jnp.sum(grad * unit, axis=0)

    back_two, v.gain_two_grad = norm_back(dn2_sum, v.unit_two, v.scale_two, v.gain_two)
    v.d_mid = v.take("cot_own").astype(F32) + back_two
    v.d_own = v.d_mid.astype(BF)
    v.far_branch = far(v.d_own)
    v.grad_up = summed([d[1] for d in v.d_mlp], v.n2)
    v.take("n2")
    v.take("d_mlp")
    v.out = [dot_nn(h, v.w_dn).astype(BF) for h in v.take("hidden")]
    v.barrier()

    v.r_down, v.r_gate = ring_step((v.y_down, 2, v.r_down), (v.y_gate, 1, None))
    (v.y_up,) = grad_y(v.take("grad_up"))
    v.d_branch = [jnp.concatenate([v.d_own, tp(v.d_own, 1)])]
    v.take("d_own")
    if parts > 1:
        v.d_branch.append(jnp.concatenate([v.far_branch, tp(v.far_branch, 1)]))
    v.take("far_branch")
    out_sum = None
    for p in reversed(range(parts)):
        part = send_sum(v.out[p], p)
        out_sum = part if out_sum is None else out_sum + part
    v.take("out")
    v.output = (v.take("resid_mid") + out_sum).astype(BF)

    def run_adjoint(p):
        return seq_call(
            adjoint_kernel,
            [
                dot_nt(v.d_branch[p], v.w_out).reshape(shape),
                v.gin[p],
                v.state[p],
                v.fwd[p][1],
                v.masks[2 * p : 2 * p + 2],
            ],
            [v.vec],
            [(shape, F32, True)] * 2 + [(shape, BF, True), ((2, 8, C), F32, True)],
            [],
            "adjoint",
            trans=2 * 2 * Lc * C,
        )

    v.adjoint = [run_adjoint(p) for p in range(parts)]
    enters = chain(jnp.stack([a[3] for a in v.adjoint]), -1)
    v.edges = [
        jnp.concatenate(
            [
                jnp.broadcast_to(v.cin[p], (2, 4, C)),
                jnp.broadcast_to(enters[p], (2, 4, C)),
            ],
            1,
        )
        for p in range(parts)
    ]
    v.take("cin")
    v.grad_output = summed(v.take("mixer"), v.take("d_branch"))
    v.d_gin = [v.adjoint[p][2].reshape(2 * Lc, C) for p in range(parts)]
    v.grad_branch = summed(v.d_gin, v.n1)
    v.barrier()

    v.r_down, v.r_gate, v.r_up = ring_step(
        (v.y_down, 3, v.r_down), (v.y_gate, 2, v.r_gate), (v.y_up, 1, None)
    )
    v.y_output, v.y_branch = grad_y(v.take("grad_output"), v.take("grad_branch"))
    pieces = back_pieces(v.take("output"))
    v.z_out = [zshift(piece, k) if k else piece for k, piece in enumerate(pieces)]
    grad_vec, grad_wa, grad_wx = 0.0, 0.0, 0.0
    v.d_rnn = [None] * parts
    for p in reversed(range(parts)):
        mixed, gate_a, gate_x = v.fwd[p]
        here = v.masks[2 * p : 2 * p + 2]
        lam, prod, _, _ = v.adjoint[p]
        drnn, head, tail, wag, wxg, vg = seq_call(
            backward_kernel,
            [
                lam,
                prod,
                v.state[p],
                gate_a,
                gate_x,
                mixed,
                v.rnn[p],
                v.halos[p],
                here,
                v.edges[p],
            ],
            [v.conv_w, v.vec, v.wa, v.wx],
            [
                (shape, BF, True),
                ((2, HALO, C), F32, True),
                ((2, HALO, C), F32, True),
                ((C, C), F32, False),
                ((C, C), F32, False),
                ((8, 8, C), F32, False),
            ],
            [pltpu.VMEM((Lc + HALO, C), F32)] * 3,
            "recurrence_back",
            flops=2 * Lc * 2 * C * C * 4,
            trans=4 * 2 * Lc * C,
        )
        following = zline(head, -1)
        fix = [jnp.zeros((2, 1, C), F32)] * HALO
        for k in range(1, 4):
            for n in range(k):
                row = HALO - k + n
                fix[row] = fix[row] + v.conv_w[k] * (
                    here[:, Lc + n : Lc + n + 1, k - 1 : k] * following[:, n : n + 1]
                )
        tail = (tail + jnp.concatenate(fix, axis=1)).astype(BF)
        drnn = put(drnn, tail, 0, Lc - HALO, 0)
        grad_vec = grad_vec + vg
        grad_wa = grad_wa + wag
        grad_wx = grad_wx + wxg
        v.d_rnn[p] = drnn.reshape(2 * Lc, C)
    for name in ("adjoint", "fwd", "state", "rnn", "halos", "edges", "gin"):
        v.take(name)
    v.grad_vec, v.grad_wa, v.grad_wx = grad_vec, grad_wa, grad_wx
    v.barrier()

    z_down = ring_end(v.take("y_down"), v.take("r_down"))
    v.r_gate, v.r_up = ring_step((v.y_gate, 3, v.r_gate), (v.y_up, 2, v.r_up))
    v.z_mixer = [
        zshift(stacked(send), M - k) if k else stacked(send)
        for k, send in enumerate(direct_sends(v.take("y_output"), v.take("y_branch")))
    ]
    v.output = back_joined(v.take("z_out"))
    gates_grad = jnp.stack(
        [
            jnp.stack(
                [g[n * bw : (n + 1) * bw, n * bw : (n + 1) * bw] for n in range(nh)]
            )
            for g in (v.take("grad_wa"), v.take("grad_wx"))
        ]
    )
    gates_grad = gates_grad.reshape(2, M, hpg, DP, bw_here, bw)
    gates_grad = gates_grad.transpose(1, 3, 0, 2, 4, 5).reshape(M, DP, gate_size)
    small = jnp.sum(v.take("grad_vec"), axis=1).reshape(2 * conv, M, O, nc)
    small = small.transpose(1, 2, 0, 3).reshape(M, O, 2 * conv * nc)
    small = put(jnp.zeros((M, DP, 2 * conv * nc), F32), small, 0, q * O, 0)
    gain_two_grad = v.take("gain_two_grad").reshape(M, DP, ng)
    gain_two_grad = jnp.stack([pick(gain_two_grad, (z - k) % M) for k in range(M)])
    gates_grad = jnp.concatenate([gates_grad, small, gain_two_grad], axis=2)
    gates_grad = jnp.pad(
        gates_grad, ((0, 0), (0, 0), (0, gate_rows * Dl - gates_grad.shape[2]))
    )
    gates_grad = gates_grad.reshape(M, DP, gate_rows, Dl).transpose(0, 2, 1, 3)
    gates_grad = gates_grad.reshape(M, gate_rows, D).astype(BF)
    grad_in = jnp.concatenate(
        [summed(v.d_rnn, v.n1).reshape(M, cz, D), gates_grad], axis=1
    ).reshape(M * (cz + gate_rows), D)
    (v.y_in,) = grad_y(grad_in)
    v.take("n1")
    dn1_sum = None
    for p in reversed(range(parts)):
        part = (dot_nn(v.d_rnn[p], v.w_in_t) + dot_nn(v.d_gin[p], v.w_br_t)).astype(BF)
        part = send_sum(part, p)
        dn1_sum = part if dn1_sum is None else dn1_sum + part
    v.dn1, v.z_down = dn1_sum, z_down
    for name in ("d_rnn", "d_gin", "w_in_t", "w_br_t", "wa", "wx", "masks", "vec"):
        v.take(name)
    v.barrier()

    z_gate = ring_end(v.take("y_gate"), v.take("r_gate"))
    (v.r_up,) = ring_step((v.y_up, 3, v.r_up))
    z_mixer = sum(piece.astype(F32) for piece in v.take("z_mixer")).astype(BF)
    v.tp_down, v.tp_gate, v.tp_mixer = exchange_grads(v.take("z_down"), z_gate, z_mixer)
    unit_one, scale_one = normed(v.own_in, v.gain_one)
    back_one, gain_one_grad = norm_back(v.take("dn1"), unit_one, scale_one, v.gain_one)
    pieces = back_pieces((v.d_mid + back_one).astype(BF))
    rows_in = cz + gate_rows
    sums = jnp.broadcast_to(gain_one_grad.astype(BF), (16, D))
    joints = []
    for k, (send,) in enumerate(direct_sends(v.take("y_in"))):
        there = (M - k) % M
        mine = [pieces[there], cut(sums, (z + there) % M, FH, 1)]
        mine += [send[:, n * FH : (n + 1) * FH] for n in range(half // FH)]
        joint = jnp.concatenate(mine)
        joints.append(zshift(joint, there) if there else joint)
    v.joints = joints
    v.barrier()

    parts_in = [joint[Lc + 16 :] for joint in v.joints]
    grad_in = sum(piece.astype(F32) for piece in parts_in).astype(BF)
    grad_in = jnp.concatenate(
        [grad_in[n * rows_in : (n + 1) * rows_in] for n in range(half // FH)], axis=1
    )
    z_up = ring_end(v.y_up, v.r_up)
    tp_up, tp_in = exchange_grads(z_up, grad_in)
    grad_up = grad_end(tp_up)
    rest_in = [piece[cz:].reshape(-1).astype(F32) for piece in tp_in]
    small = sum(piece[gate_size:] for piece in rest_in)
    grad_a = grad_end(tp_in).reshape(t, rows_in, Dl)
    input_grad = back_joined([v.joints[(M - j) % M][:Lc] for j in range(M)]).astype(F32)
    gain_one_grad = sum(joint[Lc].astype(F32) for joint in v.joints)
    step = 1
    while step < DP:
        gain_one_grad = gain_one_grad + tp(gain_one_grad, step)
        step *= 2
    gain_one_grad = cut(gain_one_grad, i_dp, ng, 0)
    grad_output = grad_end([piece[:cz] for piece in v.tp_mixer])
    grad_branch = grad_end([piece[cz:] for piece in v.tp_mixer])
    grad_down, grad_gate = grad_end(v.tp_down), grad_end(v.tp_gate)
    output = v.output

    mine = small[: 2 * conv * nc].reshape(2 * conv, nc)
    gain_two_grad = small[2 * conv * nc : 2 * conv * nc + ng]
    decay_grad = mine[conv + 3] * (-8.0 * jax.nn.sigmoid(decay_param.astype(F32)))

    gates_back = grad_a[:, cz:].reshape(t, gate_rows * Dl)[:, :gate_size]
    gates_back = gates_back.reshape(t, 2, hpg, bw_here, bw).transpose(1, 0, 2, 3, 4)
    gates_back = gates_back.reshape(2, heads_here, bw_here, bw).astype(F32)

    def flipped(value):
        rows = value.shape[-2] * (value.shape[0] if value.ndim > 2 else 1)
        return lax.optimization_barrier(value.reshape(rows, Dl)).T.astype(F32)

    return (
        output,
        input_grad,
        gain_one_grad,
        flipped(grad_a[:, :cz]),
        flipped(grad_branch),
        grad_output.astype(F32),
        mine[:conv],
        mine[conv],
        gates_back[0],
        mine[conv + 1],
        gates_back[1],
        mine[conv + 2],
        decay_grad,
        gain_two_grad,
        flipped(grad_gate),
        flipped(grad_up),
        grad_down.astype(F32),
    )


def solution(mesh):
    both = P(("mp", "dp"))
    wide = P("dp", "mp")
    tall = P("mp", "dp")
    taps = P(None, ("mp", "dp"))
    gate = P("mp", "dp", None)
    params = (both, wide, wide, tall, taps, both, gate, both, gate, both, both, both, wide, wide, tall)
    return jax.shard_map(
        functools.partial(body, mesh.shape["dp"], mesh.shape["mp"]),
        mesh=mesh,
        in_specs=(wide, wide, P("dp")) + params,
        out_specs=(wide, wide) + params,
        check_vma=False,
    )
```

```python
import functools

import jax
import jax.numpy as jnp
from jax import lax
from jax.experimental import pallas as pl
from jax.experimental.pallas import tpu as pltpu
from jax.sharding import PartitionSpec as P

SEQ = 2048
epsilon = 1e-06
BF = jnp.bfloat16
F32 = jnp.float32
ROWS = 64
HALO = 8


def dot_nt(left, right):
    return lax.dot_general(
        left, right, (((1,), (1,)), ((), ())), preferred_element_type=F32
    )


def dot_nn(left, right):
    return jnp.dot(left, right, preferred_element_type=F32)


def dot_tn(left, right):
    return lax.dot_general(
        left, right, (((0,), (0,)), ((), ())), preferred_element_type=F32
    )


def gelu_parts(value):
    inner = 0.7978845608028654 * (value + 0.044715 * value * value * value)
    tanh = jnp.tanh(inner)
    slope = 0.7978845608028654 * (1.0 + 3.0 * 0.044715 * value * value)
    gelu = 0.5 * value * (1.0 + tanh)
    grad = 0.5 * (1.0 + tanh) + 0.5 * value * (1.0 - tanh * tanh) * slope
    return gelu, grad


def sigmoid(value):
    return 1.0 / (1.0 + jnp.exp(-value))


def one_minus_exp(log_value):
    y = -2.0 * log_value
    series = y * (
        1.0
        - y
        * (1 / 2)
        * (
            1.0
            - y
            * (1 / 3)
            * (1.0 - y * (1 / 4) * (1.0 - y * (1 / 5) * (1.0 - y * (1 / 6))))
        )
    )
    return jnp.where(y < 0.25, series, 1.0 - jnp.exp(-y))


def conv_terms(ext, masks, rows):
    terms = [ext[HALO : HALO + rows]]
    for k in range(1, 4):
        moved = pltpu.roll(ext, k, axis=0)[HALO : HALO + rows]
        terms.append(moved * masks[:, k - 1 : k])
    return terms


def forward_kernel(
    rnn_ref,
    halo_ref,
    mask_ref,
    conv_ref,
    vec_ref,
    wa_ref,
    wx_ref,
    mixed_ref,
    ga_ref,
    gx_ref,
    h_ref,
    p_ref,
    end_ref,
    ext_ref,
):
    length, width = rnn_ref.shape[1:]
    ext_ref[0:HALO, :] = halo_ref[0]
    ext_ref[HALO:, :] = rnn_ref[0]
    row8 = lax.broadcasted_iota(jnp.int32, (ROWS, 1), 0) % 8

    def block(i, carry):
        h_in, p_in = carry
        r0 = pl.multiple_of(i * ROWS, ROWS)
        masks = mask_ref[0, pl.ds(r0, ROWS), :]
        terms = conv_terms(ext_ref[pl.ds(r0, ROWS + HALO), :], masks, ROWS)
        mixed = vec_ref[0:1, :] + conv_ref[0:1, :] * terms[0]
        for k in range(1, 4):
            mixed = mixed + conv_ref[k : k + 1, :] * terms[k]
        high = mixed.astype(BF)
        low = (mixed - high.astype(F32)).astype(BF)
        gate_a = sigmoid(
            dot_nn(high, wa_ref[...]) + dot_nn(low, wa_ref[...]) + vec_ref[1:2, :]
        )
        gate_x = sigmoid(
            dot_nn(high, wx_ref[...]) + dot_nn(low, wx_ref[...]) + vec_ref[2:3, :]
        )
        begins = masks[:, 3:4]
        log_a = gate_a * vec_ref[3:4, :]
        a = jnp.exp(log_a) * (1.0 - begins)
        scale = jnp.sqrt(one_minus_exp(log_a)) * (1.0 - begins) + begins
        b = mixed * gate_x * scale
        mixed_ref[0, pl.ds(r0, ROWS), :] = mixed
        ga_ref[0, pl.ds(r0, ROWS), :] = gate_a
        gx_ref[0, pl.ds(r0, ROWS), :] = gate_x
        for d in (1, 2, 4):
            valid = row8 >= d
            b = jnp.where(valid, a * pltpu.roll(b, d, axis=0) + b, b)
            a = jnp.where(valid, a * pltpu.roll(a, d, axis=0), a)
        for g in range(ROWS // 8):
            rows = slice(8 * g, 8 * g + 8)
            h = b[rows] + a[rows] * h_in
            p = a[rows] * p_in
            h_ref[0, pl.ds(r0 + 8 * g, 8), :] = h
            p_ref[0, pl.ds(r0 + 8 * g, 8), :] = p
            h_in = h[7:8]
            p_in = p[7:8]
        return h_in, p_in

    h_end, p_end = lax.fori_loop(
        0,
        length // ROWS,
        block,
        (jnp.zeros((1, width), F32), jnp.ones((1, width), F32)),
    )
    end_ref[0, 0:4, :] = jnp.broadcast_to(p_end, (4, width))
    end_ref[0, 4:8, :] = jnp.broadcast_to(h_end, (4, width))


def adjoint_kernel(
    dmix_ref,
    gate_ref,
    state_ref,
    ga_ref,
    mask_ref,
    vec_ref,
    lam_ref,
    q_ref,
    dgi_ref,
    end_ref,
):
    length, width = dmix_ref.shape[1:]
    row = lax.broadcasted_iota(jnp.int32, (ROWS, 1), 0)
    row8 = row % 8
    blocks = length // ROWS

    def block(i, carry):
        lam_in, q_in, a_next = carry
        r0 = pl.multiple_of((blocks - 1 - i) * ROWS, ROWS)
        here = pl.ds(r0, ROWS)
        begins = mask_ref[0, here, :][:, 3:4]
        d_mixer = dmix_ref[0, here, :]
        gelu, slope = gelu_parts(gate_ref[0, here, :])
        dgi_ref[0, here, :] = (d_mixer * state_ref[0, here, :] * slope).astype(BF)
        b = d_mixer * gelu
        a = jnp.exp(ga_ref[0, here, :] * vec_ref[3:4, :]) * (1.0 - begins)
        c = jnp.where(row == ROWS - 1, a_next, pltpu.roll(a, ROWS - 1, axis=0))
        for d in (1, 2, 4):
            valid = row8 < 8 - d
            b = jnp.where(valid, c * pltpu.roll(b, ROWS - d, axis=0) + b, b)
            c = jnp.where(valid, c * pltpu.roll(c, ROWS - d, axis=0), c)
        for g in reversed(range(ROWS // 8)):
            rows = slice(8 * g, 8 * g + 8)
            lam = b[rows] + c[rows] * lam_in
            q = c[rows] * q_in
            lam_ref[0, pl.ds(r0 + 8 * g, 8), :] = lam
            q_ref[0, pl.ds(r0 + 8 * g, 8), :] = q
            lam_in = lam[0:1]
            q_in = q[0:1]
        return lam_in, q_in, a[0:1]

    one = jnp.ones((1, width), F32)
    lam0, q0, a0 = lax.fori_loop(
        0, blocks, block, (jnp.zeros((1, width), F32), one, one)
    )
    end_ref[0, 0:4, :] = jnp.broadcast_to(a0 * q0, (4, width))
    end_ref[0, 4:8, :] = jnp.broadcast_to(a0 * lam0, (4, width))


def fold8(value):
    total = value[0:8]
    for g in range(1, value.shape[0] // 8):
        total = total + value[8 * g : 8 * g + 8]
    return total


def backward_kernel(
    lam_ref,
    q_ref,
    state_ref,
    ga_ref,
    gx_ref,
    mixed_ref,
    rnn_ref,
    halo_ref,
    mask_ref,
    edge_ref,
    conv_ref,
    vec_ref,
    wa_ref,
    wx_ref,
    drnn_ref,
    head_ref,
    tail_ref,
    wag_ref,
    wxg_ref,
    vg_ref,
    ext_ref,
    prev_ref,
    dm_ref,
):
    length, width = lam_ref.shape[1:]
    first = pl.program_id(0) == 0

    @pl.when(first)
    def _():
        wag_ref[...] = jnp.zeros_like(wag_ref)
        wxg_ref[...] = jnp.zeros_like(wxg_ref)
        vg_ref[...] = jnp.zeros_like(vg_ref)

    ext_ref[0:HALO, :] = halo_ref[0]
    ext_ref[HALO:, :] = rnn_ref[0]
    prev_ref[0:HALO, :] = jnp.broadcast_to(edge_ref[0, 0:1, :], (HALO, width))
    prev_ref[HALO:, :] = state_ref[0]
    dm_ref[length:, :] = jnp.zeros((HALO, width), F32)

    def block(i, carry):
        r0 = pl.multiple_of(i * ROWS, ROWS)
        here = pl.ds(r0, ROWS)
        masks = mask_ref[0, here, :]
        begins = masks[:, 3:4]
        lam = lam_ref[0, here, :] + q_ref[0, here, :] * edge_ref[0, 4:5, :]
        before = pltpu.roll(prev_ref[pl.ds(r0, ROWS + HALO), :], 1, axis=0)[
            HALO : HALO + ROWS
        ]
        gate_a = ga_ref[0, here, :]
        gate_x = gx_ref[0, here, :]
        mixed = mixed_ref[0, here, :]
        log_a = gate_a * vec_ref[3:4, :]
        decay = jnp.exp(log_a)
        inv_scale = lax.rsqrt(one_minus_exp(log_a))
        scale_raw = jnp.sqrt(one_minus_exp(log_a))
        keep = 1.0 - begins
        scale = scale_raw * keep + begins
        through = lam * mixed
        d_log = lam * before * decay * keep + jnp.where(
            begins > 0.5, 0.0, through * gate_x * (-(decay * decay) * inv_scale)
        )
        log_gate = d_log * gate_a
        d_pre_a = log_gate * (1.0 - gate_a) * vec_ref[3:4, :]
        d_pre_x = through * scale * gate_x * (1.0 - gate_x)
        pa = d_pre_a.astype(BF)
        px = d_pre_x.astype(BF)
        mb = mixed.astype(BF)
        d_mixed = (
            lam * gate_x * scale + dot_nt(pa, wa_ref[...]) + dot_nt(px, wx_ref[...])
        )
        dm_ref[here, :] = d_mixed
        wag_ref[...] += dot_tn(mb, pa)
        wxg_ref[...] += dot_tn(mb, px)
        terms = conv_terms(ext_ref[pl.ds(r0, ROWS + HALO), :], masks, ROWS)
        sums = [d_mixed * term for term in terms]
        sums += [d_mixed, d_pre_a, d_pre_x, log_gate]
        for n, value in enumerate(sums):
            vg_ref[n] += fold8(value)
        return carry

    lax.fori_loop(0, length // ROWS, block, 0)

    def shift(i, carry):
        r0 = pl.multiple_of(i * ROWS, ROWS)
        ext = dm_ref[pl.ds(r0, ROWS + HALO), :]
        masks = mask_ref[0, pl.ds(r0, ROWS + HALO), :]
        total = conv_ref[0:1, :] * ext[0:ROWS]
        for k in range(1, 4):
            moved = pltpu.roll(ext * masks[:, k - 1 : k], ROWS + HALO - k, axis=0)
            total = total + conv_ref[k : k + 1, :] * moved[0:ROWS]
        drnn_ref[0, pl.ds(r0, ROWS), :] = total.astype(BF)

        @pl.when(i == length // ROWS - 1)
        def _():
            tail_ref[0] = total[ROWS - HALO :]

        return carry

    lax.fori_loop(0, length // ROWS, shift, 0)
    head_ref[0] = dm_ref[0:HALO, :]


def block_specs(shapes):
    specs = []
    for shape, moving in shapes:
        if moving:
            specs.append(
                pl.BlockSpec((1,) + shape[1:], lambda i, n=len(shape): (i,) + (0,) * (n - 1))
            )
        else:
            specs.append(pl.BlockSpec(shape, lambda i, n=len(shape): (0,) * n))
    return specs


def cost(time):
    return pl.CostEstimate(flops=int(time * 2.5e8), bytes_accessed=0, transcendentals=0)


NT = (((1,), (1,)), ((), ()))
NN = (((1,), (0,)), ((), ()))
TN = (((0,), (0,)), ((), ()))


def seq_call(kernel, moving, fixed, outs, scratch, name, time):
    count = moving[0].shape[0]
    return pl.pallas_call(
        kernel,
        grid=(count,),
        in_specs=block_specs(
            [(a.shape, True) for a in moving] + [(a.shape, False) for a in fixed]
        ),
        out_specs=block_specs([(shape, move) for shape, _, move in outs]),
        out_shape=[jax.ShapeDtypeStruct(shape, dtype) for shape, dtype, _ in outs],
        scratch_shapes=scratch,
        compiler_params=pltpu.CompilerParams(
            dimension_semantics=("arbitrary",), vmem_limit_bytes=60 * 1024 * 1024
        ),
        cost_estimate=cost(time),
        name=name,
    )(*moving, *fixed)


def products(dims, sums, extras, outs, finish, name, base=None, width=None, halves=False):
    full = sums[0][0][1].shape[0 if dims == NT else 1]
    width = width or full
    columns = min(256, width)
    lefts, rights, where = [], [], []
    for pairs in sums:
        places = []
        for left, right in pairs:
            left = left if isinstance(left, tuple) else (left, 0, 1)
            known = [n for n, other in enumerate(lefts) if other[0] is left[0]]
            places.append(known[0] if known else len(lefts))
            if not known:
                lefts.append(left)
            rights.append(right)
        where.append(places)
    array, _, count = lefts[0]
    rows = array.shape[1] if dims == TN else array.shape[0] // count
    cuts = 2 if halves else 1
    near = len(lefts) + len(rights)

    def kernel(_, *refs):
        at, totals = len(lefts), []
        for places in where:
            total = None
            for place in places:
                term = lax.dot_general(
                    refs[place][...], refs[at][...], dims, preferred_element_type=F32
                )
                total = term if total is None else total + term
                at += 1
            totals.append(total)
        values = finish(*totals, *(ref[...] for ref in refs[near : near + len(extras)]))
        size = rows // cuts
        at = near + len(extras)
        for value in values:
            for n in range(cuts):
                refs[at][...] = value[n * size : (n + 1) * size].astype(refs[at].dtype)
                at += 1

    def whole(left):
        array, part, count = left
        shape = (array.shape[0] // count, array.shape[1])
        return pl.BlockSpec(shape, lambda j, b: (part, 0))

    def moving(array):
        if dims == NT:
            return pl.BlockSpec((columns, array.shape[1]), lambda j, b: (b[0] + j, 0))
        return pl.BlockSpec((array.shape[0], columns), lambda j, b: (0, b[0] + j))

    base = jnp.zeros((1,), jnp.int32) if base is None else (base // columns).reshape(1)
    tile = pl.BlockSpec((rows, columns), lambda j, b: (0, j))
    part = pl.BlockSpec((rows // cuts, columns), lambda j, b: (0, j))
    return pl.pallas_call(
        kernel,
        grid_spec=pltpu.PrefetchScalarGridSpec(
            num_scalar_prefetch=1,
            grid=(width // columns,),
            in_specs=[whole(a) for a in lefts]
            + [moving(a) for a in rights]
            + [tile] * len(extras),
            out_specs=[part] * (len(outs) * cuts),
        ),
        out_shape=[
            jax.ShapeDtypeStruct((rows // cuts, width), dtype)
            for dtype in outs
            for _ in range(cuts)
        ],
        compiler_params=pltpu.CompilerParams(
            dimension_semantics=("arbitrary",), vmem_limit_bytes=60 * 1024 * 1024
        ),
        cost_estimate=cost(sum(a.size for a in rights) // (width and full) * width * rows / 3.4e8),
        name=name,
    )(base, *(left[0] for left in lefts), *rights, *extras)


@jax.tree_util.register_pytree_node_class
class Joint:
    def __init__(self, rows, sizes):
        self.rows, self.sizes = rows, sizes

    def tree_flatten(self):
        return (self.rows,), self.sizes

    @classmethod
    def tree_unflatten(cls, sizes, children):
        return cls(children[0], sizes)

    def parts(self):
        at, out = 0, []
        for size in self.sizes:
            out.append(self.rows[at : at + size])
            at += size
        return out


def body(
    DP,
    M,
    inputs,
    cotangent,
    reset_mask,
    norm1_gain,
    w_input,
    w_branch,
    w_output,
    conv_weight,
    conv_bias,
    gate_a_weight,
    gate_a_bias,
    gate_x_weight,
    gate_x_bias,
    decay_param,
    norm2_gain,
    w_gate,
    w_up,
    w_down,
):
    heads_here, bw_here, bw = gate_a_weight.shape
    t = 4 if heads_here % 4 == 0 and DP % 4 == 0 else 2
    O = DP // t
    hpg = heads_here // t
    nh = M * hpg
    L, FH = inputs.shape
    D = FH * M
    Dl = w_input.shape[0]
    Lc = L // M
    half = t * Dl
    cz = w_input.shape[1] // t
    fz = w_gate.shape[1] // t
    C = M * cz
    FC = M * fz
    conv = conv_weight.shape[0]
    parts = t // 2
    last = parts - 1

    i_dp = lax.axis_index("dp")
    z = lax.axis_index("mp")
    q = i_dp % t
    o = i_dp // t

    def tp(value, j):
        return lax.ppermute(value, "dp", [(i, i ^ j) for i in range(DP)])

    def oshift(value, r):
        return lax.ppermute(
            value, "dp", [(i, ((i // t + r) % O) * t + i % t) for i in range(DP)]
        )

    def zshift(value, k):
        return lax.ppermute(value, "mp", [(i, (i + k) % M) for i in range(M)])

    def zline(value, k):
        got = lax.ppermute(
            value, "mp", [(i, i + k) for i in range(M) if 0 <= i + k < M]
        )
        return jnp.roll(got, k * cz, axis=-1)

    class Live(dict):
        __getattr__ = dict.__getitem__
        __setattr__ = dict.__setitem__

        def barrier(self):
            held = lax.optimization_barrier(dict(self))
            self.clear()
            self.update(held)

        def take(self, name):
            return self.pop(name)

    v = Live()

    def cut(array, index, size, axis):
        return lax.dynamic_slice_in_dim(array, index * size, size, axis)

    def put(array, piece, *starts):
        return lax.dynamic_update_slice(array, piece, starts)

    def pick(array, index, axis=0):
        return lax.dynamic_index_in_dim(array, index, axis, keepdims=False)

    def chunk_pieces(value, ahead=0, rider=None):
        if ahead:
            value = jnp.concatenate([jnp.zeros((ahead, FH), value.dtype), value])
        pieces = [
            lax.dynamic_slice_in_dim(value, (z + k) % M * Lc, Lc + ahead, 0)
            for k in range(M)
        ]
        if rider is not None:
            pieces[1] = jnp.concatenate([pieces[1], rider])
        return [zshift(piece, k) if k else piece for k, piece in enumerate(pieces)]

    def joined(pieces):
        own = jnp.zeros((pieces[0].shape[0], D), pieces[0].dtype)
        for k, piece in enumerate(pieces):
            own = put(own, piece, 0, ((z - k) % M) * FH)
        return own

    def far(value):
        return tp(value, 2) if parts > 1 else None

    def back_pieces(value):
        return [cut(value, (z + k) % M, FH, 1) for k in range(M)]

    def back_joined(pieces):
        out = jnp.zeros((L, FH), pieces[0].dtype)
        for k, piece in enumerate(pieces):
            out = put(out, piece, ((z - k) % M) * Lc, 0)
        return out

    def send_sum(part, p):
        mine = part[0].astype(F32) + tp(part[1], 1).astype(F32)
        if p:
            mine = tp(mine.astype(BF), 2).astype(F32)
        return mine

    def stacked(blocks):
        return jnp.concatenate(blocks) if len(blocks) > 1 else blocks[0]

    def joint(transfer, blocks):
        return Joint(transfer(stacked(blocks)), tuple(b.shape[0] for b in blocks))

    def exchange(mine):
        if parts == 1:
            return [mine(q), tp(mine(q ^ 1), 1)]
        got = tp(jnp.stack([mine(q ^ 1), mine(q ^ 3)]), 1)
        after = tp(jnp.stack([mine(q ^ 2), got[1]]), 2)
        return [mine(q), got[0], after[0], after[1]]

    def from_group(pieces):
        block = jnp.zeros((pieces[0].shape[0], half), BF)
        for j, piece in enumerate(pieces):
            block = put(block, piece, 0, (q ^ j) * Dl)
        return block

    def to_groups(*blocks):
        return [joint(lambda b: oshift(b, r), blocks) for r in range(1, O)]

    def by_block(got):
        return [list(same) for same in zip(*(g.parts() for g in got))]

    def ring_next(*blocks):
        return joint(lambda b: zshift(b, 1), blocks)

    def fill_own(full, block, s):
        return put(full, block, s * block.shape[0], o * half)

    def fill_far(full, others, s):
        for r, piece in enumerate(others, 1):
            full = put(full, piece, s * piece.shape[0], ((o - r) % O) * half)
        return full

    def mixer_parts(block):
        return block[:cz], block[cz : 2 * cz], block[2 * cz :]

    def fill_mixer_far(full, others, s):
        split = [mixer_parts(piece) for piece in others]
        return [fill_far(f, [g[n] for g in split], s) for n, f in enumerate(full)]

    def folded(block):
        return jnp.concatenate(
            [block[:, n * FH : (n + 1) * FH] for n in range(half // FH)]
        )

    def unfolded(rows):
        size = rows.shape[0] // (half // FH)
        return jnp.concatenate(
            [rows[n * size : (n + 1) * size] for n in range(half // FH)], axis=1
        )

    def grad_y(*grads):
        return [g[0] for g in grads], to_groups_of(grads)

    def to_groups_of(grads):
        return [joint(lambda b: oshift(b, r), [g[r] for g in grads]) for r in range(1, O)]

    def y_parts(held):
        own, got = held
        return [list(same) for same in zip(own, *(g.parts() for g in got))]

    def slot(pieces, k):
        size = pieces[0].shape[0] // M
        return sum(piece[k * size : (k + 1) * size].astype(F32) for piece in pieces)

    def ring_sends(*rings):
        sends = []
        for pieces, k, moving in rings:
            total = slot(pieces, k)
            if moving is not None:
                total = total + moving.astype(F32)
            sends.append(total.astype(BF))
        return sends

    def ring_step(*rings):
        return ring_next(*ring_sends(*rings))

    def ring_end(pieces, moving):
        for k in range(4, M):
            (moving,) = ring_step((pieces, k, moving)).parts()
        return (moving.astype(F32) + slot(pieces, 0)).astype(BF)

    def direct_sends(*grads):
        return [[slot(pieces, k).astype(BF) for pieces in grads] for k in range(M)]

    def grad_end(pieces):
        size = pieces[0].shape[0]
        out = jnp.zeros((t * size, Dl), BF)
        for j, piece in enumerate(pieces):
            out = put(out, piece, (q ^ j) * size, 0)
        return out

    def exchange_grads(*totals):
        sizes = tuple(total.shape[0] for total in totals)
        rows = stacked(totals)
        return [Joint(p, sizes) for p in exchange(lambda k: cut(rows, k, Dl, 1))]

    def by_grad(got):
        return [list(same) for same in zip(*(g.parts() for g in got))]

    ng, nc = norm1_gain.shape[0], conv_bias.shape[0]
    packed = jnp.concatenate(
        [
            norm1_gain,
            norm2_gain,
            conv_weight.reshape(-1),
            conv_bias,
            gate_a_bias,
            gate_x_bias,
            decay_param,
        ]
    )
    gate_size = 2 * hpg * bw_here * bw
    gate_rows = -(-(gate_size + packed.shape[0]) // (16 * Dl)) * 16
    gates_flat = jnp.stack([gate_a_weight, gate_x_weight]).reshape(
        2, t, hpg, bw_here, bw
    )
    gates_flat = gates_flat.transpose(1, 0, 2, 3, 4).reshape(t, gate_size)
    extra = gate_size + packed.shape[0]
    gates_flat = jnp.concatenate(
        [
            gates_flat,
            jnp.broadcast_to(packed, (t,) + packed.shape),
            jnp.zeros((t, gate_rows * Dl - extra), BF),
        ],
        axis=1,
    )
    mine_all = jnp.concatenate(
        [
            w_input.T.reshape(t, cz, Dl),
            w_branch.T.reshape(t, cz, Dl),
            gates_flat.reshape(t, gate_rows, Dl),
            w_output.reshape(t, cz, Dl),
            w_gate.T.reshape(t, fz, Dl),
            w_up.T.reshape(t, fz, Dl),
            w_down.reshape(t, fz, Dl),
        ],
        axis=1,
    )
    def normed(value, gain):
        wide = value.astype(F32)
        scale = lax.rsqrt(jnp.mean(wide * wide, axis=1, keepdims=True) + epsilon)
        return wide * scale, scale

    rows_a = 2 * cz + gate_rows
    v.z_in = chunk_pieces(inputs, 16)
    v.blocks = exchange(lambda k: pick(mine_all, k))
    v.cotangent = cotangent
    v.barrier()

    block = from_group(v.take("blocks"))
    block_a = block[:rows_a]
    block_b = block[rows_a : rows_a + cz]
    block_g = block[rows_a + cz : rows_a + cz + 2 * fz]
    v.d = [block[rows_a + cz + 2 * fz :]]
    v.ring_a = [block_a] + [zshift(block_a, k) for k in range(1, M)]
    v.b, v.g = [block_b], [block_g]
    v.y_first = to_groups(block_a, block_b, block_g)
    resets = jnp.pad(reset_mask.astype(BF), (0, 16 * D - L)).reshape(16, D)
    v.own_in = jnp.concatenate([joined(v.take("z_in")), resets])
    v.far_in = far(v.own_in)
    v.barrier()

    y_next = to_groups(*v.ring_a[1:])
    ring_bg = ring_next(v.b[-1], v.g[-1])
    y_a, y_b, y_g = by_block(v.take("y_first"))
    full_a = [
        jnp.zeros((M * size, D), BF) for size in (cz, cz, gate_rows)
    ]
    for k, mine in enumerate(v.take("ring_a")):
        full_a = [fill_own(f, p, k) for f, p in zip(full_a, mixer_parts(mine))]
    v.full_a = fill_mixer_far(full_a, y_a, 0)
    v.full_b = fill_far(fill_own(jnp.zeros((C, D), BF), v.b[0], 0), y_b, 0)
    full_g = [jnp.zeros((FC, D), BF)] * 2
    full_g = [fill_own(f, p, 0) for f, p in zip(full_g, (v.g[0][:fz], v.g[0][fz:]))]
    v.full_g = [
        fill_far(f, [y[n * fz : (n + 1) * fz] for y in y_g], 0)
        for n, f in enumerate(full_g)
    ]
    v.full_d = fill_own(jnp.zeros((FC, D), BF), v.d[0], 0)
    v.take("b")
    v.take("g")
    v.ring_bg = ring_bg
    slots_in = [v.own_in, tp(v.own_in, 1)]
    if parts > 1:
        slots_in += [v.far_in, tp(v.far_in, 1)]
    v.take("far_in")
    resets = jnp.stack([e[16 + Lc :].reshape(-1)[:L].astype(F32) for e in slots_in])
    open_ = 1.0 - jnp.maximum(resets, (jnp.arange(L) % SEQ == 0).astype(F32))
    back1 = jnp.pad(open_, ((0, 0), (1, 0)))[:, :L]
    back2 = jnp.pad(open_, ((0, 0), (2, 0)))[:, :L]
    masks = jnp.stack([open_, open_ * back1, open_ * back1 * back2, 1.0 - open_], axis=1)
    masks = jnp.pad(masks, ((0, 0), (0, 0), (0, HALO)))
    masks = lax.dynamic_slice(masks, (0, 0, z * Lc), (t, 4, Lc + HALO))
    masks = masks.transpose(0, 2, 1)

    v.masks = masks
    v.own_in = v.own_in[16 : 16 + Lc]
    v.groups_in = jnp.concatenate([e[16 : 16 + Lc] for e in slots_in])
    v.ahead_in = jnp.concatenate([e[:16] for e in slots_in])
    v.scale_in = normed(v.groups_in, None)[1]
    v.y_a = y_next
    v.barrier()

    def fill_gate(k, own=None, others=None):
        for n in range(2):
            rows = slice(n * fz, (n + 1) * fz)
            if own is not None:
                v.full_g[n] = fill_own(v.full_g[n], own[rows], k)
            if others is not None:
                v.full_g[n] = fill_far(v.full_g[n], [y[rows] for y in others], k)

    b_1, g_1 = v.take("ring_bg").parts()
    v.y_1 = to_groups(b_1, g_1, v.d[0])
    ring = ring_next(b_1, g_1, v.take("d")[0])
    v.full_b = fill_own(v.full_b, b_1, 1)
    fill_gate(1, own=g_1)
    b_next, g_next, v.d = ring.parts()
    v.b, v.g = [b_next], [g_next]
    v.y_2 = to_groups(b_next, g_next)
    while len(v.b) < M - 2:
        b_next, g_next = ring_next(b_next, g_next).parts()
        v.b, v.g = v.b + [b_next], v.g + [g_next]
    for k, others in enumerate(by_block(v.take("y_a")), 1):
        v.full_a = fill_mixer_far(v.full_a, others, k)
    w_in_t, w_br_t, rest = v.take("full_a")
    rest = rest.reshape(M, gate_rows, DP, Dl).transpose(0, 2, 1, 3)
    rest = rest.reshape(M, DP, gate_rows * Dl)
    gates = rest[:, :, :gate_size].reshape(M, DP, 2, hpg, bw_here, bw)
    gates = gates.transpose(2, 0, 3, 1, 4, 5).reshape(2, nh, bw, bw)
    dense = []
    for kind in range(2):
        rows = [
            jnp.pad(gates[kind, n], ((0, 0), (n * bw, (nh - 1 - n) * bw)))
            for n in range(nh)
        ]
        dense.append(jnp.concatenate(rows))
    wa, wx = dense
    v.w_in_t, v.w_br_t, v.wa, v.wx = w_in_t, w_br_t, wa, wx
    every = rest[:, :, gate_size : gate_size + packed.shape[0]].astype(F32)
    gains = jnp.stack([pick(every[:, :, : 2 * ng], (z - b) % M) for b in range(M)])
    gain_one = gains[:, :, :ng].reshape(1, D)
    gain_two = gains[:, :, ng:].reshape(1, D)
    vectors = every[:, :, 2 * ng :].reshape(M, DP, conv + 4, nc).transpose(2, 0, 1, 3)
    vectors = pick(vectors.reshape(conv + 4, M, t, cz), q, 2).reshape(conv + 4, C)
    conv_w = vectors[:conv]
    decay = vectors[conv + 3]
    log_slope = -8.0 * jax.nn.softplus(decay)
    vec = jnp.stack(
        [vectors[conv], vectors[conv + 1], vectors[conv + 2], log_slope]
        + [jnp.zeros_like(decay)] * 4
    )

    v.vec, v.conv_w, v.gain_one, v.gain_two = vec, conv_w, gain_one, gain_two
    v.n1 = (v.take("groups_in").astype(F32) * v.take("scale_in") * v.gain_one).astype(BF)
    ahead = (normed(v.take("ahead_in"), None)[0] * v.gain_one).astype(BF)

    def mixed_sum(*pairs):
        return products(
            NN, [list(pairs)], [], [BF], lambda total: (total,), "product", halves=True
        )

    def chain(ends, sign):
        total = jnp.zeros_like(ends[..., 4:5, :])
        for k in reversed(range(1, M)):
            got = zline(ends, sign * k)
            total = got[..., 4:5, :] + got[..., 0:1, :] * total
        return total

    shape = (t, Lc, C)
    v.rnn = dot_nt(v.n1, v.w_in_t).reshape(shape)
    v.gin = dot_nt(v.n1, v.w_br_t).reshape(shape)
    v.halos = dot_nt(ahead, v.w_in_t).reshape(t, 16, C)[:, 16 - HALO :]
    v.fwd = seq_call(
        forward_kernel,
        [v.rnn, v.halos, v.masks],
        [v.conv_w, v.vec, v.wa, v.wx],
        [(shape, F32, True)] * 5 + [((t, 8, C), F32, True)],
        [pltpu.VMEM((Lc + HALO, C), F32)],
        "recurrence",
        40,
    )
    v.barrier()

    y_next = to_groups(*v.b[1:])
    y_b, y_g, y_d = by_block(v.take("y_1"))
    v.full_b = fill_far(v.full_b, y_b, 1)
    fill_gate(1, others=y_g)
    v.full_d = fill_far(v.full_d, y_d, 0)
    y_b, y_g = by_block(v.take("y_2"))
    v.full_b = fill_far(v.full_b, y_b, 2)
    fill_gate(2, others=y_g)
    for k, mine in enumerate(v.take("b"), 2):
        v.full_b = fill_own(v.full_b, mine, k)
    for k, mine in enumerate(v.g, 2):
        fill_gate(k, own=mine)
    v.full_d = fill_own(v.full_d, v.d, 1)
    v.cin = chain(v.fwd[5], 1)
    v.state = v.fwd[3] + v.fwd[4] * v.cin
    v.mixer = (gelu_parts(v.gin)[0] * v.state).astype(BF).reshape(t * Lc, C)
    v.fwd = v.fwd[:3]
    v.y_b = y_next
    v.barrier()

    for k, others in enumerate(by_block(v.take("y_b")), 3):
        v.full_b = fill_far(v.full_b, others, k)
    v.w_out = v.take("full_b")
    v.y_g = to_groups(*v.take("g")[1:], v.d)
    v.d = [v.d]
    while len(v.d) < M - 2:
        v.d = v.d + ring_next(v.d[-1]).parts()
    rec_sum = None
    for p in reversed(range(parts)):
        part = send_sum(mixed_sum(((v.mixer, p, parts), v.w_out)), p)
        rec_sum = part if rec_sum is None else rec_sum + part
    v.resid_mid = v.own_in.astype(F32) + rec_sum
    v.unit_two, v.scale_two = normed(v.resid_mid, v.gain_two)
    v.n2_own = (v.unit_two * v.gain_two).astype(BF)
    v.barrier()

    got = by_block(v.take("y_g"))
    for k, others in enumerate(got[:-1], 3):
        fill_gate(k, others=others)
    v.full_d = fill_far(v.full_d, got[-1], 1)
    v.w_gate_t, v.w_up_t = v.take("full_g")
    for k, mine in enumerate(v.d[1:], 2):
        v.full_d = fill_own(v.full_d, mine, k)
    v.z_cot = chunk_pieces(v.take("cotangent"), rider=folded(v.d[-1]))
    v.n2_far = far(v.n2_own)
    v.n2 = [jnp.concatenate([v.n2_own, tp(v.n2_own, 1)])]
    v.take("n2_own")

    def mlp_forward(p):
        return products(
            NT,
            [[(v.n2[p], v.w_gate_t)], [(v.n2[p], v.w_up_t)]],
            [],
            [F32, F32, BF],
            lambda gate, up: (gate, up, gelu_parts(gate)[0] * up),
            "mlp",
        )

    v.mlp = [mlp_forward(0)]
    v.barrier()

    v.d = v.d[1:] + [unfolded(v.z_cot[1][Lc:])]
    v.z_cot[1] = v.z_cot[1][:Lc]
    v.y_d = to_groups(*v.d)
    cot_own = joined(v.take("z_cot"))
    v.cot = [jnp.concatenate([cot_own, tp(cot_own, 1)])]
    v.far_cot = far(cot_own)
    if parts > 1:
        v.n2.append(jnp.concatenate([v.n2_far, tp(v.n2_far, 1)]))
        v.mlp.append(mlp_forward(1))
    v.take("n2_far")
    v.barrier()

    def summed(lefts, rights):
        out = [
            products(
                TN,
                [list(zip(lefts, rights))],
                [],
                [BF],
                lambda total: (total,),
                "gradient",
                base=((o + r) % O) * half,
                width=half,
            )[0]
            for r in reversed(range(O))
        ]
        return out[::-1]

    v.full_d = fill_own(v.full_d, v.take("d")[-1], M - 1)
    for k, others in enumerate(by_block(v.take("y_d")), 2):
        v.full_d = fill_far(v.full_d, others, k)
    v.w_dn = v.take("full_d")
    if parts > 1:
        v.cot.append(jnp.concatenate([v.far_cot, tp(v.far_cot, 1)]))
    v.take("far_cot")

    def mlp_back(p):
        def finish(d_hidden, gate, up):
            gelu, slope = gelu_parts(gate)
            return d_hidden * up * slope, d_hidden * gelu

        return products(
            NT, [[(v.cot[p], v.w_dn)]], list(v.mlp[p][:2]), [BF, BF], finish, "mlp_back"
        )

    def mlp_back_in(p):
        gate, up = v.d_mlp[p]
        return mixed_sum((gate, v.w_gate_t), (up, v.w_up_t))

    v.grad_down = summed([m[2] for m in v.mlp], v.cot)
    v.d_mlp = [None] * parts
    v.d_mlp[last] = mlp_back(last)
    v.barrier()

    v.y_down = grad_y(v.take("grad_down"))
    v.dn2 = [None] * parts
    v.dn2[last] = mlp_back_in(last)
    v.dn2_sum = send_sum(v.dn2[last], last) if last else None
    for p in range(last):
        v.d_mlp[p] = mlp_back(p)
        v.dn2[p] = mlp_back_in(p)
    v.grad_gate = summed([d[0] for d in v.d_mlp], v.n2)
    v.hidden = [m[2] for m in v.take("mlp")]
    v.cot_own = v.take("cot")[0][:Lc]
    v.barrier()

    (v.y_down,) = y_parts(v.y_down)
    v.ring = ring_step((v.y_down, 1, None))
    v.y_gate = grad_y(v.take("grad_gate"))
    dn2_sum = v.take("dn2_sum")
    for p in reversed(range(last if last else 1)):
        part = send_sum(v.dn2[p], p)
        dn2_sum = part if dn2_sum is None else dn2_sum + part
    v.take("dn2")

    def norm_back(grad, unit, scale, gain):
        weighted = grad * gain
        dots = jnp.mean(weighted * unit, axis=1, keepdims=True)
        return scale * (weighted - unit * dots), jnp.sum(grad * unit, axis=0)

    back_two, v.gain_two_grad = norm_back(dn2_sum, v.unit_two, v.scale_two, v.gain_two)
    v.d_mid = v.take("cot_own").astype(F32) + back_two
    v.d_own = v.d_mid.astype(BF)
    v.far_branch = far(v.d_own)
    v.near_branch = tp(v.d_own, 1)
    v.grad_up = summed([d[1] for d in v.d_mlp], v.n2)
    v.take("n2")
    v.take("d_mlp")
    v.out = [mixed_sum((h, v.w_dn)) for h in v.take("hidden")]
    v.barrier()

    (v.y_gate,) = y_parts(v.y_gate)
    (r_down,) = v.ring.parts()
    v.ring = ring_step((v.y_down, 2, r_down), (v.y_gate, 1, None))
    v.y_up = grad_y(v.take("grad_up"))
    slots_of = [v.take("d_own"), v.take("near_branch")]
    if parts > 1:
        slots_of += [v.far_branch, tp(v.far_branch, 1)]
    v.take("far_branch")
    v.d_branch = jnp.concatenate(slots_of)
    out = v.take("out")
    got = joint(lambda b: tp(b, 1), [part[1] for part in out]).parts()
    out_sum = out[0][0].astype(F32) + got[0].astype(F32)
    if parts > 1:
        there = out[1][0].astype(F32) + got[1].astype(F32)
        out_sum = out_sum + tp(there.astype(BF), 2).astype(F32)
    v.output = (v.take("resid_mid") + out_sum).astype(BF)

    v.adjoint = seq_call(
        adjoint_kernel,
        [
            dot_nt(v.d_branch, v.w_out).reshape(shape),
            v.take("gin"),
            v.state,
            v.fwd[1],
            v.masks,
        ],
        [v.vec],
        [(shape, F32, True)] * 2 + [(shape, BF, True), ((t, 8, C), F32, True)],
        [],
        "adjoint",
        24,
    )
    v.barrier()

    r_down, r_gate = v.ring.parts()
    v.ring = ring_step((v.y_down, 3, r_down), (v.y_gate, 2, r_gate))
    (v.y_up,) = y_parts(v.y_up)
    v.edges = jnp.concatenate(
        [
            jnp.broadcast_to(v.take("cin"), (t, 4, C)),
            jnp.broadcast_to(chain(v.adjoint[3], -1), (t, 4, C)),
        ],
        1,
    )
    v.grad_output = summed([v.take("mixer")], [v.take("d_branch")])
    v.d_gin = v.adjoint[2].reshape(t * Lc, C)
    v.grad_branch = summed([v.d_gin], [v.n1])
    v.barrier()

    v.r_down, r_gate = v.ring.parts()
    v.ring = ring_step((v.y_gate, 3, r_gate), (v.y_up, 1, None))
    v.y_mixer = grad_y(v.take("grad_output"), v.take("grad_branch"))
    pieces = back_pieces(v.take("output"))
    v.z_out = [zshift(piece, k) if k else piece for k, piece in enumerate(pieces)]
    mixed, gate_a, gate_x = v.fwd
    lam, prod, _, _ = v.adjoint
    v.d_rnn, v.heads, v.tails, v.grad_wa, v.grad_wx, v.grad_vec = seq_call(
        backward_kernel,
        [
            lam,
            prod,
            v.state,
            gate_a,
            gate_x,
            mixed,
            v.rnn,
            v.halos,
            v.masks,
            v.edges,
        ],
        [v.conv_w, v.vec, v.wa, v.wx],
        [
            (shape, BF, True),
            ((t, HALO, C), F32, True),
            ((t, HALO, C), F32, True),
            ((C, C), F32, False),
            ((C, C), F32, False),
            ((8, 8, C), F32, False),
        ],
        [pltpu.VMEM((Lc + HALO, C), F32)] * 3,
        "recurrence_back",
        64,
    )
    for name in ("adjoint", "fwd", "state", "rnn", "halos", "edges"):
        v.take(name)
    v.barrier()

    following = zline(v.take("heads"), -1)
    fix = [jnp.zeros((t, 1, C), F32)] * HALO
    for k in range(1, 4):
        for n in range(k):
            row = HALO - k + n
            fix[row] = fix[row] + v.conv_w[k] * (
                v.masks[:, Lc + n : Lc + n + 1, k - 1 : k] * following[:, n : n + 1]
            )
    tail = (v.take("tails") + jnp.concatenate(fix, axis=1)).astype(BF)
    v.d_rnn = put(v.d_rnn, tail, 0, Lc - HALO, 0).reshape(t * Lc, C)
    z_down = ring_end(v.take("y_down"), v.take("r_down"))
    r_gate, r_up = v.take("ring").parts()
    z_gate = ring_end(v.take("y_gate"), r_gate)
    y_output, y_branch = y_parts(v.take("y_mixer"))
    rings = ring_sends((v.y_up, 2, r_up))

    def direct(rings, *grads):
        got = []
        for k, send in enumerate(direct_sends(*grads)):
            send = send + rings if k == M - 1 else send
            got.append(joint(lambda b: zshift(b, M - k) if k else b, send))
        return got

    v.z_mixer = direct(rings, y_output, y_branch)
    v.output = back_joined(v.take("z_out"))
    gates_grad = jnp.stack(
        [
            jnp.stack(
                [g[n * bw : (n + 1) * bw, n * bw : (n + 1) * bw] for n in range(nh)]
            )
            for g in (v.take("grad_wa"), v.take("grad_wx"))
        ]
    )
    gates_grad = gates_grad.reshape(2, M, hpg, DP, bw_here, bw)
    gates_grad = gates_grad.transpose(1, 3, 0, 2, 4, 5).reshape(M, DP, gate_size)
    small = jnp.sum(v.take("grad_vec"), axis=1).reshape(2 * conv, M, O, nc)
    small = small.transpose(1, 2, 0, 3).reshape(M, O, 2 * conv * nc)
    small = put(jnp.zeros((M, DP, 2 * conv * nc), F32), small, 0, q * O, 0)
    gain_two_grad = v.take("gain_two_grad").reshape(M, DP, ng)
    gain_two_grad = jnp.stack([pick(gain_two_grad, (z - k) % M) for k in range(M)])
    gates_grad = jnp.concatenate([gates_grad, small, gain_two_grad], axis=2)
    gates_grad = jnp.pad(
        gates_grad, ((0, 0), (0, 0), (0, gate_rows * Dl - gates_grad.shape[2]))
    )
    gates_grad = gates_grad.reshape(M, DP, gate_rows, Dl).transpose(0, 2, 1, 3)
    gates_grad = gates_grad.reshape(M * gate_rows, D).astype(BF)
    gates_grad = [cut(gates_grad, (o + r) % O, half, 1) for r in range(O)]
    v.y_in = grad_y(summed([v.d_rnn], [v.n1]), gates_grad)
    v.take("n1")
    v.dn1 = [
        mixed_sum(((v.d_rnn, p, parts), v.w_in_t), ((v.d_gin, p, parts), v.w_br_t))
        for p in range(parts)
    ]
    v.z_down, v.z_gate = z_down, z_gate
    for name in ("d_rnn", "d_gin", "w_in_t", "w_br_t", "wa", "wx", "masks", "vec"):
        v.take(name)
    v.barrier()

    r_up = v.z_mixer[M - 1].parts()[2]
    v.z_in = direct(ring_sends((v.y_up, 3, r_up)), *y_parts(v.take("y_in")))
    dn1_sum = None
    for p in reversed(range(parts)):
        part = send_sum(v.dn1[p], p)
        dn1_sum = part if dn1_sum is None else dn1_sum + part
    v.dn1 = dn1_sum
    v.barrier()

    def added(pieces):
        return [
            sum(p.astype(F32) for p in same).astype(BF)
            for same in zip(*(piece.parts()[:2] for piece in pieces))
        ]

    r_up = v.z_in[M - 1].parts()[2]

    z_output, z_branch = added(v.take("z_mixer"))
    z_in, z_gates = added(v.take("z_in"))
    z_up = ring_end(v.take("y_up"), r_up)
    totals = exchange_grads(
        v.take("z_down"), v.take("z_gate"), z_up, z_output, z_branch, z_in, z_gates
    )
    unit_one, scale_one = normed(v.own_in, v.gain_one)
    back_one, gain_one_grad = norm_back(v.take("dn1"), unit_one, scale_one, v.gain_one)
    pieces = back_pieces((v.d_mid + back_one).astype(BF))
    sums = jnp.broadcast_to(gain_one_grad.astype(BF), (16, D))
    joints = []
    for k, piece in enumerate(pieces):
        joint = jnp.concatenate([piece, cut(sums, (z + k) % M, FH, 1)])
        joints.append(zshift(joint, k) if k else joint)
    *whole, last_rows = by_grad(totals)
    v.joints = joints
    v.grads = [grad_end(total) for total in whole]
    v.last_rows = last_rows
    v.barrier()

    grad_down, grad_gate, grad_up, grad_output, grad_branch, grad_in = v.grads
    input_grad = back_joined([joint[:Lc] for joint in v.joints]).astype(F32)
    gain_one_grad = sum(joint[Lc].astype(F32) for joint in v.joints)
    step = 1
    while step < DP:
        gain_one_grad = gain_one_grad + tp(gain_one_grad, step)
        step *= 2
    gain_one_grad = cut(gain_one_grad, i_dp, ng, 0)
    output = v.output

    rest_in = jnp.stack([piece.reshape(-1) for piece in v.last_rows])
    small = jnp.sum(rest_in[:, gate_size:].astype(F32), axis=0)
    rest_in = jnp.stack([pick(rest_in, q ^ k) for k in range(t)])
    mine = small[: 2 * conv * nc].reshape(2 * conv, nc)
    gain_two_grad = small[2 * conv * nc : 2 * conv * nc + ng]
    decay_grad = mine[conv + 3] * (-8.0 * jax.nn.sigmoid(decay_param.astype(F32)))

    gates_back = rest_in[:, :gate_size].reshape(t, 2, hpg, bw_here, bw)
    gates_back = gates_back.transpose(1, 0, 2, 3, 4)
    gates_back = gates_back.reshape(2, heads_here, bw_here, bw).astype(F32)

    def flipped(value):
        return lax.optimization_barrier(value).T.astype(F32)

    return (
        output,
        input_grad,
        gain_one_grad,
        flipped(grad_in),
        flipped(grad_branch),
        grad_output.astype(F32),
        mine[:conv],
        mine[conv],
        gates_back[0],
        mine[conv + 1],
        gates_back[1],
        mine[conv + 2],
        decay_grad,
        gain_two_grad,
        flipped(grad_gate),
        flipped(grad_up),
        grad_down.astype(F32),
    )


def solution(mesh):
    both = P(("mp", "dp"))
    wide = P("dp", "mp")
    tall = P("mp", "dp")
    taps = P(None, ("mp", "dp"))
    gate = P("mp", "dp", None)
    params = (both, wide, wide, tall, taps, both, gate, both, gate, both, both, both, wide, wide, tall)
    return jax.shard_map(
        functools.partial(body, mesh.shape["dp"], mesh.shape["mp"]),
        mesh=mesh,
        in_specs=(wide, wide, P("dp")) + params,
        out_specs=(wide, wide) + params,
        check_vma=False,
    )
```

```python
import functools

import jax
import jax.numpy as jnp
from jax import lax
from jax.experimental import pallas as pl
from jax.experimental.pallas import tpu as pltpu
from jax.sharding import PartitionSpec as P

SEQ = 2048
epsilon = 1e-06
BF = jnp.bfloat16
F32 = jnp.float32
HALO = 8


def dot_nt(left, right):
    return lax.dot_general(
        left, right, (((1,), (1,)), ((), ())), preferred_element_type=F32
    )


def dot_nn(left, right):
    return jnp.dot(left, right, preferred_element_type=F32)


def dot_tn(left, right):
    return lax.dot_general(
        left, right, (((0,), (0,)), ((), ())), preferred_element_type=F32
    )


def gelu_parts(value):
    inner = 0.7978845608028654 * (value + 0.044715 * value * value * value)
    tanh = jnp.tanh(inner)
    slope = 0.7978845608028654 * (1.0 + 3.0 * 0.044715 * value * value)
    gelu = 0.5 * value * (1.0 + tanh)
    grad = 0.5 * (1.0 + tanh) + 0.5 * value * (1.0 - tanh * tanh) * slope
    return gelu, grad


def sigmoid(value):
    return 1.0 / (1.0 + jnp.exp(-value))


def one_minus_exp(log_value):
    y = -2.0 * log_value
    series = y * (
        1.0
        - y
        * (1 / 2)
        * (
            1.0
            - y
            * (1 / 3)
            * (1.0 - y * (1 / 4) * (1.0 - y * (1 / 5) * (1.0 - y * (1 / 6))))
        )
    )
    return jnp.where(y < 0.25, series, 1.0 - jnp.exp(-y))


def conv_terms(ext, masks, rows):
    terms = [ext[HALO : HALO + rows]]
    for k in range(1, 4):
        moved = pltpu.roll(ext, k, axis=0)[HALO : HALO + rows]
        terms.append(moved * masks[:, k - 1 : k])
    return terms


def forward_kernel(
    rnn_ref,
    halo_ref,
    mask_ref,
    conv_ref,
    vec_ref,
    wa_ref,
    wx_ref,
    mixed_ref,
    ga_ref,
    gx_ref,
    h_ref,
    p_ref,
    end_ref,
    ext_ref,
):
    length, width = rnn_ref.shape[1:]
    block_rows = min(256, length)
    ext_ref[0:HALO, :] = halo_ref[0]
    ext_ref[HALO:, :] = rnn_ref[0]
    row8 = lax.broadcasted_iota(jnp.int32, (block_rows, 1), 0) % 8

    def block(i, carry):
        h_in, p_in = carry
        r0 = pl.multiple_of(i * block_rows, block_rows)
        masks = mask_ref[0, pl.ds(r0, block_rows), :]
        terms = conv_terms(ext_ref[pl.ds(r0, block_rows + HALO), :], masks, block_rows)
        mixed = vec_ref[0:1, :] + conv_ref[0:1, :] * terms[0]
        for k in range(1, 4):
            mixed = mixed + conv_ref[k : k + 1, :] * terms[k]
        high = mixed.astype(BF)
        low = (mixed - high.astype(F32)).astype(BF)
        gate_a = sigmoid(
            dot_nn(high, wa_ref[...]) + dot_nn(low, wa_ref[...]) + vec_ref[1:2, :]
        )
        gate_x = sigmoid(
            dot_nn(high, wx_ref[...]) + dot_nn(low, wx_ref[...]) + vec_ref[2:3, :]
        )
        begins = masks[:, 3:4]
        log_a = gate_a * vec_ref[3:4, :]
        a = jnp.exp(log_a) * (1.0 - begins)
        scale = jnp.sqrt(one_minus_exp(log_a)) * (1.0 - begins) + begins
        b = mixed * gate_x * scale
        mixed_ref[0, pl.ds(r0, block_rows), :] = mixed
        ga_ref[0, pl.ds(r0, block_rows), :] = gate_a
        gx_ref[0, pl.ds(r0, block_rows), :] = gate_x
        for d in (1, 2, 4):
            valid = row8 >= d
            b = jnp.where(valid, a * pltpu.roll(b, d, axis=0) + b, b)
            a = jnp.where(valid, a * pltpu.roll(a, d, axis=0), a)
        for g in range(block_rows // 8):
            rows = slice(8 * g, 8 * g + 8)
            h = b[rows] + a[rows] * h_in
            p = a[rows] * p_in
            h_ref[0, pl.ds(r0 + 8 * g, 8), :] = h
            p_ref[0, pl.ds(r0 + 8 * g, 8), :] = p
            h_in = h[7:8]
            p_in = p[7:8]
        return h_in, p_in

    h_end, p_end = lax.fori_loop(
        0,
        length // block_rows,
        block,
        (jnp.zeros((1, width), F32), jnp.ones((1, width), F32)),
    )
    end_ref[0, 0:4, :] = jnp.broadcast_to(p_end, (4, width))
    end_ref[0, 4:8, :] = jnp.broadcast_to(h_end, (4, width))


def adjoint_kernel(
    dmix_ref,
    gate_ref,
    state_ref,
    ga_ref,
    mask_ref,
    vec_ref,
    lam_ref,
    q_ref,
    dgi_ref,
    end_ref,
):
    length, width = dmix_ref.shape[1:]
    block_rows = min(64, length)
    row = lax.broadcasted_iota(jnp.int32, (block_rows, 1), 0)
    row8 = row % 8
    blocks = length // block_rows

    def block(i, carry):
        lam_in, q_in, a_next = carry
        r0 = pl.multiple_of((blocks - 1 - i) * block_rows, block_rows)
        here = pl.ds(r0, block_rows)
        begins = mask_ref[0, here, :][:, 3:4]
        d_mixer = dmix_ref[0, here, :]
        gelu, slope = gelu_parts(gate_ref[0, here, :])
        dgi_ref[0, here, :] = (d_mixer * state_ref[0, here, :] * slope).astype(BF)
        b = d_mixer * gelu
        a = jnp.exp(ga_ref[0, here, :] * vec_ref[3:4, :]) * (1.0 - begins)
        c = jnp.where(row == block_rows - 1, a_next, pltpu.roll(a, block_rows - 1, axis=0))
        for d in (1, 2, 4):
            valid = row8 < 8 - d
            b = jnp.where(valid, c * pltpu.roll(b, block_rows - d, axis=0) + b, b)
            c = jnp.where(valid, c * pltpu.roll(c, block_rows - d, axis=0), c)
        for g in reversed(range(block_rows // 8)):
            rows = slice(8 * g, 8 * g + 8)
            lam = b[rows] + c[rows] * lam_in
            q = c[rows] * q_in
            lam_ref[0, pl.ds(r0 + 8 * g, 8), :] = lam
            q_ref[0, pl.ds(r0 + 8 * g, 8), :] = q
            lam_in = lam[0:1]
            q_in = q[0:1]
        return lam_in, q_in, a[0:1]

    one = jnp.ones((1, width), F32)
    lam0, q0, a0 = lax.fori_loop(
        0, blocks, block, (jnp.zeros((1, width), F32), one, one)
    )
    end_ref[0, 0:4, :] = jnp.broadcast_to(a0 * q0, (4, width))
    end_ref[0, 4:8, :] = jnp.broadcast_to(a0 * lam0, (4, width))


def fold8(value):
    total = value[0:8]
    for g in range(1, value.shape[0] // 8):
        total = total + value[8 * g : 8 * g + 8]
    return total


def backward_kernel(
    lam_ref,
    q_ref,
    state_ref,
    ga_ref,
    gx_ref,
    mixed_ref,
    rnn_ref,
    halo_ref,
    mask_ref,
    edge_ref,
    conv_ref,
    vec_ref,
    wa_ref,
    wx_ref,
    drnn_ref,
    head_ref,
    tail_ref,
    wag_ref,
    wxg_ref,
    vg_ref,
    ext_ref,
    prev_ref,
    dm_ref,
):
    length, width = lam_ref.shape[1:]
    block_rows = min(256, length)
    first = pl.program_id(0) == 0

    @pl.when(first)
    def _():
        wag_ref[...] = jnp.zeros_like(wag_ref)
        wxg_ref[...] = jnp.zeros_like(wxg_ref)
        vg_ref[...] = jnp.zeros_like(vg_ref)

    ext_ref[0:HALO, :] = halo_ref[0]
    ext_ref[HALO:, :] = rnn_ref[0]
    prev_ref[0:HALO, :] = jnp.broadcast_to(edge_ref[0, 0:1, :], (HALO, width))
    prev_ref[HALO:, :] = state_ref[0]
    dm_ref[length:, :] = jnp.zeros((HALO, width), F32)

    def block(i, carry):
        r0 = pl.multiple_of(i * block_rows, block_rows)
        here = pl.ds(r0, block_rows)
        masks = mask_ref[0, here, :]
        begins = masks[:, 3:4]
        lam = lam_ref[0, here, :] + q_ref[0, here, :] * edge_ref[0, 4:5, :]
        before = pltpu.roll(prev_ref[pl.ds(r0, block_rows + HALO), :], 1, axis=0)[
            HALO : HALO + block_rows
        ]
        gate_a = ga_ref[0, here, :]
        gate_x = gx_ref[0, here, :]
        mixed = mixed_ref[0, here, :]
        log_a = gate_a * vec_ref[3:4, :]
        decay = jnp.exp(log_a)
        inv_scale = lax.rsqrt(one_minus_exp(log_a))
        scale_raw = jnp.sqrt(one_minus_exp(log_a))
        keep = 1.0 - begins
        scale = scale_raw * keep + begins
        through = lam * mixed
        d_log = lam * before * decay * keep + jnp.where(
            begins > 0.5, 0.0, through * gate_x * (-(decay * decay) * inv_scale)
        )
        log_gate = d_log * gate_a
        d_pre_a = log_gate * (1.0 - gate_a) * vec_ref[3:4, :]
        d_pre_x = through * scale * gate_x * (1.0 - gate_x)
        pa = d_pre_a.astype(BF)
        px = d_pre_x.astype(BF)
        mb = mixed.astype(BF)
        d_mixed = (
            lam * gate_x * scale + dot_nt(pa, wa_ref[...]) + dot_nt(px, wx_ref[...])
        )
        dm_ref[here, :] = d_mixed
        wag_ref[...] += dot_tn(mb, pa)
        wxg_ref[...] += dot_tn(mb, px)
        terms = conv_terms(ext_ref[pl.ds(r0, block_rows + HALO), :], masks, block_rows)
        sums = [d_mixed * term for term in terms]
        sums += [d_mixed, d_pre_a, d_pre_x, log_gate]
        for n, value in enumerate(sums):
            vg_ref[n] += fold8(value)
        return carry

    lax.fori_loop(0, length // block_rows, block, 0)

    def shift(i, carry):
        r0 = pl.multiple_of(i * block_rows, block_rows)
        ext = dm_ref[pl.ds(r0, block_rows + HALO), :]
        masks = mask_ref[0, pl.ds(r0, block_rows + HALO), :]
        total = conv_ref[0:1, :] * ext[0:block_rows]
        for k in range(1, 4):
            moved = pltpu.roll(ext * masks[:, k - 1 : k], block_rows + HALO - k, axis=0)
            total = total + conv_ref[k : k + 1, :] * moved[0:block_rows]
        drnn_ref[0, pl.ds(r0, block_rows), :] = total.astype(BF)

        @pl.when(i == length // block_rows - 1)
        def _():
            tail_ref[0] = total[block_rows - HALO :]

        return carry

    lax.fori_loop(0, length // block_rows, shift, 0)
    head_ref[0] = dm_ref[0:HALO, :]


def block_specs(shapes):
    specs = []
    for shape, moving in shapes:
        if moving:
            specs.append(
                pl.BlockSpec((1,) + shape[1:], lambda i, n=len(shape): (i,) + (0,) * (n - 1))
            )
        else:
            specs.append(pl.BlockSpec(shape, lambda i, n=len(shape): (0,) * n))
    return specs


def cost(time):
    return pl.CostEstimate(flops=int(time * 1.0e8), bytes_accessed=0, transcendentals=0)


NT = (((1,), (1,)), ((), ()))
NN = (((1,), (0,)), ((), ()))
TN = (((0,), (0,)), ((), ()))


def seq_call(kernel, moving, fixed, outs, scratch, name, time):
    count = moving[0].shape[0]
    return pl.pallas_call(
        kernel,
        grid=(count,),
        in_specs=block_specs(
            [(a.shape, True) for a in moving] + [(a.shape, False) for a in fixed]
        ),
        out_specs=block_specs([(shape, move) for shape, _, move in outs]),
        out_shape=[jax.ShapeDtypeStruct(shape, dtype) for shape, dtype, _ in outs],
        scratch_shapes=scratch,
        compiler_params=pltpu.CompilerParams(
            dimension_semantics=("arbitrary",), vmem_limit_bytes=60 * 1024 * 1024
        ),
        cost_estimate=cost(time),
        name=name,
    )(*moving, *fixed)


def products(dims, sums, extras, outs, finish, name, base=None, width=None, halves=False):
    full = sums[0][0][1].shape[0 if dims == NT else 1]
    width = width or full
    columns = min(256, width)
    lefts, rights, where = [], [], []
    for pairs in sums:
        places = []
        for left, right in pairs:
            left = left if isinstance(left, tuple) else (left, 0, 1)
            known = [n for n, other in enumerate(lefts) if other[0] is left[0]]
            places.append(known[0] if known else len(lefts))
            if not known:
                lefts.append(left)
            rights.append(right)
        where.append(places)
    array, _, count = lefts[0]
    rows = array.shape[1] if dims == TN else array.shape[0] // count
    cuts = 2 if halves else 1
    near = len(lefts) + len(rights)

    def kernel(_, *refs):
        at, totals = len(lefts), []
        for places in where:
            total = None
            for place in places:
                term = lax.dot_general(
                    refs[place][...], refs[at][...], dims, preferred_element_type=F32
                )
                total = term if total is None else total + term
                at += 1
            totals.append(total)
        values = finish(*totals, *(ref[...] for ref in refs[near : near + len(extras)]))
        size = rows // cuts
        at = near + len(extras)
        for value in values:
            for n in range(cuts):
                refs[at][...] = value[n * size : (n + 1) * size].astype(refs[at].dtype)
                at += 1

    def whole(left):
        array, part, count = left
        shape = (array.shape[0] // count, array.shape[1])
        return pl.BlockSpec(shape, lambda j, b: (part, 0))

    def moving(array):
        if dims == NT:
            return pl.BlockSpec((columns, array.shape[1]), lambda j, b: (b[0] + j, 0))
        return pl.BlockSpec((array.shape[0], columns), lambda j, b: (0, b[0] + j))

    base = jnp.zeros((1,), jnp.int32) if base is None else (base // columns).reshape(1)
    tile = pl.BlockSpec((rows, columns), lambda j, b: (0, j))
    part = pl.BlockSpec((rows // cuts, columns), lambda j, b: (0, j))
    return pl.pallas_call(
        kernel,
        grid_spec=pltpu.PrefetchScalarGridSpec(
            num_scalar_prefetch=1,
            grid=(width // columns,),
            in_specs=[whole(a) for a in lefts]
            + [moving(a) for a in rights]
            + [tile] * len(extras),
            out_specs=[part] * (len(outs) * cuts),
        ),
        out_shape=[
            jax.ShapeDtypeStruct((rows // cuts, width), dtype)
            for dtype in outs
            for _ in range(cuts)
        ],
        compiler_params=pltpu.CompilerParams(
            dimension_semantics=("arbitrary",), vmem_limit_bytes=60 * 1024 * 1024
        ),
        cost_estimate=cost(sum(a.size for a in rights) // (width and full) * width * rows / 3.4e8),
        name=name,
    )(base, *(left[0] for left in lefts), *rights, *extras)


@jax.tree_util.register_pytree_node_class
class Joint:
    def __init__(self, rows, sizes):
        self.rows, self.sizes = rows, sizes

    def tree_flatten(self):
        return (self.rows,), self.sizes

    @classmethod
    def tree_unflatten(cls, sizes, children):
        return cls(children[0], sizes)

    def parts(self):
        at, out = 0, []
        for size in self.sizes:
            out.append(self.rows[at : at + size])
            at += size
        return out


def body(
    DP,
    M,
    inputs,
    cotangent,
    reset_mask,
    norm1_gain,
    w_input,
    w_branch,
    w_output,
    conv_weight,
    conv_bias,
    gate_a_weight,
    gate_a_bias,
    gate_x_weight,
    gate_x_bias,
    decay_param,
    norm2_gain,
    w_gate,
    w_up,
    w_down,
):
    heads_here, bw_here, bw = gate_a_weight.shape
    t = 4 if heads_here % 4 == 0 and DP % 4 == 0 else 2
    O = DP // t
    hpg = heads_here // t
    nh = M * hpg
    L, FH = inputs.shape
    D = FH * M
    Dl = w_input.shape[0]
    Lc = L // M
    half = t * Dl
    cz = w_input.shape[1] // t
    fz = w_gate.shape[1] // t
    C = M * cz
    FC = M * fz
    conv = conv_weight.shape[0]
    parts = t // 2
    last = parts - 1

    i_dp = lax.axis_index("dp")
    z = lax.axis_index("mp")
    q = i_dp % t
    o = i_dp // t

    def tp(value, j):
        return lax.ppermute(value, "dp", [(i, i ^ j) for i in range(DP)])

    def oshift(value, r):
        return lax.ppermute(
            value, "dp", [(i, ((i // t + r) % O) * t + i % t) for i in range(DP)]
        )

    def zshift(value, k):
        return lax.ppermute(value, "mp", [(i, (i + k) % M) for i in range(M)])

    def zline(value, k):
        got = lax.ppermute(
            value, "mp", [(i, i + k) for i in range(M) if 0 <= i + k < M]
        )
        return jnp.roll(got, k * cz, axis=-1)

    class Live(dict):
        __getattr__ = dict.__getitem__
        __setattr__ = dict.__setitem__

        def barrier(self):
            held = lax.optimization_barrier(dict(self))
            self.clear()
            self.update(held)

        def take(self, name):
            return self.pop(name)

    v = Live()

    def cut(array, index, size, axis):
        return lax.dynamic_slice_in_dim(array, index * size, size, axis)

    def put(array, piece, *starts):
        return lax.dynamic_update_slice(array, piece, starts)

    def pick(array, index, axis=0):
        return lax.dynamic_index_in_dim(array, index, axis, keepdims=False)

    def chunk_pieces(value, ahead=0, rider=None):
        if ahead:
            value = jnp.concatenate([jnp.zeros((ahead, FH), value.dtype), value])
        pieces = [
            lax.dynamic_slice_in_dim(value, (z + k) % M * Lc, Lc + ahead, 0)
            for k in range(M)
        ]
        if rider is not None:
            pieces[1] = jnp.concatenate([pieces[1], rider])
        return [zshift(piece, k) if k else piece for k, piece in enumerate(pieces)]

    def joined(pieces):
        own = jnp.zeros((pieces[0].shape[0], D), pieces[0].dtype)
        for k, piece in enumerate(pieces):
            own = put(own, piece, 0, ((z - k) % M) * FH)
        return own

    def far(value):
        return tp(value, 2) if parts > 1 else None

    def back_pieces(value):
        return [cut(value, (z + k) % M, FH, 1) for k in range(M)]

    def back_joined(pieces):
        out = jnp.zeros((L, FH), pieces[0].dtype)
        for k, piece in enumerate(pieces):
            out = put(out, piece, ((z - k) % M) * Lc, 0)
        return out

    def send_sum(part, p):
        mine = part[0].astype(F32) + tp(part[1], 1).astype(F32)
        if p:
            mine = tp(mine.astype(BF), 2).astype(F32)
        return mine

    def stacked(blocks):
        return jnp.concatenate(blocks) if len(blocks) > 1 else blocks[0]

    def joint(transfer, blocks):
        return Joint(transfer(stacked(blocks)), tuple(b.shape[0] for b in blocks))

    def exchange(mine):
        if parts == 1:
            return [mine(q), tp(mine(q ^ 1), 1)]
        got = tp(jnp.stack([mine(q ^ 1), mine(q ^ 3)]), 1)
        after = tp(jnp.stack([mine(q ^ 2), got[1]]), 2)
        return [mine(q), got[0], after[0], after[1]]

    def from_group(pieces):
        block = jnp.zeros((pieces[0].shape[0], half), BF)
        for j, piece in enumerate(pieces):
            block = put(block, piece, 0, (q ^ j) * Dl)
        return block

    def to_groups(*blocks):
        return [joint(lambda b: oshift(b, r), blocks) for r in range(1, O)]

    def by_block(got):
        return [list(same) for same in zip(*(g.parts() for g in got))]

    def ring_next(*blocks):
        return joint(lambda b: zshift(b, 1), blocks)

    def fill_own(full, block, s):
        return put(full, block, s * block.shape[0], o * half)

    def fill_far(full, others, s):
        for r, piece in enumerate(others, 1):
            full = put(full, piece, s * piece.shape[0], ((o - r) % O) * half)
        return full

    def mixer_parts(block):
        return block[:cz], block[cz : 2 * cz], block[2 * cz :]

    def fill_mixer_far(full, others, s):
        split = [mixer_parts(piece) for piece in others]
        return [fill_far(f, [g[n] for g in split], s) for n, f in enumerate(full)]

    def folded(block):
        return jnp.concatenate(
            [block[:, n * FH : (n + 1) * FH] for n in range(half // FH)]
        )

    def unfolded(rows):
        size = rows.shape[0] // (half // FH)
        return jnp.concatenate(
            [rows[n * size : (n + 1) * size] for n in range(half // FH)], axis=1
        )

    def grad_y(*grads):
        return [g[0] for g in grads], to_groups_of(grads)

    def to_groups_of(grads):
        return [joint(lambda b: oshift(b, r), [g[r] for g in grads]) for r in range(1, O)]

    def y_parts(held):
        own, got = held
        return [list(same) for same in zip(own, *(g.parts() for g in got))]

    def slot(pieces, k):
        size = pieces[0].shape[0] // M
        return sum(piece[k * size : (k + 1) * size].astype(F32) for piece in pieces)

    def ring_sends(*rings):
        sends = []
        for pieces, k, moving in rings:
            total = slot(pieces, k)
            if moving is not None:
                total = total + moving.astype(F32)
            sends.append(total.astype(BF))
        return sends

    def ring_step(*rings):
        return ring_next(*ring_sends(*rings))

    def ring_end(pieces, moving):
        for k in range(4, M):
            (moving,) = ring_step((pieces, k, moving)).parts()
        return (moving.astype(F32) + slot(pieces, 0)).astype(BF)

    def direct_sends(*grads):
        return [[slot(pieces, k).astype(BF) for pieces in grads] for k in range(M)]

    def grad_end(pieces):
        size = pieces[0].shape[0]
        out = jnp.zeros((t * size, Dl), BF)
        for j, piece in enumerate(pieces):
            out = put(out, piece, (q ^ j) * size, 0)
        return out

    def exchange_grads(*totals):
        sizes = tuple(total.shape[0] for total in totals)
        rows = stacked(totals)
        return [Joint(p, sizes) for p in exchange(lambda k: cut(rows, k, Dl, 1))]

    def by_grad(got):
        return [list(same) for same in zip(*(g.parts() for g in got))]

    ng, nc = norm1_gain.shape[0], conv_bias.shape[0]
    packed = jnp.concatenate(
        [
            norm1_gain,
            norm2_gain,
            conv_weight.reshape(-1),
            conv_bias,
            gate_a_bias,
            gate_x_bias,
            decay_param,
        ]
    )
    gate_size = 2 * hpg * bw_here * bw
    gate_rows = -(-(gate_size + packed.shape[0]) // (16 * Dl)) * 16
    gates_flat = jnp.stack([gate_a_weight, gate_x_weight]).reshape(
        2, t, hpg, bw_here, bw
    )
    gates_flat = gates_flat.transpose(1, 0, 2, 3, 4).reshape(t, gate_size)
    extra = gate_size + packed.shape[0]
    gates_flat = jnp.concatenate(
        [
            gates_flat,
            jnp.broadcast_to(packed, (t,) + packed.shape),
            jnp.zeros((t, gate_rows * Dl - extra), BF),
        ],
        axis=1,
    )
    mine_all = jnp.concatenate(
        [
            w_input.T.reshape(t, cz, Dl),
            w_branch.T.reshape(t, cz, Dl),
            gates_flat.reshape(t, gate_rows, Dl),
            w_output.reshape(t, cz, Dl),
            w_gate.T.reshape(t, fz, Dl),
            w_up.T.reshape(t, fz, Dl),
        ],
        axis=1,
    )
    def normed(value, gain):
        wide = value.astype(F32)
        scale = lax.rsqrt(jnp.mean(wide * wide, axis=1, keepdims=True) + epsilon)
        return wide * scale, scale

    rows_a = 2 * cz + gate_rows
    v.z_in = chunk_pieces(inputs, 16)
    v.blocks = exchange(lambda k: pick(mine_all, k))
    v.cotangent, v.w_down = cotangent, w_down
    v.zeros = [jnp.zeros((M * size, D), BF) for size in (cz, cz, gate_rows, cz, fz, fz, fz)]
    v.barrier()

    block = from_group(v.take("blocks"))
    block_a = block[:rows_a]
    block_b = block[rows_a : rows_a + cz]
    block_g = block[rows_a + cz :]
    v.ring_a = [block_a] + [zshift(block_a, k) for k in range(1, M)]
    v.b, v.g = [block_b], [block_g]
    v.y_first = to_groups(block_a, block_b, block_g)
    zeros = v.take("zeros")
    v.full_a = [fill_own(f, p, 0) for f, p in zip(zeros[:3], mixer_parts(block_a))]
    v.full_b = fill_own(zeros[3], block_b, 0)
    v.full_g = [
        fill_own(f, p, 0) for f, p in zip(zeros[4:6], (block_g[:fz], block_g[fz:]))
    ]
    v.full_d = zeros[6]
    resets = jnp.pad(reset_mask.astype(BF), (0, 16 * D - L)).reshape(16, D)
    v.own_in = jnp.concatenate([joined(v.take("z_in")), resets])
    v.far_in = far(v.own_in)
    v.barrier()

    y_next = to_groups(*v.ring_a[1:])
    ring_bg = ring_next(v.b[-1], v.g[-1])
    y_a, y_b, y_g = by_block(v.take("y_first"))
    v.d = exchange(lambda k: cut(v.w_down, k, fz, 0))
    v.take("w_down")
    v.full_a = fill_mixer_far(v.full_a, y_a, 0)
    for k, mine in enumerate(v.take("ring_a")[1:], 1):
        v.full_a = [fill_own(f, p, k) for f, p in zip(v.full_a, mixer_parts(mine))]
    v.full_b = fill_far(v.full_b, y_b, 0)
    v.full_g = [
        fill_far(f, [y[n * fz : (n + 1) * fz] for y in y_g], 0)
        for n, f in enumerate(v.full_g)
    ]
    v.take("b")
    v.take("g")
    v.ring_bg = ring_bg
    slots_in = [v.own_in, tp(v.own_in, 1)]
    if parts > 1:
        slots_in += [v.far_in, tp(v.far_in, 1)]
    v.take("far_in")
    resets = jnp.stack([e[16 + Lc :].reshape(-1)[:L].astype(F32) for e in slots_in])
    open_ = 1.0 - jnp.maximum(resets, (jnp.arange(L) % SEQ == 0).astype(F32))
    back1 = jnp.pad(open_, ((0, 0), (1, 0)))[:, :L]
    back2 = jnp.pad(open_, ((0, 0), (2, 0)))[:, :L]
    masks = jnp.stack([open_, open_ * back1, open_ * back1 * back2, 1.0 - open_], axis=1)
    masks = jnp.pad(masks, ((0, 0), (0, 0), (0, HALO)))
    masks = lax.dynamic_slice(masks, (0, 0, z * Lc), (t, 4, Lc + HALO))
    masks = masks.transpose(0, 2, 1)

    v.masks = masks
    v.own_in = v.own_in[16 : 16 + Lc]
    v.groups_in = jnp.concatenate([e[16 : 16 + Lc] for e in slots_in])
    v.ahead_in = jnp.concatenate([e[:16] for e in slots_in])
    v.scale_in = normed(v.groups_in, None)[1]
    v.y_a = y_next
    v.barrier()

    def fill_gate(k, own=None, others=None):
        for n in range(2):
            rows = slice(n * fz, (n + 1) * fz)
            if own is not None:
                v.full_g[n] = fill_own(v.full_g[n], own[rows], k)
            if others is not None:
                v.full_g[n] = fill_far(v.full_g[n], [y[rows] for y in others], k)

    b_1, g_1 = v.take("ring_bg").parts()
    d_0 = from_group(v.take("d"))
    v.full_d = fill_own(v.full_d, d_0, 0)
    v.y_1 = to_groups(b_1, g_1, d_0)
    v.ring = ring_next(b_1, g_1, d_0)
    v.full_b = fill_own(v.full_b, b_1, 1)
    fill_gate(1, own=g_1)
    for k, others in enumerate(by_block(v.take("y_a")), 1):
        v.full_a = fill_mixer_far(v.full_a, others, k)
    w_in_t, w_br_t, rest = v.take("full_a")
    rest = rest.reshape(M, gate_rows, DP, Dl).transpose(0, 2, 1, 3)
    rest = rest.reshape(M, DP, gate_rows * Dl)
    gates = rest[:, :, :gate_size].reshape(M, DP, 2, hpg, bw_here, bw)
    gates = gates.transpose(2, 0, 3, 1, 4, 5).reshape(2, nh, bw, bw)
    dense = []
    for kind in range(2):
        rows = [
            jnp.pad(gates[kind, n], ((0, 0), (n * bw, (nh - 1 - n) * bw)))
            for n in range(nh)
        ]
        dense.append(jnp.concatenate(rows))
    wa, wx = dense
    v.w_in_t, v.w_br_t, v.wa, v.wx = w_in_t, w_br_t, wa, wx
    every = rest[:, :, gate_size : gate_size + packed.shape[0]].astype(F32)
    gains = jnp.stack([pick(every[:, :, : 2 * ng], (z - b) % M) for b in range(M)])
    gain_one = gains[:, :, :ng].reshape(1, D)
    gain_two = gains[:, :, ng:].reshape(1, D)
    vectors = every[:, :, 2 * ng :].reshape(M, DP, conv + 4, nc).transpose(2, 0, 1, 3)
    vectors = pick(vectors.reshape(conv + 4, M, t, cz), q, 2).reshape(conv + 4, C)
    conv_w = vectors[:conv]
    decay = vectors[conv + 3]
    log_slope = -8.0 * jax.nn.softplus(decay)
    vec = jnp.stack(
        [vectors[conv], vectors[conv + 1], vectors[conv + 2], log_slope]
        + [jnp.zeros_like(decay)] * 4
    )

    v.vec, v.conv_w, v.gain_one, v.gain_two = vec, conv_w, gain_one, gain_two
    v.n1 = (v.take("groups_in").astype(F32) * v.take("scale_in") * v.gain_one).astype(BF)
    ahead = (normed(v.take("ahead_in"), None)[0] * v.gain_one).astype(BF)

    def mixed_sum(*pairs):
        return products(
            NN, [list(pairs)], [], [BF], lambda total: (total,), "product", halves=True
        )

    def chain(ends, sign):
        total = jnp.zeros_like(ends[..., 4:5, :])
        for k in reversed(range(1, M)):
            got = zline(ends, sign * k)
            total = got[..., 4:5, :] + got[..., 0:1, :] * total
        return total

    shape = (t, Lc, C)
    v.rnn = dot_nt(v.n1, v.w_in_t).reshape(shape)
    v.gin = dot_nt(v.n1, v.w_br_t).reshape(shape)
    v.halos = dot_nt(ahead, v.w_in_t).reshape(t, 16, C)[:, 16 - HALO :]
    v.barrier()

    b_next, g_next, v.d = v.take("ring").parts()
    v.b, v.g = [b_next], [g_next]
    v.y_2 = to_groups(b_next, g_next)
    while len(v.b) < M - 2:
        b_next, g_next = ring_next(b_next, g_next).parts()
        v.b, v.g = v.b + [b_next], v.g + [g_next]
    v.fwd = seq_call(
        forward_kernel,
        [v.rnn, v.halos, v.masks],
        [v.conv_w, v.vec, v.wa, v.wx],
        [(shape, F32, True)] * 5 + [((t, 8, C), F32, True)],
        [pltpu.VMEM((Lc + HALO, C), F32)],
        "recurrence",
        40,
    )
    v.barrier()

    y_next = to_groups(*v.b[1:])
    y_b, y_g, y_d = by_block(v.take("y_1"))
    v.full_b = fill_far(v.full_b, y_b, 1)
    fill_gate(1, others=y_g)
    v.full_d = fill_far(v.full_d, y_d, 0)
    y_b, y_g = by_block(v.take("y_2"))
    v.full_b = fill_far(v.full_b, y_b, 2)
    fill_gate(2, others=y_g)
    for k, mine in enumerate(v.take("b"), 2):
        v.full_b = fill_own(v.full_b, mine, k)
    for k, mine in enumerate(v.g, 2):
        fill_gate(k, own=mine)
    v.full_d = fill_own(v.full_d, v.d, 1)
    v.cin = chain(v.fwd[5], 1)
    v.state = v.fwd[3] + v.fwd[4] * v.cin
    v.mixer = (gelu_parts(v.gin)[0] * v.state).astype(BF).reshape(t * Lc, C)
    v.fwd = v.fwd[:3]
    v.y_b = y_next
    v.barrier()

    for k, others in enumerate(by_block(v.take("y_b")), 3):
        v.full_b = fill_far(v.full_b, others, k)
    v.w_out = v.take("full_b")
    v.y_g = to_groups(*v.take("g")[1:], v.d)
    v.d = [v.d]
    while len(v.d) < M - 2:
        v.d = v.d + ring_next(v.d[-1]).parts()
    rec_sum = None
    for p in reversed(range(parts)):
        part = send_sum(mixed_sum(((v.mixer, p, parts), v.w_out)), p)
        rec_sum = part if rec_sum is None else rec_sum + part
    v.resid_mid = v.own_in.astype(F32) + rec_sum
    v.unit_two, v.scale_two = normed(v.resid_mid, v.gain_two)
    v.n2_own = (v.unit_two * v.gain_two).astype(BF)
    v.barrier()

    got = by_block(v.take("y_g"))
    for k, others in enumerate(got[:-1], 3):
        fill_gate(k, others=others)
    v.full_d = fill_far(v.full_d, got[-1], 1)
    v.w_gate_t, v.w_up_t = v.take("full_g")
    for k, mine in enumerate(v.d[1:], 2):
        v.full_d = fill_own(v.full_d, mine, k)
    v.z_cot = chunk_pieces(v.take("cotangent"), rider=folded(v.d[-1]))
    v.n2_far = far(v.n2_own)
    v.n2 = [jnp.concatenate([v.n2_own, tp(v.n2_own, 1)])]
    v.take("n2_own")

    def mlp_forward(p):
        return products(
            NT,
            [[(v.n2[p], v.w_gate_t)], [(v.n2[p], v.w_up_t)]],
            [],
            [F32, F32, BF],
            lambda gate, up: (gate, up, gelu_parts(gate)[0] * up),
            "mlp",
        )

    v.mlp = [mlp_forward(0)]
    v.barrier()

    v.d = v.d[1:] + [unfolded(v.z_cot[1][Lc:])]
    v.z_cot[1] = v.z_cot[1][:Lc]
    v.y_d = to_groups(*v.d)
    cot_own = joined(v.take("z_cot"))
    v.cot = [jnp.concatenate([cot_own, tp(cot_own, 1)])]
    v.far_cot = far(cot_own)
    if parts > 1:
        v.n2.append(jnp.concatenate([v.n2_far, tp(v.n2_far, 1)]))
        v.mlp.append(mlp_forward(1))
    v.take("n2_far")
    v.barrier()

    def summed(lefts, rights, groups=None):
        groups = range(O) if groups is None else groups
        out = [
            products(
                TN,
                [list(zip(lefts, rights))],
                [],
                [BF],
                lambda total: (total,),
                "gradient",
                base=((o + r) % O) * half,
                width=half,
            )[0]
            for r in reversed(groups)
        ]
        return out[::-1]

    v.full_d = fill_own(v.full_d, v.take("d")[-1], M - 1)
    for k, others in enumerate(by_block(v.take("y_d")), 2):
        v.full_d = fill_far(v.full_d, others, k)
    v.w_dn = v.take("full_d")
    if parts > 1:
        v.cot.append(jnp.concatenate([v.far_cot, tp(v.far_cot, 1)]))
    v.take("far_cot")

    def mlp_back(p):
        def finish(d_hidden, gate, up):
            gelu, slope = gelu_parts(gate)
            return d_hidden * up * slope, d_hidden * gelu

        return products(
            NT, [[(v.cot[p], v.w_dn)]], list(v.mlp[p][:2]), [BF, BF], finish, "mlp_back"
        )

    def mlp_back_in(p):
        gate, up = v.d_mlp[p]
        return mixed_sum((gate, v.w_gate_t), (up, v.w_up_t))

    out = [mixed_sum((m[2], v.w_dn)) for m in v.mlp]
    got = joint(lambda b: tp(b, 1), [part[1] for part in out]).parts()
    out_sum = out[0][0].astype(F32) + got[0].astype(F32)
    if parts > 1:
        there = out[1][0].astype(F32) + got[1].astype(F32)
        out_sum = out_sum + tp(there.astype(BF), 2).astype(F32)
    v.output = (v.take("resid_mid") + out_sum).astype(BF)
    v.grad_down = summed([m[2] for m in v.mlp], v.cot)
    v.d_mlp = [None] * parts
    v.d_mlp[last] = mlp_back(last)
    v.barrier()

    v.y_down = grad_y(v.take("grad_down"))
    pieces = back_pieces(v.take("output"))
    v.z_out = [zshift(piece, k) if k else piece for k, piece in enumerate(pieces)]
    v.dn2 = [None] * parts
    v.dn2[last] = mlp_back_in(last)
    v.dn2_sum = send_sum(v.dn2[last], last) if last else None
    for p in range(last):
        v.d_mlp[p] = mlp_back(p)
        v.dn2[p] = mlp_back_in(p)
    v.grad_gate = summed([d[0] for d in v.d_mlp], v.n2, range(1, O))
    v.take("mlp")
    v.cot_own = v.take("cot")[0][:Lc]
    v.barrier()

    (v.y_down,) = y_parts(v.y_down)
    v.output = back_joined(v.take("z_out"))
    v.ring = ring_step((v.y_down, 1, None))
    v.y_gate = grad_y(
        summed([d[0] for d in v.d_mlp], v.n2, range(1)) + v.take("grad_gate")
    )
    dn2_sum = v.take("dn2_sum")
    for p in reversed(range(last if last else 1)):
        part = send_sum(v.dn2[p], p)
        dn2_sum = part if dn2_sum is None else dn2_sum + part
    v.take("dn2")

    def norm_back(grad, unit, scale, gain):
        weighted = grad * gain
        dots = jnp.mean(weighted * unit, axis=1, keepdims=True)
        return scale * (weighted - unit * dots), jnp.sum(grad * unit, axis=0)

    back_two, v.gain_two_grad = norm_back(dn2_sum, v.unit_two, v.scale_two, v.gain_two)
    v.d_mid = v.take("cot_own").astype(F32) + back_two
    v.d_own = v.d_mid.astype(BF)
    v.far_branch = far(v.d_own)
    v.near_branch = tp(v.d_own, 1)
    v.grad_up = summed([d[1] for d in v.d_mlp], v.n2)
    v.take("n2")
    v.take("d_mlp")
    v.barrier()

    (v.y_gate,) = y_parts(v.y_gate)
    (r_down,) = v.ring.parts()
    v.ring = ring_step((v.y_down, 2, r_down), (v.y_gate, 1, None))
    v.y_up = grad_y(v.take("grad_up"))
    slots_of = [v.take("d_own"), v.take("near_branch")]
    if parts > 1:
        slots_of += [v.far_branch, tp(v.far_branch, 1)]
    v.take("far_branch")
    v.d_branch = jnp.concatenate(slots_of)
    v.adjoint = seq_call(
        adjoint_kernel,
        [
            dot_nt(v.d_branch, v.w_out).reshape(shape),
            v.take("gin"),
            v.state,
            v.fwd[1],
            v.masks,
        ],
        [v.vec],
        [(shape, F32, True)] * 2 + [(shape, BF, True), ((t, 8, C), F32, True)],
        [],
        "adjoint",
        24,
    )
    v.d_gin = v.adjoint[2].reshape(t * Lc, C)
    v.grad_branch = summed([v.d_gin], [v.n1])
    v.barrier()

    (v.y_up,) = y_parts(v.y_up)
    v.edges = jnp.concatenate(
        [
            jnp.broadcast_to(v.take("cin"), (t, 4, C)),
            jnp.broadcast_to(chain(v.adjoint[3], -1), (t, 4, C)),
        ],
        1,
    )
    v.grad_output = summed([v.take("mixer")], [v.take("d_branch")])
    v.barrier()

    r_down, r_gate = v.ring.parts()
    v.ring = ring_step((v.y_down, 3, r_down), (v.y_gate, 2, r_gate), (v.y_up, 1, None))
    v.y_mixer = grad_y(v.take("grad_output"), v.take("grad_branch"))
    mixed, gate_a, gate_x = v.fwd
    lam, prod, _, _ = v.adjoint

    def run_back(rows, time):
        tokens = [lam, prod, v.state, gate_a, gate_x, mixed, v.rnn]
        if rows < Lc:
            tokens = [array[:, :rows] for array in tokens]
        return seq_call(
            backward_kernel,
            tokens + [v.halos, v.masks[:, : rows + HALO], v.edges],
            [v.conv_w, v.vec, v.wa, v.wx],
            [
                ((t, rows, C), BF, True),
                ((t, HALO, C), F32, True),
                ((t, HALO, C), F32, True),
                ((C, C), F32, False),
                ((C, C), F32, False),
                ((8, 8, C), F32, False),
            ],
            [pltpu.VMEM((rows + HALO, C), F32)] * 3,
            "recurrence_back",
            time,
        )

    v.following = zline(run_back(2 * HALO, 4)[1], -1)
    v.d_rnn, _, v.tails, v.grad_wa, v.grad_wx, v.grad_vec = run_back(Lc, 40)
    for name in ("adjoint", "fwd", "state", "rnn", "halos", "edges"):
        v.take(name)
    v.barrier()

    following = v.take("following")
    fix = [jnp.zeros((t, 1, C), F32)] * HALO
    for k in range(1, 4):
        for n in range(k):
            row = HALO - k + n
            fix[row] = fix[row] + v.conv_w[k] * (
                v.masks[:, Lc + n : Lc + n + 1, k - 1 : k] * following[:, n : n + 1]
            )
    tail = (v.take("tails") + jnp.concatenate(fix, axis=1)).astype(BF)
    v.d_rnn = put(v.d_rnn, tail, 0, Lc - HALO, 0).reshape(t * Lc, C)
    v.r_down, r_gate, r_up = v.take("ring").parts()
    y_output, y_branch = y_parts(v.take("y_mixer"))
    rings = ring_sends((v.y_gate, 3, r_gate), (v.y_up, 2, r_up))

    def direct(rings, *grads):
        got = []
        for k, send in enumerate(direct_sends(*grads)):
            send = send + rings if k == M - 1 else send
            got.append(joint(lambda b: zshift(b, M - k) if k else b, send))
        return got

    v.z_mixer = direct(rings, y_output, y_branch)
    gates_grad = jnp.stack(
        [
            jnp.stack(
                [g[n * bw : (n + 1) * bw, n * bw : (n + 1) * bw] for n in range(nh)]
            )
            for g in (v.take("grad_wa"), v.take("grad_wx"))
        ]
    )
    gates_grad = gates_grad.reshape(2, M, hpg, DP, bw_here, bw)
    gates_grad = gates_grad.transpose(1, 3, 0, 2, 4, 5).reshape(M, DP, gate_size)
    small = jnp.sum(v.take("grad_vec"), axis=1).reshape(2 * conv, M, O, nc)
    small = small.transpose(1, 2, 0, 3).reshape(M, O, 2 * conv * nc)
    small = put(jnp.zeros((M, DP, 2 * conv * nc), F32), small, 0, q * O, 0)
    gain_two_grad = v.take("gain_two_grad").reshape(M, DP, ng)
    gain_two_grad = jnp.stack([pick(gain_two_grad, (z - k) % M) for k in range(M)])
    gates_grad = jnp.concatenate([gates_grad, small, gain_two_grad], axis=2)
    gates_grad = jnp.pad(
        gates_grad, ((0, 0), (0, 0), (0, gate_rows * Dl - gates_grad.shape[2]))
    )
    gates_grad = gates_grad.reshape(M, DP, gate_rows, Dl).transpose(0, 2, 1, 3)
    gates_grad = gates_grad.reshape(M * gate_rows, D).astype(BF)
    gates_grad = [cut(gates_grad, (o + r) % O, half, 1) for r in range(O)]
    v.y_in = grad_y(summed([v.d_rnn], [v.n1]), gates_grad)
    v.take("n1")
    v.dn1 = [
        mixed_sum(((v.d_rnn, p, parts), v.w_in_t), ((v.d_gin, p, parts), v.w_br_t))
        for p in range(parts)
    ]
    for name in ("d_rnn", "d_gin", "w_in_t", "w_br_t", "wa", "wx", "masks", "vec"):
        v.take(name)
    v.barrier()

    v.z_down = ring_end(v.take("y_down"), v.take("r_down"))
    r_gate, r_up = v.z_mixer[M - 1].parts()[2:]
    v.z_gate = ring_end(v.take("y_gate"), r_gate)
    v.z_in = direct(ring_sends((v.y_up, 3, r_up)), *y_parts(v.take("y_in")))
    dn1_sum = None
    for p in reversed(range(parts)):
        part = send_sum(v.dn1[p], p)
        dn1_sum = part if dn1_sum is None else dn1_sum + part
    v.dn1 = dn1_sum
    v.barrier()

    def added(pieces):
        return [
            sum(p.astype(F32) for p in same).astype(BF)
            for same in zip(*(piece.parts()[:2] for piece in pieces))
        ]

    r_up = v.z_in[M - 1].parts()[2]

    z_output, z_branch = added(v.take("z_mixer"))
    z_in, z_gates = added(v.take("z_in"))
    z_up = ring_end(v.take("y_up"), r_up)
    totals = exchange_grads(
        v.take("z_down"), v.take("z_gate"), z_up, z_output, z_branch, z_in, z_gates
    )
    unit_one, scale_one = normed(v.own_in, v.gain_one)
    back_one, gain_one_grad = norm_back(v.take("dn1"), unit_one, scale_one, v.gain_one)
    pieces = back_pieces((v.d_mid + back_one).astype(BF))
    sums = jnp.broadcast_to(gain_one_grad.astype(BF), (16, D))
    joints = []
    for k, piece in enumerate(pieces):
        joint = jnp.concatenate([piece, cut(sums, (z + k) % M, FH, 1)])
        joints.append(zshift(joint, k) if k else joint)
    *whole, last_rows = by_grad(totals)
    v.joints = joints
    v.grads = [grad_end(total) for total in whole]
    v.last_rows = last_rows
    v.barrier()

    grad_down, grad_gate, grad_up, grad_output, grad_branch, grad_in = v.grads
    input_grad = back_joined([joint[:Lc] for joint in v.joints]).astype(F32)
    gain_one_grad = sum(joint[Lc].astype(F32) for joint in v.joints)
    step = 1
    while step < DP:
        gain_one_grad = gain_one_grad + tp(gain_one_grad, step)
        step *= 2
    gain_one_grad = cut(gain_one_grad, i_dp, ng, 0)
    output = v.output

    rest_in = jnp.stack([piece.reshape(-1) for piece in v.last_rows])
    small = jnp.sum(rest_in[:, gate_size:].astype(F32), axis=0)
    rest_in = jnp.stack([pick(rest_in, q ^ k) for k in range(t)])
    mine = small[: 2 * conv * nc].reshape(2 * conv, nc)
    gain_two_grad = small[2 * conv * nc : 2 * conv * nc + ng]
    decay_grad = mine[conv + 3] * (-8.0 * jax.nn.sigmoid(decay_param.astype(F32)))

    gates_back = rest_in[:, :gate_size].reshape(t, 2, hpg, bw_here, bw)
    gates_back = gates_back.transpose(1, 0, 2, 3, 4)
    gates_back = gates_back.reshape(2, heads_here, bw_here, bw).astype(F32)

    def flipped(value):
        return lax.optimization_barrier(value).T.astype(F32)

    return (
        output,
        input_grad,
        gain_one_grad,
        flipped(grad_in),
        flipped(grad_branch),
        grad_output.astype(F32),
        mine[:conv],
        mine[conv],
        gates_back[0],
        mine[conv + 1],
        gates_back[1],
        mine[conv + 2],
        decay_grad,
        gain_two_grad,
        flipped(grad_gate),
        flipped(grad_up),
        grad_down.astype(F32),
    )


def solution(mesh):
    both = P(("mp", "dp"))
    wide = P("dp", "mp")
    tall = P("mp", "dp")
    taps = P(None, ("mp", "dp"))
    gate = P("mp", "dp", None)
    params = (both, wide, wide, tall, taps, both, gate, both, gate, both, both, both, wide, wide, tall)
    return jax.shard_map(
        functools.partial(body, mesh.shape["dp"], mesh.shape["mp"]),
        mesh=mesh,
        in_specs=(wide, wide, P("dp")) + params,
        out_specs=(wide, wide) + params,
        check_vma=False,
    )
```

```python
import functools

import jax
import jax.numpy as jnp
from jax import lax
from jax.experimental import pallas as pl
from jax.experimental.pallas import tpu as pltpu
from jax.sharding import PartitionSpec as P

SEQ = 2048
epsilon = 1e-06
BF = jnp.bfloat16
F32 = jnp.float32
HALO = 8


def dot_nt(left, right):
    return lax.dot_general(
        left, right, (((1,), (1,)), ((), ())), preferred_element_type=F32
    )


def dot_nn(left, right):
    return jnp.dot(left, right, preferred_element_type=F32)


def dot_tn(left, right):
    return lax.dot_general(
        left, right, (((0,), (0,)), ((), ())), preferred_element_type=F32
    )


def gelu_parts(value):
    inner = 0.7978845608028654 * (value + 0.044715 * value * value * value)
    tanh = jnp.tanh(inner)
    slope = 0.7978845608028654 * (1.0 + 3.0 * 0.044715 * value * value)
    gelu = 0.5 * value * (1.0 + tanh)
    grad = 0.5 * (1.0 + tanh) + 0.5 * value * (1.0 - tanh * tanh) * slope
    return gelu, grad


def sigmoid(value):
    return 1.0 / (1.0 + jnp.exp(-value))


def one_minus_exp(log_value):
    y = -2.0 * log_value
    series = y * (
        1.0
        - y
        * (1 / 2)
        * (
            1.0
            - y
            * (1 / 3)
            * (1.0 - y * (1 / 4) * (1.0 - y * (1 / 5) * (1.0 - y * (1 / 6))))
        )
    )
    return jnp.where(y < 0.25, series, 1.0 - jnp.exp(-y))


def conv_terms(ext, masks, rows):
    terms = [ext[HALO : HALO + rows]]
    for k in range(1, 4):
        moved = pltpu.roll(ext, k, axis=0)[HALO : HALO + rows]
        terms.append(moved * masks[:, k - 1 : k])
    return terms


def forward_kernel(
    rnn_ref,
    halo_ref,
    mask_ref,
    conv_ref,
    vec_ref,
    wa_ref,
    wx_ref,
    mixed_ref,
    ga_ref,
    gx_ref,
    h_ref,
    p_ref,
    end_ref,
    ext_ref,
):
    length, width = rnn_ref.shape[1:]
    block_rows = min(256, length)
    ext_ref[0:HALO, :] = halo_ref[0]
    ext_ref[HALO:, :] = rnn_ref[0]
    row8 = lax.broadcasted_iota(jnp.int32, (block_rows, 1), 0) % 8

    def block(i, carry):
        h_in, p_in = carry
        r0 = pl.multiple_of(i * block_rows, block_rows)
        masks = mask_ref[0, pl.ds(r0, block_rows), :]
        terms = conv_terms(ext_ref[pl.ds(r0, block_rows + HALO), :], masks, block_rows)
        mixed = vec_ref[0:1, :] + conv_ref[0:1, :] * terms[0]
        for k in range(1, 4):
            mixed = mixed + conv_ref[k : k + 1, :] * terms[k]
        high = mixed.astype(BF)
        low = (mixed - high.astype(F32)).astype(BF)
        gate_a = sigmoid(
            dot_nn(high, wa_ref[...]) + dot_nn(low, wa_ref[...]) + vec_ref[1:2, :]
        )
        gate_x = sigmoid(
            dot_nn(high, wx_ref[...]) + dot_nn(low, wx_ref[...]) + vec_ref[2:3, :]
        )
        begins = masks[:, 3:4]
        log_a = gate_a * vec_ref[3:4, :]
        a = jnp.exp(log_a) * (1.0 - begins)
        scale = jnp.sqrt(one_minus_exp(log_a)) * (1.0 - begins) + begins
        b = mixed * gate_x * scale
        mixed_ref[0, pl.ds(r0, block_rows), :] = mixed
        ga_ref[0, pl.ds(r0, block_rows), :] = gate_a
        gx_ref[0, pl.ds(r0, block_rows), :] = gate_x
        for d in (1, 2, 4):
            valid = row8 >= d
            b = jnp.where(valid, a * pltpu.roll(b, d, axis=0) + b, b)
            a = jnp.where(valid, a * pltpu.roll(a, d, axis=0), a)
        for g in range(block_rows // 8):
            rows = slice(8 * g, 8 * g + 8)
            h = b[rows] + a[rows] * h_in
            p = a[rows] * p_in
            h_ref[0, pl.ds(r0 + 8 * g, 8), :] = h
            p_ref[0, pl.ds(r0 + 8 * g, 8), :] = p
            h_in = h[7:8]
            p_in = p[7:8]
        return h_in, p_in

    h_end, p_end = lax.fori_loop(
        0,
        length // block_rows,
        block,
        (jnp.zeros((1, width), F32), jnp.ones((1, width), F32)),
    )
    end_ref[0, 0:4, :] = jnp.broadcast_to(p_end, (4, width))
    end_ref[0, 4:8, :] = jnp.broadcast_to(h_end, (4, width))


def adjoint_kernel(
    dmix_ref,
    gate_ref,
    state_ref,
    ga_ref,
    mask_ref,
    vec_ref,
    lam_ref,
    q_ref,
    dgi_ref,
    end_ref,
):
    length, width = dmix_ref.shape[1:]
    block_rows = min(64, length)
    row = lax.broadcasted_iota(jnp.int32, (block_rows, 1), 0)
    row8 = row % 8
    blocks = length // block_rows

    def block(i, carry):
        lam_in, q_in, a_next = carry
        r0 = pl.multiple_of((blocks - 1 - i) * block_rows, block_rows)
        here = pl.ds(r0, block_rows)
        begins = mask_ref[0, here, :][:, 3:4]
        d_mixer = dmix_ref[0, here, :]
        gelu, slope = gelu_parts(gate_ref[0, here, :])
        dgi_ref[0, here, :] = (d_mixer * state_ref[0, here, :] * slope).astype(BF)
        b = d_mixer * gelu
        a = jnp.exp(ga_ref[0, here, :] * vec_ref[3:4, :]) * (1.0 - begins)
        c = jnp.where(row == block_rows - 1, a_next, pltpu.roll(a, block_rows - 1, axis=0))
        for d in (1, 2, 4):
            valid = row8 < 8 - d
            b = jnp.where(valid, c * pltpu.roll(b, block_rows - d, axis=0) + b, b)
            c = jnp.where(valid, c * pltpu.roll(c, block_rows - d, axis=0), c)
        for g in reversed(range(block_rows // 8)):
            rows = slice(8 * g, 8 * g + 8)
            lam = b[rows] + c[rows] * lam_in
            q = c[rows] * q_in
            lam_ref[0, pl.ds(r0 + 8 * g, 8), :] = lam
            q_ref[0, pl.ds(r0 + 8 * g, 8), :] = q
            lam_in = lam[0:1]
            q_in = q[0:1]
        return lam_in, q_in, a[0:1]

    one = jnp.ones((1, width), F32)
    lam0, q0, a0 = lax.fori_loop(
        0, blocks, block, (jnp.zeros((1, width), F32), one, one)
    )
    end_ref[0, 0:4, :] = jnp.broadcast_to(a0 * q0, (4, width))
    end_ref[0, 4:8, :] = jnp.broadcast_to(a0 * lam0, (4, width))


def fold8(value):
    total = value[0:8]
    for g in range(1, value.shape[0] // 8):
        total = total + value[8 * g : 8 * g + 8]
    return total


def backward_kernel(
    lam_ref,
    q_ref,
    state_ref,
    ga_ref,
    gx_ref,
    mixed_ref,
    rnn_ref,
    halo_ref,
    mask_ref,
    edge_ref,
    conv_ref,
    vec_ref,
    wa_ref,
    wx_ref,
    drnn_ref,
    head_ref,
    tail_ref,
    wag_ref,
    wxg_ref,
    vg_ref,
    ext_ref,
    prev_ref,
    dm_ref,
):
    length, width = lam_ref.shape[1:]
    block_rows = min(256, length)
    first = pl.program_id(0) == 0

    @pl.when(first)
    def _():
        wag_ref[...] = jnp.zeros_like(wag_ref)
        wxg_ref[...] = jnp.zeros_like(wxg_ref)
        vg_ref[...] = jnp.zeros_like(vg_ref)

    ext_ref[0:HALO, :] = halo_ref[0]
    ext_ref[HALO:, :] = rnn_ref[0]
    prev_ref[0:HALO, :] = jnp.broadcast_to(edge_ref[0, 0:1, :], (HALO, width))
    prev_ref[HALO:, :] = state_ref[0]
    dm_ref[length:, :] = jnp.zeros((HALO, width), F32)

    def block(i, carry):
        r0 = pl.multiple_of(i * block_rows, block_rows)
        here = pl.ds(r0, block_rows)
        masks = mask_ref[0, here, :]
        begins = masks[:, 3:4]
        lam = lam_ref[0, here, :] + q_ref[0, here, :] * edge_ref[0, 4:5, :]
        before = pltpu.roll(prev_ref[pl.ds(r0, block_rows + HALO), :], 1, axis=0)[
            HALO : HALO + block_rows
        ]
        gate_a = ga_ref[0, here, :]
        gate_x = gx_ref[0, here, :]
        mixed = mixed_ref[0, here, :]
        log_a = gate_a * vec_ref[3:4, :]
        decay = jnp.exp(log_a)
        inv_scale = lax.rsqrt(one_minus_exp(log_a))
        scale_raw = jnp.sqrt(one_minus_exp(log_a))
        keep = 1.0 - begins
        scale = scale_raw * keep + begins
        through = lam * mixed
        d_log = lam * before * decay * keep + jnp.where(
            begins > 0.5, 0.0, through * gate_x * (-(decay * decay) * inv_scale)
        )
        log_gate = d_log * gate_a
        d_pre_a = log_gate * (1.0 - gate_a) * vec_ref[3:4, :]
        d_pre_x = through * scale * gate_x * (1.0 - gate_x)
        pa = d_pre_a.astype(BF)
        px = d_pre_x.astype(BF)
        mb = mixed.astype(BF)
        d_mixed = (
            lam * gate_x * scale + dot_nt(pa, wa_ref[...]) + dot_nt(px, wx_ref[...])
        )
        dm_ref[here, :] = d_mixed
        wag_ref[...] += dot_tn(mb, pa)
        wxg_ref[...] += dot_tn(mb, px)
        terms = conv_terms(ext_ref[pl.ds(r0, block_rows + HALO), :], masks, block_rows)
        sums = [d_mixed * term for term in terms]
        sums += [d_mixed, d_pre_a, d_pre_x, log_gate]
        for n, value in enumerate(sums):
            vg_ref[n] += fold8(value)
        return carry

    lax.fori_loop(0, length // block_rows, block, 0)

    def shift(i, carry):
        r0 = pl.multiple_of(i * block_rows, block_rows)
        ext = dm_ref[pl.ds(r0, block_rows + HALO), :]
        masks = mask_ref[0, pl.ds(r0, block_rows + HALO), :]
        total = conv_ref[0:1, :] * ext[0:block_rows]
        for k in range(1, 4):
            moved = pltpu.roll(ext * masks[:, k - 1 : k], block_rows + HALO - k, axis=0)
            total = total + conv_ref[k : k + 1, :] * moved[0:block_rows]
        drnn_ref[0, pl.ds(r0, block_rows), :] = total.astype(BF)

        @pl.when(i == length // block_rows - 1)
        def _():
            tail_ref[0] = total[block_rows - HALO :]

        return carry

    lax.fori_loop(0, length // block_rows, shift, 0)
    head_ref[0] = dm_ref[0:HALO, :]


def block_specs(shapes):
    specs = []
    for shape, moving in shapes:
        if moving:
            specs.append(
                pl.BlockSpec((1,) + shape[1:], lambda i, n=len(shape): (i,) + (0,) * (n - 1))
            )
        else:
            specs.append(pl.BlockSpec(shape, lambda i, n=len(shape): (0,) * n))
    return specs


def cost(time):
    return pl.CostEstimate(flops=int(time * 1.0e8), bytes_accessed=0, transcendentals=0)


NT = (((1,), (1,)), ((), ()))
NN = (((1,), (0,)), ((), ()))
TN = (((0,), (0,)), ((), ()))


def seq_call(kernel, moving, fixed, outs, scratch, name, time):
    count = moving[0].shape[0]
    return pl.pallas_call(
        kernel,
        grid=(count,),
        in_specs=block_specs(
            [(a.shape, True) for a in moving] + [(a.shape, False) for a in fixed]
        ),
        out_specs=block_specs([(shape, move) for shape, _, move in outs]),
        out_shape=[jax.ShapeDtypeStruct(shape, dtype) for shape, dtype, _ in outs],
        scratch_shapes=scratch,
        compiler_params=pltpu.CompilerParams(
            dimension_semantics=("arbitrary",), vmem_limit_bytes=60 * 1024 * 1024
        ),
        cost_estimate=cost(time),
        name=name,
    )(*moving, *fixed)


def products(dims, sums, extras, outs, finish, name, base=None, width=None, halves=False):
    full = sums[0][0][1].shape[0 if dims == NT else 1]
    width = width or full
    columns = min(256, width)
    lefts, rights, where = [], [], []
    for pairs in sums:
        places = []
        for left, right in pairs:
            left = left if isinstance(left, tuple) else (left, 0, 1)
            known = [n for n, other in enumerate(lefts) if other[0] is left[0]]
            places.append(known[0] if known else len(lefts))
            if not known:
                lefts.append(left)
            rights.append(right)
        where.append(places)
    array, _, count = lefts[0]
    rows = array.shape[1] if dims == TN else array.shape[0] // count
    cuts = 2 if halves else 1
    near = len(lefts) + len(rights)

    def kernel(_, *refs):
        at, totals = len(lefts), []
        for places in where:
            total = None
            for place in places:
                term = lax.dot_general(
                    refs[place][...], refs[at][...], dims, preferred_element_type=F32
                )
                total = term if total is None else total + term
                at += 1
            totals.append(total)
        values = finish(*totals, *(ref[...] for ref in refs[near : near + len(extras)]))
        size = rows // cuts
        at = near + len(extras)
        for value in values:
            for n in range(cuts):
                refs[at][...] = value[n * size : (n + 1) * size].astype(refs[at].dtype)
                at += 1

    def whole(left):
        array, part, count = left
        shape = (array.shape[0] // count, array.shape[1])
        return pl.BlockSpec(shape, lambda j, b: (part, 0))

    def moving(array):
        if dims == NT:
            return pl.BlockSpec((columns, array.shape[1]), lambda j, b: (b[0] + j, 0))
        return pl.BlockSpec((array.shape[0], columns), lambda j, b: (0, b[0] + j))

    base = jnp.zeros((1,), jnp.int32) if base is None else (base // columns).reshape(1)
    tile = pl.BlockSpec((rows, columns), lambda j, b: (0, j))
    part = pl.BlockSpec((rows // cuts, columns), lambda j, b: (0, j))
    return pl.pallas_call(
        kernel,
        grid_spec=pltpu.PrefetchScalarGridSpec(
            num_scalar_prefetch=1,
            grid=(width // columns,),
            in_specs=[whole(a) for a in lefts]
            + [moving(a) for a in rights]
            + [tile] * len(extras),
            out_specs=[part] * (len(outs) * cuts),
        ),
        out_shape=[
            jax.ShapeDtypeStruct((rows // cuts, width), dtype)
            for dtype in outs
            for _ in range(cuts)
        ],
        compiler_params=pltpu.CompilerParams(
            dimension_semantics=("arbitrary",), vmem_limit_bytes=60 * 1024 * 1024
        ),
        cost_estimate=cost(sum(a.size for a in rights) // (width and full) * width * rows / 3.4e8),
        name=name,
    )(base, *(left[0] for left in lefts), *rights, *extras)


@jax.tree_util.register_pytree_node_class
class Joint:
    def __init__(self, rows, sizes):
        self.rows, self.sizes = rows, sizes

    def tree_flatten(self):
        return (self.rows,), self.sizes

    @classmethod
    def tree_unflatten(cls, sizes, children):
        return cls(children[0], sizes)

    def parts(self):
        at, out = 0, []
        for size in self.sizes:
            out.append(self.rows[at : at + size])
            at += size
        return out


def body(
    DP,
    M,
    inputs,
    cotangent,
    reset_mask,
    norm1_gain,
    w_input,
    w_branch,
    w_output,
    conv_weight,
    conv_bias,
    gate_a_weight,
    gate_a_bias,
    gate_x_weight,
    gate_x_bias,
    decay_param,
    norm2_gain,
    w_gate,
    w_up,
    w_down,
):
    heads_here, bw_here, bw = gate_a_weight.shape
    t = 4 if heads_here % 4 == 0 and DP % 4 == 0 else 2
    O = DP // t
    hpg = heads_here // t
    nh = M * hpg
    L, FH = inputs.shape
    D = FH * M
    Dl = w_input.shape[0]
    Lc = L // M
    half = t * Dl
    cz = w_input.shape[1] // t
    fz = w_gate.shape[1] // t
    C = M * cz
    FC = M * fz
    conv = conv_weight.shape[0]
    parts = t // 2
    last = parts - 1

    i_dp = lax.axis_index("dp")
    z = lax.axis_index("mp")
    q = i_dp % t
    o = i_dp // t

    def tp(value, j):
        return lax.ppermute(value, "dp", [(i, i ^ j) for i in range(DP)])

    def oshift(value, r):
        return lax.ppermute(
            value, "dp", [(i, ((i // t + r) % O) * t + i % t) for i in range(DP)]
        )

    def zshift(value, k):
        return lax.ppermute(value, "mp", [(i, (i + k) % M) for i in range(M)])

    def zline(value, k):
        got = lax.ppermute(
            value, "mp", [(i, i + k) for i in range(M) if 0 <= i + k < M]
        )
        return jnp.roll(got, k * cz, axis=-1)

    class Live(dict):
        __getattr__ = dict.__getitem__
        __setattr__ = dict.__setitem__

        def barrier(self):
            held = lax.optimization_barrier(dict(self))
            self.clear()
            self.update(held)

        def take(self, name):
            return self.pop(name)

    v = Live()

    def cut(array, index, size, axis):
        return lax.dynamic_slice_in_dim(array, index * size, size, axis)

    def put(array, piece, *starts):
        return lax.dynamic_update_slice(array, piece, starts)

    def pick(array, index, axis=0):
        return lax.dynamic_index_in_dim(array, index, axis, keepdims=False)

    def chunk_pieces(value, ahead=0, rider=None, which=range(M)):
        if ahead:
            value = jnp.concatenate([jnp.zeros((ahead, FH), value.dtype), value])
        pieces = [
            lax.dynamic_slice_in_dim(value, (z + k) % M * Lc, Lc + ahead, 0)
            for k in range(M)
        ]
        if rider is not None:
            pieces[1] = jnp.concatenate([pieces[1], rider])
        return {k: zshift(pieces[k], k) if k else pieces[k] for k in which}

    def joined(pieces):
        own = jnp.zeros((pieces[0].shape[0], D), pieces[0].dtype)
        for k, piece in pieces.items():
            own = put(own, piece, 0, ((z - k) % M) * FH)
        return own

    def far(value):
        return tp(value, 2) if parts > 1 else None

    def back_pieces(value):
        return [cut(value, (z + k) % M, FH, 1) for k in range(M)]

    def back_joined(pieces):
        out = jnp.zeros((L, FH), pieces[0].dtype)
        for k, piece in enumerate(pieces):
            out = put(out, piece, ((z - k) % M) * Lc, 0)
        return out

    def send_sum(part, p):
        mine = part[0].astype(F32) + tp(part[1], 1).astype(F32)
        if p:
            mine = tp(mine.astype(BF), 2).astype(F32)
        return mine

    def stacked(blocks):
        return jnp.concatenate(blocks) if len(blocks) > 1 else blocks[0]

    def joint(transfer, blocks):
        return Joint(transfer(stacked(blocks)), tuple(b.shape[0] for b in blocks))

    def exchange(mine):
        if parts == 1:
            return [mine(q), tp(mine(q ^ 1), 1)]
        got = tp(jnp.stack([mine(q ^ 1), mine(q ^ 3)]), 1)
        after = tp(jnp.stack([mine(q ^ 2), got[1]]), 2)
        return [mine(q), got[0], after[0], after[1]]

    def from_group(pieces):
        block = jnp.zeros((pieces[0].shape[0], half), BF)
        for j, piece in enumerate(pieces):
            block = put(block, piece, 0, (q ^ j) * Dl)
        return block

    def to_groups(*blocks):
        return [joint(lambda b: oshift(b, r), blocks) for r in range(1, O)]

    def by_block(got):
        return [list(same) for same in zip(*(g.parts() for g in got))]

    def ring_next(*blocks):
        return joint(lambda b: zshift(b, 1), blocks)

    def fill_own(full, block, s):
        return put(full, block, s * block.shape[0], o * half)

    def fill_far(full, others, s):
        for r, piece in enumerate(others, 1):
            full = put(full, piece, s * piece.shape[0], ((o - r) % O) * half)
        return full

    def mixer_parts(block):
        return block[:cz], block[cz : 2 * cz], block[2 * cz :]

    def fill_mixer_far(full, others, s):
        split = [mixer_parts(piece) for piece in others]
        return [fill_far(f, [g[n] for g in split], s) for n, f in enumerate(full)]

    def folded(block):
        return jnp.concatenate(
            [block[:, n * FH : (n + 1) * FH] for n in range(half // FH)]
        )

    def unfolded(rows):
        size = rows.shape[0] // (half // FH)
        return jnp.concatenate(
            [rows[n * size : (n + 1) * size] for n in range(half // FH)], axis=1
        )

    def grad_y(*grads):
        return [g[0] for g in grads], to_groups_of(grads)

    def to_groups_of(grads):
        return [joint(lambda b: oshift(b, r), [g[r] for g in grads]) for r in range(1, O)]

    def y_parts(held):
        own, got = held
        return [list(same) for same in zip(own, *(g.parts() for g in got))]

    def slot(pieces, k):
        size = pieces[0].shape[0] // M
        return sum(piece[k * size : (k + 1) * size].astype(F32) for piece in pieces)

    def ring_sends(*rings):
        sends = []
        for pieces, k, moving in rings:
            total = slot(pieces, k)
            if moving is not None:
                total = total + moving.astype(F32)
            sends.append(total.astype(BF))
        return sends

    def ring_step(*rings):
        return ring_next(*ring_sends(*rings))

    def ring_end(pieces, moving):
        for k in range(4, M):
            (moving,) = ring_step((pieces, k, moving)).parts()
        return (moving.astype(F32) + slot(pieces, 0)).astype(BF)

    def direct_sends(*grads):
        return [[slot(pieces, k).astype(BF) for pieces in grads] for k in range(M)]

    def grad_end(pieces):
        size = pieces[0].shape[0]
        out = jnp.zeros((t * size, Dl), BF)
        for j, piece in enumerate(pieces):
            out = put(out, piece, (q ^ j) * size, 0)
        return out

    def exchange_grads(*totals):
        sizes = tuple(total.shape[0] for total in totals)
        rows = stacked(totals)
        return [Joint(p, sizes) for p in exchange(lambda k: cut(rows, k, Dl, 1))]

    def by_grad(got):
        return [list(same) for same in zip(*(g.parts() for g in got))]

    ng, nc = norm1_gain.shape[0], conv_bias.shape[0]
    packed = jnp.concatenate(
        [
            norm1_gain,
            norm2_gain,
            conv_weight.reshape(-1),
            conv_bias,
            gate_a_bias,
            gate_x_bias,
            decay_param,
        ]
    )
    gate_size = 2 * hpg * bw_here * bw
    gate_rows = -(-(gate_size + packed.shape[0]) // (16 * Dl)) * 16
    gates_flat = jnp.stack([gate_a_weight, gate_x_weight]).reshape(
        2, t, hpg, bw_here, bw
    )
    gates_flat = gates_flat.transpose(1, 0, 2, 3, 4).reshape(t, gate_size)
    extra = gate_size + packed.shape[0]
    gates_flat = jnp.concatenate(
        [
            gates_flat,
            jnp.broadcast_to(packed, (t,) + packed.shape),
            jnp.zeros((t, gate_rows * Dl - extra), BF),
        ],
        axis=1,
    )
    mine_all = jnp.concatenate(
        [
            w_input.T.reshape(t, cz, Dl),
            w_branch.T.reshape(t, cz, Dl),
            gates_flat.reshape(t, gate_rows, Dl),
            w_output.reshape(t, cz, Dl),
            w_gate.T.reshape(t, fz, Dl),
            w_up.T.reshape(t, fz, Dl),
        ],
        axis=1,
    )
    def normed(value, gain):
        wide = value.astype(F32)
        scale = lax.rsqrt(jnp.mean(wide * wide, axis=1, keepdims=True) + epsilon)
        return wide * scale, scale

    rows_a = 2 * cz + gate_rows
    v.z_in = chunk_pieces(inputs, 16)
    v.blocks = exchange(lambda k: pick(mine_all, k))
    v.cotangent, v.w_down = cotangent, w_down
    v.zeros = [jnp.zeros((M * size, D), BF) for size in (cz, cz, gate_rows, cz, fz, fz, fz)]
    v.barrier()

    block = from_group(v.take("blocks"))
    block_a = block[:rows_a]
    block_b = block[rows_a : rows_a + cz]
    block_g = block[rows_a + cz :]
    v.ring_a = [block_a]
    for _ in range(1, M):
        v.ring_a.append(zshift(v.ring_a[-1], 1))
    v.b, v.g = [block_b], [block_g]
    v.y_first = to_groups(block_a, block_b, block_g)
    zeros = v.take("zeros")
    v.full_a = [fill_own(f, p, 0) for f, p in zip(zeros[:3], mixer_parts(block_a))]
    v.full_b = fill_own(zeros[3], block_b, 0)
    v.full_g = [
        fill_own(f, p, 0) for f, p in zip(zeros[4:6], (block_g[:fz], block_g[fz:]))
    ]
    v.full_d = zeros[6]
    resets = jnp.pad(reset_mask.astype(BF), (0, 16 * D - L)).reshape(16, D)
    v.own_in = jnp.concatenate([joined(v.take("z_in")), resets])
    v.far_in = far(v.own_in)
    v.barrier()

    y_next = to_groups(*v.ring_a[1:])
    ring_bg = ring_next(v.b[-1], v.g[-1])
    y_a, y_b, y_g = by_block(v.take("y_first"))
    v.d = exchange(lambda k: cut(v.w_down, k, fz, 0))
    v.take("w_down")
    v.full_a = fill_mixer_far(v.full_a, y_a, 0)
    for k, mine in enumerate(v.take("ring_a")[1:], 1):
        v.full_a = [fill_own(f, p, k) for f, p in zip(v.full_a, mixer_parts(mine))]
    v.full_b = fill_far(v.full_b, y_b, 0)
    v.full_g = [
        fill_far(f, [y[n * fz : (n + 1) * fz] for y in y_g], 0)
        for n, f in enumerate(v.full_g)
    ]
    v.take("b")
    v.take("g")
    v.ring_bg = ring_bg
    slots_in = [v.own_in, tp(v.own_in, 1)]
    if parts > 1:
        slots_in += [v.far_in, tp(v.far_in, 1)]
    v.take("far_in")
    resets = jnp.stack([e[16 + Lc :].reshape(-1)[:L].astype(F32) for e in slots_in])
    open_ = 1.0 - jnp.maximum(resets, (jnp.arange(L) % SEQ == 0).astype(F32))
    back1 = jnp.pad(open_, ((0, 0), (1, 0)))[:, :L]
    back2 = jnp.pad(open_, ((0, 0), (2, 0)))[:, :L]
    masks = jnp.stack([open_, open_ * back1, open_ * back1 * back2, 1.0 - open_], axis=1)
    masks = jnp.pad(masks, ((0, 0), (0, 0), (0, HALO)))
    masks = lax.dynamic_slice(masks, (0, 0, z * Lc), (t, 4, Lc + HALO))
    masks = masks.transpose(0, 2, 1)

    v.masks = masks
    v.own_in = v.own_in[16 : 16 + Lc]
    v.groups_in = jnp.concatenate([e[16 : 16 + Lc] for e in slots_in])
    v.ahead_in = jnp.concatenate([e[:16] for e in slots_in])
    v.scale_in = normed(v.groups_in, None)[1]
    v.y_a = y_next
    v.barrier()

    def fill_gate(k, own=None, others=None):
        for n in range(2):
            rows = slice(n * fz, (n + 1) * fz)
            if own is not None:
                v.full_g[n] = fill_own(v.full_g[n], own[rows], k)
            if others is not None:
                v.full_g[n] = fill_far(v.full_g[n], [y[rows] for y in others], k)

    b_1, g_1 = v.take("ring_bg").parts()
    d_0 = from_group(v.take("d"))
    v.full_d = fill_own(v.full_d, d_0, 0)
    v.y_1 = to_groups(b_1, g_1, d_0)
    v.ring = ring_next(b_1, g_1, d_0)
    v.full_b = fill_own(v.full_b, b_1, 1)
    fill_gate(1, own=g_1)
    for k, others in enumerate(by_block(v.take("y_a")), 1):
        v.full_a = fill_mixer_far(v.full_a, others, k)
    w_in_t, w_br_t, rest = v.take("full_a")
    rest = rest.reshape(M, gate_rows, DP, Dl).transpose(0, 2, 1, 3)
    rest = rest.reshape(M, DP, gate_rows * Dl)
    gates = rest[:, :, :gate_size].reshape(M, DP, 2, hpg, bw_here, bw)
    gates = gates.transpose(2, 0, 3, 1, 4, 5).reshape(2, nh, bw, bw)
    dense = []
    for kind in range(2):
        rows = [
            jnp.pad(gates[kind, n], ((0, 0), (n * bw, (nh - 1 - n) * bw)))
            for n in range(nh)
        ]
        dense.append(jnp.concatenate(rows))
    wa, wx = dense
    v.w_in_t, v.w_br_t, v.wa, v.wx = w_in_t, w_br_t, wa, wx
    every = rest[:, :, gate_size : gate_size + packed.shape[0]].astype(F32)
    gains = jnp.stack([pick(every[:, :, : 2 * ng], (z - b) % M) for b in range(M)])
    gain_one = gains[:, :, :ng].reshape(1, D)
    gain_two = gains[:, :, ng:].reshape(1, D)
    vectors = every[:, :, 2 * ng :].reshape(M, DP, conv + 4, nc).transpose(2, 0, 1, 3)
    vectors = pick(vectors.reshape(conv + 4, M, t, cz), q, 2).reshape(conv + 4, C)
    conv_w = vectors[:conv]
    decay = vectors[conv + 3]
    log_slope = -8.0 * jax.nn.softplus(decay)
    vec = jnp.stack(
        [vectors[conv], vectors[conv + 1], vectors[conv + 2], log_slope]
        + [jnp.zeros_like(decay)] * 4
    )

    v.vec, v.conv_w, v.gain_one, v.gain_two = vec, conv_w, gain_one, gain_two
    v.n1 = (v.take("groups_in").astype(F32) * v.take("scale_in") * v.gain_one).astype(BF)
    ahead = (normed(v.take("ahead_in"), None)[0] * v.gain_one).astype(BF)

    def mixed_sum(*pairs):
        return products(
            NN, [list(pairs)], [], [BF], lambda total: (total,), "product", halves=True
        )

    def chain(ends, sign):
        total = jnp.zeros_like(ends[..., 4:5, :])
        for k in reversed(range(1, M)):
            got = zline(ends, sign * k)
            total = got[..., 4:5, :] + got[..., 0:1, :] * total
        return total

    shape = (t, Lc, C)
    v.rnn = dot_nt(v.n1, v.w_in_t).reshape(shape)
    v.gin = dot_nt(v.n1, v.w_br_t).reshape(shape)
    v.halos = dot_nt(ahead, v.w_in_t).reshape(t, 16, C)[:, 16 - HALO :]
    v.barrier()

    b_next, g_next, v.d = v.take("ring").parts()
    v.b, v.g = [b_next], [g_next]
    v.y_2 = to_groups(b_next, g_next)
    while len(v.b) < M - 2:
        b_next, g_next = ring_next(b_next, g_next).parts()
        v.b, v.g = v.b + [b_next], v.g + [g_next]
    v.fwd = seq_call(
        forward_kernel,
        [v.rnn, v.halos, v.masks],
        [v.conv_w, v.vec, v.wa, v.wx],
        [(shape, F32, True)] * 5 + [((t, 8, C), F32, True)],
        [pltpu.VMEM((Lc + HALO, C), F32)],
        "recurrence",
        40,
    )
    v.barrier()

    y_next = to_groups(*v.b[1:])
    y_b, y_g, y_d = by_block(v.take("y_1"))
    v.full_b = fill_far(v.full_b, y_b, 1)
    fill_gate(1, others=y_g)
    v.full_d = fill_far(v.full_d, y_d, 0)
    y_b, y_g = by_block(v.take("y_2"))
    v.full_b = fill_far(v.full_b, y_b, 2)
    fill_gate(2, others=y_g)
    for k, mine in enumerate(v.take("b"), 2):
        v.full_b = fill_own(v.full_b, mine, k)
    for k, mine in enumerate(v.g, 2):
        fill_gate(k, own=mine)
    v.full_d = fill_own(v.full_d, v.d, 1)
    v.cin = chain(v.fwd[5], 1)
    v.state = v.fwd[3] + v.fwd[4] * v.cin
    v.mixer = (gelu_parts(v.gin)[0] * v.state).astype(BF).reshape(t * Lc, C)
    v.fwd = v.fwd[:3]
    v.y_b = y_next
    v.barrier()

    for k, others in enumerate(by_block(v.take("y_b")), 3):
        v.full_b = fill_far(v.full_b, others, k)
    v.w_out = v.take("full_b")
    v.y_g = to_groups(*v.take("g")[1:], v.d)
    v.d = [v.d]
    while len(v.d) < M - 3:
        v.d = v.d + ring_next(v.d[-1]).parts()
    v.z_cot = chunk_pieces(v.cotangent, rider=folded(v.d[-1]), which=(0, 1, M - 1))
    rec_sum = None
    for p in reversed(range(parts)):
        part = send_sum(mixed_sum(((v.mixer, p, parts), v.w_out)), p)
        rec_sum = part if rec_sum is None else rec_sum + part
    v.resid_mid = v.own_in.astype(F32) + rec_sum
    v.unit_two, v.scale_two = normed(v.resid_mid, v.gain_two)
    v.n2_own = (v.unit_two * v.gain_two).astype(BF)
    v.barrier()

    got = by_block(v.take("y_g"))
    for k, others in enumerate(got[:-1], 3):
        fill_gate(k, others=others)
    v.full_d = fill_far(v.full_d, got[-1], 1)
    v.w_gate_t, v.w_up_t = v.take("full_g")
    v.d = v.d + [unfolded(v.z_cot[1][Lc:])]
    v.z_cot[1] = v.z_cot[1][:Lc]
    for k, mine in enumerate(v.d[1:], 2):
        v.full_d = fill_own(v.full_d, mine, k)
    v.d_last = ring_next(v.d[-1])
    v.z_cot = {
        **v.z_cot, **chunk_pieces(v.take("cotangent"), which=range(2, M - 1))
    }
    v.n2_far = far(v.n2_own)
    v.n2 = [jnp.concatenate([v.n2_own, tp(v.n2_own, 1)])]
    v.take("n2_own")

    def mlp_forward(p):
        return products(
            NT,
            [[(v.n2[p], v.w_gate_t)], [(v.n2[p], v.w_up_t)]],
            [],
            [F32, F32, BF],
            lambda gate, up: (gate, up, gelu_parts(gate)[0] * up),
            "mlp",
        )

    v.mlp = [mlp_forward(0)]
    v.barrier()

    v.d = v.d[1:] + v.take("d_last").parts()
    v.y_d = to_groups(*v.d)
    cot_own = joined(v.take("z_cot"))
    v.cot = [jnp.concatenate([cot_own, tp(cot_own, 1)])]
    v.far_cot = far(cot_own)
    if parts > 1:
        v.n2.append(jnp.concatenate([v.n2_far, tp(v.n2_far, 1)]))
        v.mlp.append(mlp_forward(1))
    v.take("n2_far")
    v.barrier()

    def summed(lefts, rights, groups=None):
        groups = range(O) if groups is None else groups
        out = [
            products(
                TN,
                [list(zip(lefts, rights))],
                [],
                [BF],
                lambda total: (total,),
                "gradient",
                base=((o + r) % O) * half,
                width=half,
            )[0]
            for r in reversed(groups)
        ]
        return out[::-1]

    v.full_d = fill_own(v.full_d, v.take("d")[-1], M - 1)
    for k, others in enumerate(by_block(v.take("y_d")), 2):
        v.full_d = fill_far(v.full_d, others, k)
    v.w_dn = v.take("full_d")
    if parts > 1:
        v.cot.append(jnp.concatenate([v.far_cot, tp(v.far_cot, 1)]))
    v.take("far_cot")

    def mlp_back(p):
        def finish(d_hidden, gate, up):
            gelu, slope = gelu_parts(gate)
            return d_hidden * up * slope, d_hidden * gelu

        return products(
            NT, [[(v.cot[p], v.w_dn)]], list(v.mlp[p][:2]), [BF, BF], finish, "mlp_back"
        )

    def mlp_back_in(p):
        gate, up = v.d_mlp[p]
        return mixed_sum((gate, v.w_gate_t), (up, v.w_up_t))

    out_sum = None
    for p in reversed(range(parts)):
        part = send_sum(mixed_sum((v.mlp[p][2], v.w_dn)), p)
        out_sum = part if out_sum is None else out_sum + part
    v.output = (v.take("resid_mid") + out_sum).astype(BF)
    v.grad_down = summed([m[2] for m in v.mlp], v.cot, range(1, O))
    v.d_mlp = [None] * parts
    v.d_mlp[last] = mlp_back(last)
    v.barrier()

    v.y_down = to_groups_of([[None] + v.take("grad_down")])
    v.hidden = [m[2] for m in v.mlp]
    pieces = back_pieces(v.take("output"))
    v.z_out = [zshift(piece, k) if k else piece for k, piece in enumerate(pieces)]
    v.dn2 = [None] * parts
    v.dn2[last] = mlp_back_in(last)
    v.dn2_sum = send_sum(v.dn2[last], last) if last else None
    for p in range(last):
        v.d_mlp[p] = mlp_back(p)
        v.dn2[p] = mlp_back_in(p)
    v.grad_gate = summed([d[0] for d in v.d_mlp], v.n2, range(1, O))
    v.take("mlp")
    v.cot_own = v.cot[0][:Lc]
    v.barrier()

    own = summed(v.take("hidden"), v.take("cot"), range(1))
    (v.y_down,) = y_parts((own, v.y_down))
    v.output = back_joined(v.take("z_out"))
    v.ring = ring_step((v.y_down, 1, None))
    v.y_gate = to_groups_of([[None] + v.take("grad_gate")])
    dn2_sum = v.take("dn2_sum")
    for p in reversed(range(last if last else 1)):
        part = send_sum(v.dn2[p], p)
        dn2_sum = part if dn2_sum is None else dn2_sum + part
    v.take("dn2")

    def norm_back(grad, unit, scale, gain):
        weighted = grad * gain
        dots = jnp.mean(weighted * unit, axis=1, keepdims=True)
        return scale * (weighted - unit * dots), jnp.sum(grad * unit, axis=0)

    back_two, v.gain_two_grad = norm_back(dn2_sum, v.unit_two, v.scale_two, v.gain_two)
    v.d_mid = v.take("cot_own").astype(F32) + back_two
    v.d_own = v.d_mid.astype(BF)
    v.far_branch = far(v.d_own)
    v.near_branch = tp(v.d_own, 1)
    v.grad_up = summed([d[1] for d in v.d_mlp], v.n2)
    v.gate_own = summed([d[0] for d in v.take("d_mlp")], v.take("n2"), range(1))
    v.barrier()

    (v.y_gate,) = y_parts((v.take("gate_own"), v.y_gate))
    (r_down,) = v.ring.parts()
    v.ring = ring_step((v.y_down, 2, r_down), (v.y_gate, 1, None))
    v.y_up = grad_y(v.take("grad_up"))
    slots_of = [v.take("d_own"), v.take("near_branch")]
    if parts > 1:
        slots_of += [v.far_branch, tp(v.far_branch, 1)]
    v.take("far_branch")
    v.d_branch = jnp.concatenate(slots_of)
    v.adjoint = seq_call(
        adjoint_kernel,
        [
            dot_nt(v.d_branch, v.w_out).reshape(shape),
            v.take("gin"),
            v.state,
            v.fwd[1],
            v.masks,
        ],
        [v.vec],
        [(shape, F32, True)] * 2 + [(shape, BF, True), ((t, 8, C), F32, True)],
        [],
        "adjoint",
        24,
    )
    v.d_gin = v.adjoint[2].reshape(t * Lc, C)
    v.grad_branch = summed([v.d_gin], [v.n1])
    v.barrier()

    (v.y_up,) = y_parts(v.y_up)
    v.edges = jnp.concatenate(
        [
            jnp.broadcast_to(v.take("cin"), (t, 4, C)),
            jnp.broadcast_to(chain(v.adjoint[3], -1), (t, 4, C)),
        ],
        1,
    )
    v.grad_output = summed([v.take("mixer")], [v.take("d_branch")])
    v.barrier()

    r_down, r_gate = v.ring.parts()
    v.ring = ring_step((v.y_down, 3, r_down), (v.y_gate, 2, r_gate), (v.y_up, 1, None))
    v.y_mixer = grad_y(v.take("grad_output"), v.take("grad_branch"))
    mixed, gate_a, gate_x = v.fwd
    lam, prod, _, _ = v.adjoint

    def run_back(rows, time):
        tokens = [lam, prod, v.state, gate_a, gate_x, mixed, v.rnn]
        if rows < Lc:
            tokens = [array[:, :rows] for array in tokens]
        return seq_call(
            backward_kernel,
            tokens + [v.halos, v.masks[:, : rows + HALO], v.edges],
            [v.conv_w, v.vec, v.wa, v.wx],
            [
                ((t, rows, C), BF, True),
                ((t, HALO, C), F32, True),
                ((t, HALO, C), F32, True),
                ((C, C), F32, False),
                ((C, C), F32, False),
                ((8, 8, C), F32, False),
            ],
            [pltpu.VMEM((rows + HALO, C), F32)] * 3,
            "recurrence_back",
            time,
        )

    v.following = zline(run_back(2 * HALO, 4)[1], -1)
    v.d_rnn, _, v.tails, v.grad_wa, v.grad_wx, v.grad_vec = run_back(Lc, 40)
    for name in ("adjoint", "fwd", "state", "rnn", "halos", "edges"):
        v.take(name)
    v.barrier()

    following = v.take("following")
    fix = [jnp.zeros((t, 1, C), F32)] * HALO
    for k in range(1, 4):
        for n in range(k):
            row = HALO - k + n
            fix[row] = fix[row] + v.conv_w[k] * (
                v.masks[:, Lc + n : Lc + n + 1, k - 1 : k] * following[:, n : n + 1]
            )
    tail = (v.take("tails") + jnp.concatenate(fix, axis=1)).astype(BF)
    v.d_rnn = put(v.d_rnn, tail, 0, Lc - HALO, 0).reshape(t * Lc, C)
    v.r_down, r_gate, r_up = v.take("ring").parts()
    y_output, y_branch = y_parts(v.take("y_mixer"))
    rings = ring_sends((v.y_gate, 3, r_gate), (v.y_up, 2, r_up))

    def direct(rings, *grads):
        got = []
        for k, send in enumerate(direct_sends(*grads)):
            send = send + rings if k == M - 1 else send
            got.append(joint(lambda b: zshift(b, M - k) if k else b, send))
        return got

    v.z_mixer = direct(rings, y_output, y_branch)
    v.y_in = grad_y(summed([v.d_rnn], [v.n1]))
    v.take("n1")
    v.dn1 = [
        mixed_sum(((v.d_rnn, p, parts), v.w_in_t), ((v.d_gin, p, parts), v.w_br_t))
        for p in range(parts)
    ]
    for name in ("d_rnn", "d_gin", "w_in_t", "w_br_t", "wa", "wx", "masks", "vec"):
        v.take(name)
    v.barrier()

    gates_grad = jnp.stack(
        [
            jnp.stack(
                [g[n * bw : (n + 1) * bw, n * bw : (n + 1) * bw] for n in range(nh)]
            )
            for g in (v.take("grad_wa"), v.take("grad_wx"))
        ]
    )
    gates_grad = gates_grad.reshape(2, M, hpg, DP, bw_here, bw)
    gates_grad = gates_grad.transpose(1, 3, 0, 2, 4, 5).reshape(M, DP, gate_size)
    small = jnp.sum(v.take("grad_vec"), axis=1).reshape(2 * conv, M, O, nc)
    small = small.transpose(1, 2, 0, 3).reshape(M, O, 2 * conv * nc)
    small = put(jnp.zeros((M, DP, 2 * conv * nc), F32), small, 0, q * O, 0)
    gain_two_grad = v.take("gain_two_grad").reshape(M, DP, ng)
    gain_two_grad = jnp.stack([pick(gain_two_grad, (z - k) % M) for k in range(M)])
    gates_grad = jnp.concatenate([gates_grad, small, gain_two_grad], axis=2)
    gates_grad = jnp.pad(
        gates_grad, ((0, 0), (0, 0), (0, gate_rows * Dl - gates_grad.shape[2]))
    )
    gates_grad = gates_grad.reshape(M, DP, gate_rows, Dl).transpose(0, 2, 1, 3)
    gates_grad = gates_grad.reshape(M * gate_rows, D).astype(BF)
    gates_grad = [cut(gates_grad, (o + r) % O, half, 1) for r in range(O)]
    v.y_gates = grad_y(gates_grad)
    v.z_down = ring_end(v.take("y_down"), v.take("r_down"))
    r_gate, r_up = v.z_mixer[M - 1].parts()[2:]
    v.z_gate = ring_end(v.take("y_gate"), r_gate)
    v.z_in = direct(ring_sends((v.y_up, 3, r_up)), *y_parts(v.take("y_in")))
    dn1_sum = None
    for p in reversed(range(parts)):
        part = send_sum(v.dn1[p], p)
        dn1_sum = part if dn1_sum is None else dn1_sum + part
    v.dn1 = dn1_sum
    v.barrier()

    def added(pieces, count=1):
        return [
            sum(p.astype(F32) for p in same).astype(BF)
            for same in zip(*(p.parts()[:count] for p in pieces))
        ]

    r_up = v.z_in[M - 1].parts()[1]

    z_output, z_branch = added(v.take("z_mixer"), 2)
    (z_in,) = added(v.take("z_in"))
    z_up = ring_end(v.take("y_up"), r_up)
    totals = exchange_grads(
        v.take("z_down"), v.take("z_gate"), z_up, z_output, z_branch, z_in
    )
    unit_one, scale_one = normed(v.own_in, v.gain_one)
    back_one, gain_one_grad = norm_back(v.take("dn1"), unit_one, scale_one, v.gain_one)
    pieces = back_pieces((v.d_mid + back_one).astype(BF))
    sums = jnp.broadcast_to(gain_one_grad.astype(BF), (16, D))
    joints = []
    sends = direct_sends(*y_parts(v.take("y_gates")))
    for k, piece in enumerate(pieces):
        gates_send = folded(sends[(M - k) % M][0])
        joint = jnp.concatenate([piece, cut(sums, (z + k) % M, FH, 1), gates_send])
        joints.append(zshift(joint, k) if k else joint)
    v.joints = joints
    v.grads = [grad_end(total) for total in by_grad(totals)]
    v.barrier()

    grad_down, grad_gate, grad_up, grad_output, grad_branch, grad_in = v.grads
    input_grad = back_joined([joint[:Lc] for joint in v.joints]).astype(F32)
    gates_sum = unfolded(sum(joint[Lc + 16 :].astype(F32) for joint in v.joints))
    gates_sum = gates_sum.astype(BF)
    last_rows = exchange(lambda k: cut(gates_sum, k, Dl, 1))
    gain_one_grad = sum(joint[Lc].astype(F32) for joint in v.joints)
    step = 1
    while step < DP:
        gain_one_grad = gain_one_grad + tp(gain_one_grad, step)
        step *= 2
    gain_one_grad = cut(gain_one_grad, i_dp, ng, 0)
    output = v.output

    rest_in = jnp.stack([piece.reshape(-1) for piece in last_rows])
    small = jnp.sum(rest_in[:, gate_size:].astype(F32), axis=0)
    rest_in = jnp.stack([pick(rest_in, q ^ k) for k in range(t)])
    mine = small[: 2 * conv * nc].reshape(2 * conv, nc)
    gain_two_grad = small[2 * conv * nc : 2 * conv * nc + ng]
    decay_grad = mine[conv + 3] * (-8.0 * jax.nn.sigmoid(decay_param.astype(F32)))

    gates_back = rest_in[:, :gate_size].reshape(t, 2, hpg, bw_here, bw)
    gates_back = gates_back.transpose(1, 0, 2, 3, 4)
    gates_back = gates_back.reshape(2, heads_here, bw_here, bw).astype(F32)

    def flipped(value):
        return lax.optimization_barrier(value).T.astype(F32)

    return (
        output,
        input_grad,
        gain_one_grad,
        flipped(grad_in),
        flipped(grad_branch),
        grad_output.astype(F32),
        mine[:conv],
        mine[conv],
        gates_back[0],
        mine[conv + 1],
        gates_back[1],
        mine[conv + 2],
        decay_grad,
        gain_two_grad,
        flipped(grad_gate),
        flipped(grad_up),
        grad_down.astype(F32),
    )


def solution(mesh):
    both = P(("mp", "dp"))
    wide = P("dp", "mp")
    tall = P("mp", "dp")
    taps = P(None, ("mp", "dp"))
    gate = P("mp", "dp", None)
    params = (both, wide, wide, tall, taps, both, gate, both, gate, both, both, both, wide, wide, tall)
    return jax.shard_map(
        functools.partial(body, mesh.shape["dp"], mesh.shape["mp"]),
        mesh=mesh,
        in_specs=(wide, wide, P("dp")) + params,
        out_specs=(wide, wide) + params,
        check_vma=False,
    )
```

```python
import functools

import jax
import jax.numpy as jnp
from jax import lax
from jax.experimental import pallas as pl
from jax.experimental.pallas import tpu as pltpu
from jax.sharding import PartitionSpec as P

SEQ = 2048
epsilon = 1e-06
BF = jnp.bfloat16
F32 = jnp.float32
HALO = 8


def dot_nt(left, right):
    return lax.dot_general(
        left, right, (((1,), (1,)), ((), ())), preferred_element_type=F32
    )


def dot_nn(left, right):
    return jnp.dot(left, right, preferred_element_type=F32)


def dot_tn(left, right):
    return lax.dot_general(
        left, right, (((0,), (0,)), ((), ())), preferred_element_type=F32
    )


def gelu_parts(value):
    inner = 0.7978845608028654 * (value + 0.044715 * value * value * value)
    tanh = jnp.tanh(inner)
    slope = 0.7978845608028654 * (1.0 + 3.0 * 0.044715 * value * value)
    gelu = 0.5 * value * (1.0 + tanh)
    grad = 0.5 * (1.0 + tanh) + 0.5 * value * (1.0 - tanh * tanh) * slope
    return gelu, grad


def sigmoid(value):
    return 1.0 / (1.0 + jnp.exp(-value))


def one_minus_exp(log_value):
    y = -2.0 * log_value
    series = y * (
        1.0
        - y
        * (1 / 2)
        * (
            1.0
            - y
            * (1 / 3)
            * (1.0 - y * (1 / 4) * (1.0 - y * (1 / 5) * (1.0 - y * (1 / 6))))
        )
    )
    return jnp.where(y < 0.25, series, 1.0 - jnp.exp(-y))


def conv_terms(ext, masks, rows):
    terms = [ext[HALO : HALO + rows]]
    for k in range(1, 4):
        moved = pltpu.roll(ext, k, axis=0)[HALO : HALO + rows]
        terms.append(moved * masks[:, k - 1 : k])
    return terms


def forward_kernel(
    rnn_ref,
    halo_ref,
    mask_ref,
    conv_ref,
    vec_ref,
    wa_ref,
    wx_ref,
    mixed_ref,
    ga_ref,
    gx_ref,
    h_ref,
    p_ref,
    end_ref,
    ext_ref,
):
    length, width = rnn_ref.shape[1:]
    block_rows = min(256, length)
    ext_ref[0:HALO, :] = halo_ref[0]
    ext_ref[HALO:, :] = rnn_ref[0]
    row8 = lax.broadcasted_iota(jnp.int32, (block_rows, 1), 0) % 8

    def block(i, carry):
        h_in, p_in = carry
        r0 = pl.multiple_of(i * block_rows, block_rows)
        masks = mask_ref[0, pl.ds(r0, block_rows), :]
        terms = conv_terms(ext_ref[pl.ds(r0, block_rows + HALO), :], masks, block_rows)
        mixed = vec_ref[0:1, :] + conv_ref[0:1, :] * terms[0]
        for k in range(1, 4):
            mixed = mixed + conv_ref[k : k + 1, :] * terms[k]
        high = mixed.astype(BF)
        low = (mixed - high.astype(F32)).astype(BF)
        gate_a = sigmoid(
            dot_nn(high, wa_ref[...]) + dot_nn(low, wa_ref[...]) + vec_ref[1:2, :]
        )
        gate_x = sigmoid(
            dot_nn(high, wx_ref[...]) + dot_nn(low, wx_ref[...]) + vec_ref[2:3, :]
        )
        begins = masks[:, 3:4]
        log_a = gate_a * vec_ref[3:4, :]
        a = jnp.exp(log_a) * (1.0 - begins)
        scale = jnp.sqrt(one_minus_exp(log_a)) * (1.0 - begins) + begins
        b = mixed * gate_x * scale
        mixed_ref[0, pl.ds(r0, block_rows), :] = mixed
        ga_ref[0, pl.ds(r0, block_rows), :] = gate_a
        gx_ref[0, pl.ds(r0, block_rows), :] = gate_x
        for d in (1, 2, 4):
            valid = row8 >= d
            b = jnp.where(valid, a * pltpu.roll(b, d, axis=0) + b, b)
            a = jnp.where(valid, a * pltpu.roll(a, d, axis=0), a)
        for g in range(block_rows // 8):
            rows = slice(8 * g, 8 * g + 8)
            h = b[rows] + a[rows] * h_in
            p = a[rows] * p_in
            h_ref[0, pl.ds(r0 + 8 * g, 8), :] = h
            p_ref[0, pl.ds(r0 + 8 * g, 8), :] = p
            h_in = h[7:8]
            p_in = p[7:8]
        return h_in, p_in

    h_end, p_end = lax.fori_loop(
        0,
        length // block_rows,
        block,
        (jnp.zeros((1, width), F32), jnp.ones((1, width), F32)),
    )
    end_ref[0, 0:4, :] = jnp.broadcast_to(p_end, (4, width))
    end_ref[0, 4:8, :] = jnp.broadcast_to(h_end, (4, width))


def adjoint_kernel(
    dmix_ref,
    gate_ref,
    state_ref,
    ga_ref,
    mask_ref,
    vec_ref,
    lam_ref,
    q_ref,
    dgi_ref,
    end_ref,
):
    length, width = dmix_ref.shape[1:]
    block_rows = min(64, length)
    row = lax.broadcasted_iota(jnp.int32, (block_rows, 1), 0)
    row8 = row % 8
    blocks = length // block_rows

    def block(i, carry):
        lam_in, q_in, a_next = carry
        r0 = pl.multiple_of((blocks - 1 - i) * block_rows, block_rows)
        here = pl.ds(r0, block_rows)
        begins = mask_ref[0, here, :][:, 3:4]
        d_mixer = dmix_ref[0, here, :]
        gelu, slope = gelu_parts(gate_ref[0, here, :])
        dgi_ref[0, here, :] = (d_mixer * state_ref[0, here, :] * slope).astype(BF)
        b = d_mixer * gelu
        a = jnp.exp(ga_ref[0, here, :] * vec_ref[3:4, :]) * (1.0 - begins)
        c = jnp.where(row == block_rows - 1, a_next, pltpu.roll(a, block_rows - 1, axis=0))
        for d in (1, 2, 4):
            valid = row8 < 8 - d
            b = jnp.where(valid, c * pltpu.roll(b, block_rows - d, axis=0) + b, b)
            c = jnp.where(valid, c * pltpu.roll(c, block_rows - d, axis=0), c)
        for g in reversed(range(block_rows // 8)):
            rows = slice(8 * g, 8 * g + 8)
            lam = b[rows] + c[rows] * lam_in
            q = c[rows] * q_in
            lam_ref[0, pl.ds(r0 + 8 * g, 8), :] = lam
            q_ref[0, pl.ds(r0 + 8 * g, 8), :] = q
            lam_in = lam[0:1]
            q_in = q[0:1]
        return lam_in, q_in, a[0:1]

    one = jnp.ones((1, width), F32)
    lam0, q0, a0 = lax.fori_loop(
        0, blocks, block, (jnp.zeros((1, width), F32), one, one)
    )
    end_ref[0, 0:4, :] = jnp.broadcast_to(a0 * q0, (4, width))
    end_ref[0, 4:8, :] = jnp.broadcast_to(a0 * lam0, (4, width))


def fold8(value):
    total = value[0:8]
    for g in range(1, value.shape[0] // 8):
        total = total + value[8 * g : 8 * g + 8]
    return total


def backward_kernel(
    lam_ref,
    q_ref,
    state_ref,
    ga_ref,
    gx_ref,
    mixed_ref,
    rnn_ref,
    halo_ref,
    mask_ref,
    edge_ref,
    conv_ref,
    vec_ref,
    wa_ref,
    wx_ref,
    drnn_ref,
    head_ref,
    tail_ref,
    wag_ref,
    wxg_ref,
    vg_ref,
    ext_ref,
    prev_ref,
    dm_ref,
):
    length, width = lam_ref.shape[1:]
    block_rows = min(512, length)
    first = pl.program_id(0) == 0

    @pl.when(first)
    def _():
        wag_ref[...] = jnp.zeros_like(wag_ref)
        wxg_ref[...] = jnp.zeros_like(wxg_ref)
        vg_ref[...] = jnp.zeros_like(vg_ref)

    ext_ref[0:HALO, :] = halo_ref[0]
    ext_ref[HALO:, :] = rnn_ref[0]
    prev_ref[0:HALO, :] = jnp.broadcast_to(edge_ref[0, 0:1, :], (HALO, width))
    prev_ref[HALO:, :] = state_ref[0]
    dm_ref[length:, :] = jnp.zeros((HALO, width), F32)

    def block(i, carry):
        r0 = pl.multiple_of(i * block_rows, block_rows)
        here = pl.ds(r0, block_rows)
        masks = mask_ref[0, here, :]
        begins = masks[:, 3:4]
        lam = lam_ref[0, here, :] + q_ref[0, here, :] * edge_ref[0, 4:5, :]
        before = pltpu.roll(prev_ref[pl.ds(r0, block_rows + HALO), :], 1, axis=0)[
            HALO : HALO + block_rows
        ]
        gate_a = ga_ref[0, here, :]
        gate_x = gx_ref[0, here, :]
        mixed = mixed_ref[0, here, :]
        log_a = gate_a * vec_ref[3:4, :]
        decay = jnp.exp(log_a)
        inv_scale = lax.rsqrt(one_minus_exp(log_a))
        scale_raw = jnp.sqrt(one_minus_exp(log_a))
        keep = 1.0 - begins
        scale = scale_raw * keep + begins
        through = lam * mixed
        d_log = lam * before * decay * keep + jnp.where(
            begins > 0.5, 0.0, through * gate_x * (-(decay * decay) * inv_scale)
        )
        log_gate = d_log * gate_a
        d_pre_a = log_gate * (1.0 - gate_a) * vec_ref[3:4, :]
        d_pre_x = through * scale * gate_x * (1.0 - gate_x)
        pa = d_pre_a.astype(BF)
        px = d_pre_x.astype(BF)
        mb = mixed.astype(BF)
        d_mixed = (
            lam * gate_x * scale + dot_nt(pa, wa_ref[...]) + dot_nt(px, wx_ref[...])
        )
        dm_ref[here, :] = d_mixed
        wag_ref[...] += dot_tn(mb, pa)
        wxg_ref[...] += dot_tn(mb, px)
        terms = conv_terms(ext_ref[pl.ds(r0, block_rows + HALO), :], masks, block_rows)
        sums = [d_mixed * term for term in terms]
        sums += [d_mixed, d_pre_a, d_pre_x, log_gate]
        for n, value in enumerate(sums):
            vg_ref[n] += fold8(value)
        return carry

    lax.fori_loop(0, length // block_rows, block, 0)

    def shift(i, carry):
        r0 = pl.multiple_of(i * block_rows, block_rows)
        ext = dm_ref[pl.ds(r0, block_rows + HALO), :]
        masks = mask_ref[0, pl.ds(r0, block_rows + HALO), :]
        total = conv_ref[0:1, :] * ext[0:block_rows]
        for k in range(1, 4):
            moved = pltpu.roll(ext * masks[:, k - 1 : k], block_rows + HALO - k, axis=0)
            total = total + conv_ref[k : k + 1, :] * moved[0:block_rows]
        drnn_ref[0, pl.ds(r0, block_rows), :] = total.astype(BF)

        @pl.when(i == length // block_rows - 1)
        def _():
            tail_ref[0] = total[block_rows - HALO :]

        return carry

    lax.fori_loop(0, length // block_rows, shift, 0)
    head_ref[0] = dm_ref[0:HALO, :]


def block_specs(shapes):
    specs = []
    for shape, moving in shapes:
        if moving:
            specs.append(
                pl.BlockSpec((1,) + shape[1:], lambda i, n=len(shape): (i,) + (0,) * (n - 1))
            )
        else:
            specs.append(pl.BlockSpec(shape, lambda i, n=len(shape): (0,) * n))
    return specs


def cost(time):
    return pl.CostEstimate(flops=int(time * 1.0e8), bytes_accessed=0, transcendentals=0)


NT = (((1,), (1,)), ((), ()))
NN = (((1,), (0,)), ((), ()))
TN = (((0,), (0,)), ((), ()))


def seq_call(kernel, moving, fixed, outs, scratch, name, time):
    count = moving[0].shape[0]
    return pl.pallas_call(
        kernel,
        grid=(count,),
        in_specs=block_specs(
            [(a.shape, True) for a in moving] + [(a.shape, False) for a in fixed]
        ),
        out_specs=block_specs([(shape, move) for shape, _, move in outs]),
        out_shape=[jax.ShapeDtypeStruct(shape, dtype) for shape, dtype, _ in outs],
        scratch_shapes=scratch,
        compiler_params=pltpu.CompilerParams(
            dimension_semantics=("arbitrary",), vmem_limit_bytes=60 * 1024 * 1024
        ),
        cost_estimate=cost(time),
        name=name,
    )(*moving, *fixed)


def products(dims, sums, extras, outs, finish, name, base=None, width=None, halves=False):
    full = sums[0][0][1].shape[0 if dims == NT else 1]
    width = width or full
    columns = min(256, width)
    lefts, rights, where = [], [], []
    for pairs in sums:
        places = []
        for left, right in pairs:
            left = left if isinstance(left, tuple) else (left, 0, 1)
            known = [n for n, other in enumerate(lefts) if other[0] is left[0]]
            places.append(known[0] if known else len(lefts))
            if not known:
                lefts.append(left)
            rights.append(right)
        where.append(places)
    array, _, count = lefts[0]
    rows = array.shape[1] if dims == TN else array.shape[0] // count
    cuts = 2 if halves else 1
    near = len(lefts) + len(rights)

    def kernel(_, *refs):
        at, totals = len(lefts), []
        for places in where:
            total = None
            for place in places:
                term = lax.dot_general(
                    refs[place][...], refs[at][...], dims, preferred_element_type=F32
                )
                total = term if total is None else total + term
                at += 1
            totals.append(total)
        values = finish(*totals, *(ref[...] for ref in refs[near : near + len(extras)]))
        size = rows // cuts
        at = near + len(extras)
        for value in values:
            for n in range(cuts):
                refs[at][...] = value[n * size : (n + 1) * size].astype(refs[at].dtype)
                at += 1

    def whole(left):
        array, part, count = left
        shape = (array.shape[0] // count, array.shape[1])
        return pl.BlockSpec(shape, lambda j, b: (part, 0))

    def moving(array):
        if dims == NT:
            return pl.BlockSpec((columns, array.shape[1]), lambda j, b: (b[0] + j, 0))
        return pl.BlockSpec((array.shape[0], columns), lambda j, b: (0, b[0] + j))

    base = jnp.zeros((1,), jnp.int32) if base is None else (base // columns).reshape(1)
    tile = pl.BlockSpec((rows, columns), lambda j, b: (0, j))
    part = pl.BlockSpec((rows // cuts, columns), lambda j, b: (0, j))
    return pl.pallas_call(
        kernel,
        grid_spec=pltpu.PrefetchScalarGridSpec(
            num_scalar_prefetch=1,
            grid=(width // columns,),
            in_specs=[whole(a) for a in lefts]
            + [moving(a) for a in rights]
            + [tile] * len(extras),
            out_specs=[part] * (len(outs) * cuts),
        ),
        out_shape=[
            jax.ShapeDtypeStruct((rows // cuts, width), dtype)
            for dtype in outs
            for _ in range(cuts)
        ],
        compiler_params=pltpu.CompilerParams(
            dimension_semantics=("arbitrary",), vmem_limit_bytes=60 * 1024 * 1024
        ),
        cost_estimate=cost(sum(a.size for a in rights) // (width and full) * width * rows / 3.4e8),
        name=name,
    )(base, *(left[0] for left in lefts), *rights, *extras)


@jax.tree_util.register_pytree_node_class
class Joint:
    def __init__(self, rows, sizes):
        self.rows, self.sizes = rows, sizes

    def tree_flatten(self):
        return (self.rows,), self.sizes

    @classmethod
    def tree_unflatten(cls, sizes, children):
        return cls(children[0], sizes)

    def parts(self):
        at, out = 0, []
        for size in self.sizes:
            out.append(self.rows[at : at + size])
            at += size
        return out


def body(
    DP,
    M,
    inputs,
    cotangent,
    reset_mask,
    norm1_gain,
    w_input,
    w_branch,
    w_output,
    conv_weight,
    conv_bias,
    gate_a_weight,
    gate_a_bias,
    gate_x_weight,
    gate_x_bias,
    decay_param,
    norm2_gain,
    w_gate,
    w_up,
    w_down,
):
    heads_here, bw_here, bw = gate_a_weight.shape
    t = 4 if heads_here % 4 == 0 and DP % 4 == 0 else 2
    O = DP // t
    hpg = heads_here // t
    nh = M * hpg
    L, FH = inputs.shape
    D = FH * M
    Dl = w_input.shape[0]
    Lc = L // M
    half = t * Dl
    cz = w_input.shape[1] // t
    fz = w_gate.shape[1] // t
    C = M * cz
    FC = M * fz
    conv = conv_weight.shape[0]
    parts = t // 2
    last = parts - 1

    i_dp = lax.axis_index("dp")
    z = lax.axis_index("mp")
    q = i_dp % t
    o = i_dp // t

    def tp(value, j):
        return lax.ppermute(value, "dp", [(i, i ^ j) for i in range(DP)])

    def oshift(value, r):
        return lax.ppermute(
            value, "dp", [(i, ((i // t + r) % O) * t + i % t) for i in range(DP)]
        )

    def zshift(value, k):
        return lax.ppermute(value, "mp", [(i, (i + k) % M) for i in range(M)])

    def zline(value, k):
        got = lax.ppermute(
            value, "mp", [(i, i + k) for i in range(M) if 0 <= i + k < M]
        )
        return jnp.roll(got, k * cz, axis=-1)

    class Live(dict):
        __getattr__ = dict.__getitem__
        __setattr__ = dict.__setitem__

        def barrier(self):
            held = lax.optimization_barrier(dict(self))
            self.clear()
            self.update(held)

        def take(self, name):
            return self.pop(name)

    v = Live()

    def cut(array, index, size, axis):
        return lax.dynamic_slice_in_dim(array, index * size, size, axis)

    def put(array, piece, *starts):
        return lax.dynamic_update_slice(array, piece, starts)

    def pick(array, index, axis=0):
        return lax.dynamic_index_in_dim(array, index, axis, keepdims=False)

    def chunk_pieces(value, ahead=0, rider=None, which=range(M)):
        if ahead:
            value = jnp.concatenate([jnp.zeros((ahead, FH), value.dtype), value])
        pieces = [
            lax.dynamic_slice_in_dim(value, (z + k) % M * Lc, Lc + ahead, 0)
            for k in range(M)
        ]
        if rider is not None:
            pieces[1] = jnp.concatenate([pieces[1], rider])
        return {k: zshift(pieces[k], k) if k else pieces[k] for k in which}

    def joined(pieces):
        own = jnp.zeros((pieces[0].shape[0], D), pieces[0].dtype)
        for k, piece in pieces.items():
            own = put(own, piece, 0, ((z - k) % M) * FH)
        return own

    def far(value):
        return tp(value, 2) if parts > 1 else None

    def back_pieces(value):
        return [cut(value, (z + k) % M, FH, 1) for k in range(M)]

    def back_joined(pieces):
        out = jnp.zeros((L, FH), pieces[0].dtype)
        for k, piece in enumerate(pieces):
            out = put(out, piece, ((z - k) % M) * Lc, 0)
        return out

    def send_sum(part, p):
        mine = part[0].astype(F32) + tp(part[1], 1).astype(F32)
        if p:
            mine = tp(mine.astype(BF), 2).astype(F32)
        return mine

    def stacked(blocks):
        return jnp.concatenate(blocks) if len(blocks) > 1 else blocks[0]

    def joint(transfer, blocks):
        return Joint(transfer(stacked(blocks)), tuple(b.shape[0] for b in blocks))

    def exchange(mine):
        if parts == 1:
            return [mine(q), tp(mine(q ^ 1), 1)]
        got = tp(jnp.stack([mine(q ^ 1), mine(q ^ 3)]), 1)
        after = tp(jnp.stack([mine(q ^ 2), got[1]]), 2)
        return [mine(q), got[0], after[0], after[1]]

    def from_group(pieces):
        block = jnp.zeros((pieces[0].shape[0], half), BF)
        for j, piece in enumerate(pieces):
            block = put(block, piece, 0, (q ^ j) * Dl)
        return block

    def to_groups(*blocks):
        return [joint(lambda b: oshift(b, r), blocks) for r in range(1, O)]

    def by_block(got):
        return [list(same) for same in zip(*(g.parts() for g in got))]

    def ring_next(*blocks):
        return joint(lambda b: zshift(b, 1), blocks)

    def fill_own(full, block, s):
        return put(full, block, s * block.shape[0], o * half)

    def fill_far(full, others, s):
        for r, piece in enumerate(others, 1):
            full = put(full, piece, s * piece.shape[0], ((o - r) % O) * half)
        return full

    def mixer_parts(block):
        return block[:cz], block[cz : 2 * cz], block[2 * cz :]

    def fill_mixer_far(full, others, s):
        split = [mixer_parts(piece) for piece in others]
        return [fill_far(f, [g[n] for g in split], s) for n, f in enumerate(full)]

    def folded(block):
        return jnp.concatenate(
            [block[:, n * FH : (n + 1) * FH] for n in range(half // FH)]
        )

    def unfolded(rows):
        size = rows.shape[0] // (half // FH)
        return jnp.concatenate(
            [rows[n * size : (n + 1) * size] for n in range(half // FH)], axis=1
        )

    def grad_y(*grads):
        return [g[0] for g in grads], to_groups_of(grads)

    def to_groups_of(grads):
        return [joint(lambda b: oshift(b, r), [g[r] for g in grads]) for r in range(1, O)]

    def y_parts(held):
        own, got = held
        return [list(same) for same in zip(own, *(g.parts() for g in got))]

    def slot(pieces, k):
        size = pieces[0].shape[0] // M
        return sum(piece[k * size : (k + 1) * size].astype(F32) for piece in pieces)

    def ring_sends(*rings):
        sends = []
        for pieces, k, moving in rings:
            total = slot(pieces, k)
            if moving is not None:
                total = total + moving.astype(F32)
            sends.append(total.astype(BF))
        return sends

    def ring_step(*rings):
        return ring_next(*ring_sends(*rings))

    def ring_end(pieces, moving):
        for k in range(4, M):
            (moving,) = ring_step((pieces, k, moving)).parts()
        return (moving.astype(F32) + slot(pieces, 0)).astype(BF)

    def direct_sends(*grads):
        return [[slot(pieces, k).astype(BF) for pieces in grads] for k in range(M)]

    def grad_end(pieces):
        size = pieces[0].shape[0]
        out = jnp.zeros((t * size, Dl), BF)
        for j, piece in enumerate(pieces):
            out = put(out, piece, (q ^ j) * size, 0)
        return out

    def exchange_grads(*totals):
        sizes = tuple(total.shape[0] for total in totals)
        rows = stacked(totals)
        return [Joint(p, sizes) for p in exchange(lambda k: cut(rows, k, Dl, 1))]

    def by_grad(got):
        return [list(same) for same in zip(*(g.parts() for g in got))]

    ng, nc = norm1_gain.shape[0], conv_bias.shape[0]
    packed = jnp.concatenate(
        [
            norm1_gain,
            norm2_gain,
            conv_weight.reshape(-1),
            conv_bias,
            gate_a_bias,
            gate_x_bias,
            decay_param,
        ]
    )
    gate_size = 2 * hpg * bw_here * bw
    gate_rows = -(-(gate_size + packed.shape[0]) // (16 * Dl)) * 16
    gates_flat = jnp.stack([gate_a_weight, gate_x_weight]).reshape(
        2, t, hpg, bw_here, bw
    )
    gates_flat = gates_flat.transpose(1, 0, 2, 3, 4).reshape(t, gate_size)
    extra = gate_size + packed.shape[0]
    gates_flat = jnp.concatenate(
        [
            gates_flat,
            jnp.broadcast_to(packed, (t,) + packed.shape),
            jnp.zeros((t, gate_rows * Dl - extra), BF),
        ],
        axis=1,
    )
    mine_all = jnp.concatenate(
        [
            w_input.T.reshape(t, cz, Dl),
            w_branch.T.reshape(t, cz, Dl),
            gates_flat.reshape(t, gate_rows, Dl),
            w_output.reshape(t, cz, Dl),
            w_gate.T.reshape(t, fz, Dl),
            w_up.T.reshape(t, fz, Dl),
        ],
        axis=1,
    )
    def normed(value, gain):
        wide = value.astype(F32)
        scale = lax.rsqrt(jnp.mean(wide * wide, axis=1, keepdims=True) + epsilon)
        return wide * scale, scale

    rows_a = 2 * cz + gate_rows
    v.z_in = chunk_pieces(inputs, 16)
    v.blocks = exchange(lambda k: pick(mine_all, k))
    v.cotangent, v.w_down = cotangent, w_down
    v.zeros = [jnp.zeros((M * size, D), BF) for size in (cz, cz, gate_rows, cz, fz, fz, fz)]
    v.barrier()

    block = from_group(v.take("blocks"))
    block_a = block[:rows_a]
    block_b = block[rows_a : rows_a + cz]
    block_g = block[rows_a + cz :]
    v.ring_a = [block_a]
    for _ in range(1, M):
        v.ring_a.append(zshift(v.ring_a[-1], 1))
    v.b, v.g = [block_b], [block_g]
    v.y_first = to_groups(block_a, block_b, block_g)
    zeros = v.take("zeros")
    v.full_a = [fill_own(f, p, 0) for f, p in zip(zeros[:3], mixer_parts(block_a))]
    v.full_b = fill_own(zeros[3], block_b, 0)
    v.full_g = [
        fill_own(f, p, 0) for f, p in zip(zeros[4:6], (block_g[:fz], block_g[fz:]))
    ]
    v.full_d = zeros[6]
    resets = jnp.pad(reset_mask.astype(BF), (0, 16 * D - L)).reshape(16, D)
    v.own_in = jnp.concatenate([joined(v.take("z_in")), resets])
    v.far_in = far(v.own_in)
    v.barrier()

    y_next = to_groups(*v.ring_a[1:])
    ring_bg = ring_next(v.b[-1], v.g[-1])
    y_a, y_b, y_g = by_block(v.take("y_first"))
    v.d = exchange(lambda k: cut(v.w_down, k, fz, 0))
    v.take("w_down")
    v.full_a = fill_mixer_far(v.full_a, y_a, 0)
    for k, mine in enumerate(v.take("ring_a")[1:], 1):
        v.full_a = [fill_own(f, p, k) for f, p in zip(v.full_a, mixer_parts(mine))]
    v.full_b = fill_far(v.full_b, y_b, 0)
    v.full_g = [
        fill_far(f, [y[n * fz : (n + 1) * fz] for y in y_g], 0)
        for n, f in enumerate(v.full_g)
    ]
    v.take("b")
    v.take("g")
    v.ring_bg = ring_bg
    slots_in = [v.own_in, tp(v.own_in, 1)]
    if parts > 1:
        slots_in += [v.far_in, tp(v.far_in, 1)]
    v.take("far_in")
    resets = jnp.stack([e[16 + Lc :].reshape(-1)[:L].astype(F32) for e in slots_in])
    open_ = 1.0 - jnp.maximum(resets, (jnp.arange(L) % SEQ == 0).astype(F32))
    back1 = jnp.pad(open_, ((0, 0), (1, 0)))[:, :L]
    back2 = jnp.pad(open_, ((0, 0), (2, 0)))[:, :L]
    masks = jnp.stack([open_, open_ * back1, open_ * back1 * back2, 1.0 - open_], axis=1)
    masks = jnp.pad(masks, ((0, 0), (0, 0), (0, HALO)))
    masks = lax.dynamic_slice(masks, (0, 0, z * Lc), (t, 4, Lc + HALO))
    masks = masks.transpose(0, 2, 1)

    v.masks = masks
    v.own_in = v.own_in[16 : 16 + Lc]
    v.groups_in = jnp.concatenate([e[16 : 16 + Lc] for e in slots_in])
    v.ahead_in = jnp.concatenate([e[:16] for e in slots_in])
    v.scale_in = normed(v.groups_in, None)[1]
    v.y_a = y_next
    v.barrier()

    def fill_gate(k, own=None, others=None):
        for n in range(2):
            rows = slice(n * fz, (n + 1) * fz)
            if own is not None:
                v.full_g[n] = fill_own(v.full_g[n], own[rows], k)
            if others is not None:
                v.full_g[n] = fill_far(v.full_g[n], [y[rows] for y in others], k)

    b_1, g_1 = v.take("ring_bg").parts()
    d_0 = from_group(v.take("d"))
    v.full_d = fill_own(v.full_d, d_0, 0)
    v.y_1 = to_groups(b_1, g_1, d_0)
    v.ring = ring_next(b_1, g_1, d_0)
    v.full_b = fill_own(v.full_b, b_1, 1)
    fill_gate(1, own=g_1)
    for k, others in enumerate(by_block(v.take("y_a")), 1):
        v.full_a = fill_mixer_far(v.full_a, others, k)
    w_in_t, w_br_t, rest = v.take("full_a")
    rest = rest.reshape(M, gate_rows, DP, Dl).transpose(0, 2, 1, 3)
    rest = rest.reshape(M, DP, gate_rows * Dl)
    gates = rest[:, :, :gate_size].reshape(M, DP, 2, hpg, bw_here, bw)
    gates = gates.transpose(2, 0, 3, 1, 4, 5).reshape(2, nh, bw, bw)
    dense = []
    for kind in range(2):
        rows = [
            jnp.pad(gates[kind, n], ((0, 0), (n * bw, (nh - 1 - n) * bw)))
            for n in range(nh)
        ]
        dense.append(jnp.concatenate(rows))
    wa, wx = dense
    v.w_in_t, v.w_br_t, v.wa, v.wx = w_in_t, w_br_t, wa, wx
    every = rest[:, :, gate_size : gate_size + packed.shape[0]].astype(F32)
    gains = jnp.stack([pick(every[:, :, : 2 * ng], (z - b) % M) for b in range(M)])
    gain_one = gains[:, :, :ng].reshape(1, D)
    gain_two = gains[:, :, ng:].reshape(1, D)
    vectors = every[:, :, 2 * ng :].reshape(M, DP, conv + 4, nc).transpose(2, 0, 1, 3)
    vectors = pick(vectors.reshape(conv + 4, M, t, cz), q, 2).reshape(conv + 4, C)
    conv_w = vectors[:conv]
    decay = vectors[conv + 3]
    log_slope = -8.0 * jax.nn.softplus(decay)
    vec = jnp.stack(
        [vectors[conv], vectors[conv + 1], vectors[conv + 2], log_slope]
        + [jnp.zeros_like(decay)] * 4
    )

    v.vec, v.conv_w, v.gain_one, v.gain_two = vec, conv_w, gain_one, gain_two
    v.n1 = (v.take("groups_in").astype(F32) * v.take("scale_in") * v.gain_one).astype(BF)
    ahead = (normed(v.take("ahead_in"), None)[0] * v.gain_one).astype(BF)

    def mixed_sum(*pairs):
        return products(
            NN, [list(pairs)], [], [BF], lambda total: (total,), "product", halves=True
        )

    def chain(ends, sign):
        total = jnp.zeros_like(ends[..., 4:5, :])
        for k in reversed(range(1, M)):
            got = zline(ends, sign * k)
            total = got[..., 4:5, :] + got[..., 0:1, :] * total
        return total

    shape = (t, Lc, C)
    v.rnn = dot_nt(v.n1, v.w_in_t).reshape(shape)
    v.gin = dot_nt(v.n1, v.w_br_t).reshape(shape)
    v.halos = dot_nt(ahead, v.w_in_t).reshape(t, 16, C)[:, 16 - HALO :]
    v.barrier()

    b_next, g_next, v.d = v.take("ring").parts()
    v.b, v.g = [b_next], [g_next]
    v.y_2 = to_groups(b_next, g_next)
    while len(v.b) < M - 2:
        b_next, g_next = ring_next(b_next, g_next).parts()
        v.b, v.g = v.b + [b_next], v.g + [g_next]
    v.fwd = seq_call(
        forward_kernel,
        [v.rnn, v.halos, v.masks],
        [v.conv_w, v.vec, v.wa, v.wx],
        [(shape, F32, True)] * 5 + [((t, 8, C), F32, True)],
        [pltpu.VMEM((Lc + HALO, C), F32)],
        "recurrence",
        40,
    )
    v.barrier()

    y_next = to_groups(*v.b[1:])
    y_b, y_g, y_d = by_block(v.take("y_1"))
    v.full_b = fill_far(v.full_b, y_b, 1)
    fill_gate(1, others=y_g)
    v.full_d = fill_far(v.full_d, y_d, 0)
    y_b, y_g = by_block(v.take("y_2"))
    v.full_b = fill_far(v.full_b, y_b, 2)
    fill_gate(2, others=y_g)
    for k, mine in enumerate(v.take("b"), 2):
        v.full_b = fill_own(v.full_b, mine, k)
    for k, mine in enumerate(v.g, 2):
        fill_gate(k, own=mine)
    v.full_d = fill_own(v.full_d, v.d, 1)
    v.cin = chain(v.fwd[5], 1)
    v.state = v.fwd[3] + v.fwd[4] * v.cin
    v.mixer = (gelu_parts(v.gin)[0] * v.state).astype(BF).reshape(t * Lc, C)
    v.fwd = v.fwd[:3]
    v.y_b = y_next
    v.barrier()

    for k, others in enumerate(by_block(v.take("y_b")), 3):
        v.full_b = fill_far(v.full_b, others, k)
    v.w_out = v.take("full_b")
    v.y_g = to_groups(*v.take("g")[1:], v.d)
    v.d = [v.d]
    while len(v.d) < M - 3:
        v.d = v.d + ring_next(v.d[-1]).parts()
    v.z_cot = chunk_pieces(v.cotangent, rider=folded(v.d[-1]), which=(0, 1, M - 1))
    rec_sum = None
    for p in reversed(range(parts)):
        part = send_sum(mixed_sum(((v.mixer, p, parts), v.w_out)), p)
        rec_sum = part if rec_sum is None else rec_sum + part
    v.resid_mid = v.own_in.astype(F32) + rec_sum
    v.unit_two, v.scale_two = normed(v.resid_mid, v.gain_two)
    v.n2_own = (v.unit_two * v.gain_two).astype(BF)
    v.barrier()

    got = by_block(v.take("y_g"))
    for k, others in enumerate(got[:-1], 3):
        fill_gate(k, others=others)
    v.full_d = fill_far(v.full_d, got[-1], 1)
    v.w_gate_t, v.w_up_t = v.take("full_g")
    v.d = v.d + [unfolded(v.z_cot[1][Lc:])]
    v.z_cot[1] = v.z_cot[1][:Lc]
    for k, mine in enumerate(v.d[1:], 2):
        v.full_d = fill_own(v.full_d, mine, k)
    v.d_last = ring_next(v.d[-1])
    v.z_cot = {
        **v.z_cot, **chunk_pieces(v.take("cotangent"), which=range(2, M - 1))
    }
    v.n2_far = far(v.n2_own)
    v.n2 = [jnp.concatenate([v.n2_own, tp(v.n2_own, 1)])]
    v.take("n2_own")

    def mlp_forward(p):
        return products(
            NT,
            [[(v.n2[p], v.w_gate_t)], [(v.n2[p], v.w_up_t)]],
            [],
            [F32, F32, BF],
            lambda gate, up: (gate, up, gelu_parts(gate)[0] * up),
            "mlp",
        )

    v.mlp = [mlp_forward(0)]
    v.barrier()

    v.d = v.d[1:] + v.take("d_last").parts()
    v.y_d = to_groups(*v.d)
    cot_own = joined(v.take("z_cot"))
    v.cot = [jnp.concatenate([cot_own, tp(cot_own, 1)])]
    v.far_cot = far(cot_own)
    if parts > 1:
        v.n2.append(jnp.concatenate([v.n2_far, tp(v.n2_far, 1)]))
        v.mlp.append(mlp_forward(1))
    v.take("n2_far")
    v.barrier()

    def summed(lefts, rights, groups=None):
        groups = range(O) if groups is None else groups
        out = [
            products(
                TN,
                [list(zip(lefts, rights))],
                [],
                [BF],
                lambda total: (total,),
                "gradient",
                base=((o + r) % O) * half,
                width=half,
            )[0]
            for r in reversed(groups)
        ]
        return out[::-1]

    v.full_d = fill_own(v.full_d, v.take("d")[-1], M - 1)
    for k, others in enumerate(by_block(v.take("y_d")), 2):
        v.full_d = fill_far(v.full_d, others, k)
    v.w_dn = v.take("full_d")
    if parts > 1:
        v.cot.append(jnp.concatenate([v.far_cot, tp(v.far_cot, 1)]))
    v.take("far_cot")

    def mlp_back(p):
        def finish(d_hidden, gate, up):
            gelu, slope = gelu_parts(gate)
            return d_hidden * up * slope, d_hidden * gelu

        return products(
            NT, [[(v.cot[p], v.w_dn)]], list(v.mlp[p][:2]), [BF, BF], finish, "mlp_back"
        )

    def mlp_back_in(p):
        gate, up = v.d_mlp[p]
        return mixed_sum((gate, v.w_gate_t), (up, v.w_up_t))

    out_sum = None
    for p in reversed(range(parts)):
        part = send_sum(mixed_sum((v.mlp[p][2], v.w_dn)), p)
        out_sum = part if out_sum is None else out_sum + part
    v.output = (v.take("resid_mid") + out_sum).astype(BF)
    v.grad_down = summed([m[2] for m in v.mlp], v.cot, range(1, O))
    v.d_mlp = [None] * parts
    v.d_mlp[last] = mlp_back(last)
    v.barrier()

    v.y_down = to_groups_of([[None] + v.take("grad_down")])
    v.hidden = [m[2] for m in v.mlp]
    pieces = back_pieces(v.take("output"))
    v.z_out = [zshift(piece, k) if k else piece for k, piece in enumerate(pieces)]
    v.dn2 = [None] * parts
    v.dn2[last] = mlp_back_in(last)
    v.dn2_sum = send_sum(v.dn2[last], last) if last else None
    for p in range(last):
        v.d_mlp[p] = mlp_back(p)
        v.dn2[p] = mlp_back_in(p)
    v.grad_gate = summed([d[0] for d in v.d_mlp], v.n2, range(1, O))
    v.take("mlp")
    v.cot_own = v.cot[0][:Lc]
    v.barrier()

    own = summed(v.take("hidden"), v.take("cot"), range(1))
    (v.y_down,) = y_parts((own, v.y_down))
    v.output = back_joined(v.take("z_out"))
    v.ring = ring_step((v.y_down, 1, None))
    v.y_gate = to_groups_of([[None] + v.take("grad_gate")])
    dn2_sum = v.take("dn2_sum")
    for p in reversed(range(last if last else 1)):
        part = send_sum(v.dn2[p], p)
        dn2_sum = part if dn2_sum is None else dn2_sum + part
    v.take("dn2")

    def norm_back(grad, unit, scale, gain):
        weighted = grad * gain
        dots = jnp.mean(weighted * unit, axis=1, keepdims=True)
        return scale * (weighted - unit * dots), jnp.sum(grad * unit, axis=0)

    back_two, v.gain_two_grad = norm_back(dn2_sum, v.unit_two, v.scale_two, v.gain_two)
    v.d_mid = v.take("cot_own").astype(F32) + back_two
    v.d_own = v.d_mid.astype(BF)
    v.far_branch = far(v.d_own)
    v.near_branch = tp(v.d_own, 1)
    v.grad_up = summed([d[1] for d in v.d_mlp], v.n2)
    v.gate_own = summed([d[0] for d in v.take("d_mlp")], v.take("n2"), range(1))
    v.barrier()

    (v.y_gate,) = y_parts((v.take("gate_own"), v.y_gate))
    (r_down,) = v.ring.parts()
    v.ring = ring_step((v.y_down, 2, r_down), (v.y_gate, 1, None))
    v.y_up = grad_y(v.take("grad_up"))
    slots_of = [v.take("d_own"), v.take("near_branch")]
    if parts > 1:
        slots_of += [v.far_branch, tp(v.far_branch, 1)]
    v.take("far_branch")
    v.d_branch = jnp.concatenate(slots_of)
    v.adjoint = seq_call(
        adjoint_kernel,
        [
            dot_nt(v.d_branch, v.w_out).reshape(shape),
            v.take("gin"),
            v.state,
            v.fwd[1],
            v.masks,
        ],
        [v.vec],
        [(shape, F32, True)] * 2 + [(shape, BF, True), ((t, 8, C), F32, True)],
        [],
        "adjoint",
        24,
    )
    v.d_gin = v.adjoint[2].reshape(t * Lc, C)
    v.grad_branch = summed([v.d_gin], [v.n1])
    v.barrier()

    (v.y_up,) = y_parts(v.y_up)
    v.edges = jnp.concatenate(
        [
            jnp.broadcast_to(v.take("cin"), (t, 4, C)),
            jnp.broadcast_to(chain(v.adjoint[3], -1), (t, 4, C)),
        ],
        1,
    )
    v.grad_output = summed([v.take("mixer")], [v.take("d_branch")])
    v.barrier()

    r_down, r_gate = v.ring.parts()
    v.ring = ring_step((v.y_down, 3, r_down), (v.y_gate, 2, r_gate), (v.y_up, 1, None))
    v.y_mixer = grad_y(v.take("grad_output"), v.take("grad_branch"))
    mixed, gate_a, gate_x = v.fwd
    lam, prod, _, _ = v.adjoint

    def run_back(rows, time):
        tokens = [lam, prod, v.state, gate_a, gate_x, mixed, v.rnn]
        if rows < Lc:
            tokens = [array[:, :rows] for array in tokens]
        return seq_call(
            backward_kernel,
            tokens + [v.halos, v.masks[:, : rows + HALO], v.edges],
            [v.conv_w, v.vec, v.wa, v.wx],
            [
                ((t, rows, C), BF, True),
                ((t, HALO, C), F32, True),
                ((t, HALO, C), F32, True),
                ((C, C), F32, False),
                ((C, C), F32, False),
                ((8, 8, C), F32, False),
            ],
            [pltpu.VMEM((rows + HALO, C), F32)] * 3,
            "recurrence_back",
            time,
        )

    v.following = zline(run_back(2 * HALO, 4)[1], -1)
    v.d_rnn, _, v.tails, v.grad_wa, v.grad_wx, v.grad_vec = run_back(Lc, 40)
    for name in ("adjoint", "fwd", "state", "rnn", "halos", "edges"):
        v.take(name)
    v.barrier()

    following = v.take("following")
    fix = [jnp.zeros((t, 1, C), F32)] * HALO
    for k in range(1, 4):
        for n in range(k):
            row = HALO - k + n
            fix[row] = fix[row] + v.conv_w[k] * (
                v.masks[:, Lc + n : Lc + n + 1, k - 1 : k] * following[:, n : n + 1]
            )
    tail = (v.take("tails") + jnp.concatenate(fix, axis=1)).astype(BF)
    v.d_rnn = put(v.d_rnn, tail, 0, Lc - HALO, 0).reshape(t * Lc, C)
    v.r_down, r_gate, r_up = v.take("ring").parts()
    y_output, y_branch = y_parts(v.take("y_mixer"))
    rings = ring_sends((v.y_gate, 3, r_gate), (v.y_up, 2, r_up))

    def direct(rings, *grads):
        got = []
        for k, send in enumerate(direct_sends(*grads)):
            send = send + rings if k == M - 1 else send
            got.append(joint(lambda b: zshift(b, M - k) if k else b, send))
        return got

    v.z_mixer = direct(rings, y_output, y_branch)
    v.y_in = grad_y(summed([v.d_rnn], [v.n1]))
    v.take("n1")
    v.dn1 = [
        mixed_sum(((v.d_rnn, p, parts), v.w_in_t), ((v.d_gin, p, parts), v.w_br_t))
        for p in range(parts)
    ]
    for name in ("d_rnn", "d_gin", "w_in_t", "w_br_t", "wa", "wx", "masks", "vec"):
        v.take(name)
    v.barrier()

    gates_grad = jnp.stack(
        [
            jnp.stack(
                [g[n * bw : (n + 1) * bw, n * bw : (n + 1) * bw] for n in range(nh)]
            )
            for g in (v.take("grad_wa"), v.take("grad_wx"))
        ]
    )
    gates_grad = gates_grad.reshape(2, M, hpg, DP, bw_here, bw)
    gates_grad = gates_grad.transpose(1, 3, 0, 2, 4, 5).reshape(M, DP, gate_size)
    small = jnp.sum(v.take("grad_vec"), axis=1).reshape(2 * conv, M, O, nc)
    small = small.transpose(1, 2, 0, 3).reshape(M, O, 2 * conv * nc)
    small = put(jnp.zeros((M, DP, 2 * conv * nc), F32), small, 0, q * O, 0)
    gain_two_grad = v.take("gain_two_grad").reshape(M, DP, ng)
    gain_two_grad = jnp.stack([pick(gain_two_grad, (z - k) % M) for k in range(M)])
    gates_grad = jnp.concatenate([gates_grad, small, gain_two_grad], axis=2)
    gates_grad = jnp.pad(
        gates_grad, ((0, 0), (0, 0), (0, gate_rows * Dl - gates_grad.shape[2]))
    )
    gates_grad = gates_grad.reshape(M, DP, gate_rows, Dl).transpose(0, 2, 1, 3)
    gates_grad = gates_grad.reshape(M * gate_rows, D).astype(BF)
    gates_grad = [cut(gates_grad, (o + r) % O, half, 1) for r in range(O)]
    v.y_gates = grad_y(gates_grad)
    v.z_down = ring_end(v.take("y_down"), v.take("r_down"))
    r_gate, r_up = v.z_mixer[M - 1].parts()[2:]
    v.z_gate = ring_end(v.take("y_gate"), r_gate)
    v.z_in = direct(ring_sends((v.y_up, 3, r_up)), *y_parts(v.take("y_in")))
    dn1_sum = None
    for p in reversed(range(parts)):
        part = send_sum(v.dn1[p], p)
        dn1_sum = part if dn1_sum is None else dn1_sum + part
    v.dn1 = dn1_sum
    v.barrier()

    def added(pieces, count=1):
        return [
            sum(p.astype(F32) for p in same).astype(BF)
            for same in zip(*(p.parts()[:count] for p in pieces))
        ]

    r_up = v.z_in[M - 1].parts()[1]

    z_output, z_branch = added(v.take("z_mixer"), 2)
    (z_in,) = added(v.take("z_in"))
    z_up = ring_end(v.take("y_up"), r_up)
    totals = exchange_grads(
        v.take("z_down"), v.take("z_gate"), z_up, z_output, z_branch, z_in
    )
    unit_one, scale_one = normed(v.own_in, v.gain_one)
    back_one, gain_one_grad = norm_back(v.take("dn1"), unit_one, scale_one, v.gain_one)
    pieces = back_pieces((v.d_mid + back_one).astype(BF))
    sums = jnp.broadcast_to(gain_one_grad.astype(BF), (16, D))
    joints = []
    sends = direct_sends(*y_parts(v.take("y_gates")))
    for k, piece in enumerate(pieces):
        gates_send = folded(sends[(M - k) % M][0])
        joint = jnp.concatenate([piece, cut(sums, (z + k) % M, FH, 1), gates_send])
        joints.append(zshift(joint, k) if k else joint)
    v.joints = joints
    v.grads = [grad_end(total) for total in by_grad(totals)]
    v.barrier()

    grad_down, grad_gate, grad_up, grad_output, grad_branch, grad_in = v.grads
    input_grad = back_joined([joint[:Lc] for joint in v.joints]).astype(F32)
    gates_sum = unfolded(sum(joint[Lc + 16 :].astype(F32) for joint in v.joints))
    gates_sum = gates_sum.astype(BF)
    last_rows = exchange(lambda k: cut(gates_sum, k, Dl, 1))
    gain_one_grad = sum(joint[Lc].astype(F32) for joint in v.joints)
    step = 1
    while step < DP:
        gain_one_grad = gain_one_grad + tp(gain_one_grad, step)
        step *= 2
    gain_one_grad = cut(gain_one_grad, i_dp, ng, 0)
    output = v.output

    rest_in = jnp.stack([piece.reshape(-1) for piece in last_rows])
    small = jnp.sum(rest_in[:, gate_size:].astype(F32), axis=0)
    rest_in = jnp.stack([pick(rest_in, q ^ k) for k in range(t)])
    mine = small[: 2 * conv * nc].reshape(2 * conv, nc)
    gain_two_grad = small[2 * conv * nc : 2 * conv * nc + ng]
    decay_grad = mine[conv + 3] * (-8.0 * jax.nn.sigmoid(decay_param.astype(F32)))

    gates_back = rest_in[:, :gate_size].reshape(t, 2, hpg, bw_here, bw)
    gates_back = gates_back.transpose(1, 0, 2, 3, 4)
    gates_back = gates_back.reshape(2, heads_here, bw_here, bw).astype(F32)

    def flipped(value):
        return lax.optimization_barrier(value).T.astype(F32)

    return (
        output,
        input_grad,
        gain_one_grad,
        flipped(grad_in),
        flipped(grad_branch),
        grad_output.astype(F32),
        mine[:conv],
        mine[conv],
        gates_back[0],
        mine[conv + 1],
        gates_back[1],
        mine[conv + 2],
        decay_grad,
        gain_two_grad,
        flipped(grad_gate),
        flipped(grad_up),
        grad_down.astype(F32),
    )


def solution(mesh):
    both = P(("mp", "dp"))
    wide = P("dp", "mp")
    tall = P("mp", "dp")
    taps = P(None, ("mp", "dp"))
    gate = P("mp", "dp", None)
    params = (both, wide, wide, tall, taps, both, gate, both, gate, both, both, both, wide, wide, tall)
    return jax.shard_map(
        functools.partial(body, mesh.shape["dp"], mesh.shape["mp"]),
        mesh=mesh,
        in_specs=(wide, wide, P("dp")) + params,
        out_specs=(wide, wide) + params,
        check_vma=False,
    )
```
